32 devices in a mesh: rows: 8 (over z, y), ffn: 4 (over x, core).
Axes of the slice: x: 2, y: 2, z: 4, core: 2. Of those that a mesh axis runs over, the one named last changes fastest.
Arguments:
- tokens: bfloat16 [16384, 768], P(('rows', 'ffn')), may hold values from -6 to 6
- seq_lengths: int32 [8, 3], P('rows'), may hold values from 1 to 1024, 2048 in all within a row
- key_keep: int32 [16384], P('rows'), may hold values 0 or 1
- pre_gain: bfloat16 [768], P(('rows', 'ffn')), may hold values from 0.5 to 1.5
- pre_bias: bfloat16 [768], P(('rows', 'ffn')), may hold values from -1.75 to 1.75
- qkv_weight: bfloat16 [768, 2304], P(('rows', 'ffn')), may hold values from -0.21875 to 0.21875
- query_bias: bfloat16 [768], P(('rows', 'ffn')), may hold values from -3 to 3
- value_bias: bfloat16 [768], P(('rows', 'ffn')), may hold values from -3 to 3
- sub_gain: bfloat16 [768], P(('rows', 'ffn')), may hold values from 0.5 to 1.5
- sub_bias: bfloat16 [768], P(('rows', 'ffn')), may hold values from -1.75 to 1.75
- out_weight: bfloat16 [768, 768], P(('rows', 'ffn')), may hold values from -0.21875 to 0.21875
- out_bias: bfloat16 [768], P(('rows', 'ffn')), may hold values from -1.75 to 1.75
- ffn_gain: bfloat16 [768], P(('rows', 'ffn')), may hold values from 0.5 to 1.5
- ffn_bias: bfloat16 [768], P(('rows', 'ffn')), may hold values from -1.75 to 1.75
- up_bias: bfloat16 [3072], P(('rows', 'ffn')), may hold values from -3 to 3
- hidden_gain: bfloat16 [3072], P(('rows', 'ffn')), may hold values from 0.5 to 1.5
- hidden_bias: bfloat16 [3072], P(('rows', 'ffn')), may hold values from -1.75 to 1.75
- down_bias: bfloat16 [768], P(('rows', 'ffn')), may hold values from -1.75 to 1.75
- up_weight: bfloat16 [768, 3072], P('rows', 'ffn'), may hold values from -0.21875 to 0.21875
- down_weight: bfloat16 [3072, 768], P('ffn', 'rows'), may hold values from -0.109375 to 0.109375
- out_grad: float32 [16384, 768], P(('rows', 'ffn')), may hold values from -6 to 6
Outputs:
- layer_out: bfloat16 [16384, 768], P(('rows', 'ffn'))
- tokens_grad: float32 [16384, 768], P(('rows', 'ffn'))
- pre_gain_grad: float32 [768], P(('rows', 'ffn'))
- pre_bias_grad: float32 [768], P(('rows', 'ffn'))
- qkv_weight_grad: float32 [768, 2304], P(('rows', 'ffn'))
- query_bias_grad: float32 [768], P(('rows', 'ffn'))
- value_bias_grad: float32 [768], P(('rows', 'ffn'))
- sub_gain_grad: float32 [768], P(('rows', 'ffn'))
- sub_bias_grad: float32 [768], P(('rows', 'ffn'))
- out_weight_grad: float32 [768, 768], P(('rows', 'ffn'))
- out_bias_grad: float32 [768], P(('rows', 'ffn'))
- ffn_gain_grad: float32 [768], P(('rows', 'ffn'))
- ffn_bias_grad: float32 [768], P(('rows', 'ffn'))
- up_bias_grad: float32 [3072], P(('rows', 'ffn'))
- hidden_gain_grad: float32 [3072], P(('rows', 'ffn'))
- hidden_bias_grad: float32 [3072], P(('rows', 'ffn'))
- down_bias_grad: float32 [768], P(('rows', 'ffn'))
- up_weight_grad: float32 [768, 3072], P('rows', 'ffn')
- down_weight_grad: float32 [3072, 768], P('ffn', 'rows')
The draws below stay inside these ranges and needn't reach their ends.
Inputs may be any that keep to these rules, and one draw needn't show every extreme that they name: `seq_lengths`: row r lists in order the lengths of the 3 sequences packed into tokens r * 2048 to (r + 1) * 2048 - 1; each row sums to 2048 and its largest entry is 1024. `key_keep`: 1 marks a token that later tokens of its sequence may attend to, 0 a padding slot.
All inputs are finite; a program needn't handle non-finite values. No bound on the sum of `key_keep` on one device may be relied on, other than what follows from the above.
Results may differ from the reference program's by a relative error of at most 0.015.
Values may be sent and summed in bfloat16 or wider, within the bound.
No kernel may reach another device: no remote copies, remote signals or barrier semaphores. Data moves between devices by JAX's collectives and lax.ppermute only.
A program may use at most 192 MiB of HBM per device.

```python
import math
import jax
import jax.numpy as jnp
import numpy as np
from jax import lax

D = 768
HEADS = 12
HEAD_DIM = 64
FF = 3072
PACK = 2048
SEQS = 3
MAX_LEN = 1024
TOKENS = 16384
N_ROWS = 8


def plant(values, rng, low, top_value):
    spot = [jax.random.randint(jax.random.fold_in(rng, axis), (), 0, length) for axis, length in enumerate(values.shape)]
    longest = values.shape.index(max(values.shape))
    beside = spot[:longest] + [(spot[longest] + 1) % values.shape[longest]] + spot[longest + 1:]
    return values.at[tuple(spot)].set(low).at[tuple(beside)].set(top_value)


def steps_of(stream_key, dims, shards, smallest, largest):
    def one(position, blocks):
        draws = jax.random.uniform(jax.random.fold_in(jax.random.fold_in(stream_key, 6), position), (blocks,), jnp.float32, smallest / len(shards), largest / len(shards))
        return jnp.repeat(jnp.exp(draws), dims[position] // blocks).reshape((-1,) + (1,) * (len(dims) - position - 1))

    gain = one(*shards[0])
    for cut in shards[1:]:
        gain = gain * one(*cut)
    return gain


def profile(count, total, most, lean):
    weights = [(1 << 20) // math.isqrt(rank ** lean) + 1 for rank in range(2, count + 1)]
    surplus, given = total - most - (count - 1), [1] * (count - 1)
    while surplus > 0:
        candidates = [i for i in range(count - 1) if given[i] < most]
        mass, left = sum([weights[i] for i in candidates]), surplus
        for i in candidates:
            addition = min(most - given[i], max(1, left * weights[i] // mass), surplus)
            given[i] = given[i] + addition
            surplus = surplus - addition
    return np.array([most] + given)


def ragged(rng, number_of, total, bound, lean):
    if number_of == 2:
        one = jax.random.randint(rng, (), max(1, total - bound), min(bound, total - 1) + 1)
        return jnp.stack([one, total - one])
    tallies = jnp.asarray(profile(number_of, total, bound, lean), jnp.int32)
    couples = (number_of - 1) // 2
    donor, taker = tallies[1:1 + 2 * couples:2], tallies[2:2 + 2 * couples:2]
    room = jnp.minimum(donor - 1, bound - taker)
    moved = jax.random.randint(jax.random.fold_in(rng, 1), (couples,), 0, 1 << 20) % (room + 1)
    tallies = tallies.at[1:1 + 2 * couples:2].set(donor - moved).at[2:2 + 2 * couples:2].set(taker + moved)
    return tallies[jax.random.permutation(jax.random.fold_in(rng, 2), number_of)]


def noise(key, shape, scale, reach, cuts=(), kind=jnp.bfloat16):
    level = steps_of(key, shape, cuts, -0.22, 0.18) if cuts else 1.0
    values = jax.random.normal(key, shape, jnp.float32) * scale * level
    return jnp.minimum(jnp.maximum(values, -reach), reach).astype(kind)


def setup_inputs(seed: int = 0) -> dict:
    seeds = jax.random.split(jax.random.key(seed), 22)
    return {
        "tokens": noise(seeds[0], (TOKENS, D), 1.0, 6.0, ((0, 32),)),
        "seq_lengths": jax.vmap(lambda own: ragged(own, SEQS, PACK, MAX_LEN, 2))(jax.random.split(seeds[1], N_ROWS)).reshape((N_ROWS, SEQS)).astype(jnp.int32),
        "key_keep": plant((jax.random.randint(seeds[2], (TOKENS,), 0, 8) < 7).astype(jnp.int32), jax.random.fold_in(seeds[2], 1), 0, 1),
        "pre_gain": jnp.clip(1.0 + 0.1 * jax.random.normal(seeds[3], (D,), jnp.float32), 0.5, 1.5).astype(jnp.bfloat16),
        "pre_bias": noise(seeds[4], (D,), 0.3, 1.75, ((0, 32),)),
        "qkv_weight": noise(seeds[5], (D, 3 * D), D ** -0.5, 0.21875, ((0, 32),)),
        "query_bias": noise(seeds[6], (D,), 0.5, 3.0, ((0, 32),)),
        "value_bias": noise(seeds[7], (D,), 0.5, 3.0, ((0, 32),)),
        "sub_gain": jnp.clip(1.0 + 0.1 * jax.random.normal(seeds[8], (D,), jnp.float32), 0.5, 1.5).astype(jnp.bfloat16),
        "sub_bias": noise(seeds[9], (D,), 0.3, 1.75, ((0, 32),)),
        "out_weight": noise(seeds[10], (D, D), D ** -0.5, 0.21875, ((0, 32),)),
        "out_bias": noise(seeds[11], (D,), 0.3, 1.75, ((0, 32),)),
        "ffn_gain": jnp.clip(1.0 + 0.1 * jax.random.normal(seeds[12], (D,), jnp.float32), 0.5, 1.5).astype(jnp.bfloat16),
        "ffn_bias": noise(seeds[13], (D,), 0.3, 1.75, ((0, 32),)),
        "up_bias": noise(seeds[14], (FF,), 0.5, 3.0, ((0, 32),)),
        "hidden_gain": jnp.clip(1.0 + 0.1 * jax.random.normal(seeds[15], (FF,), jnp.float32), 0.5, 1.5).astype(jnp.bfloat16),
        "hidden_bias": noise(seeds[16], (FF,), 0.3, 1.75, ((0, 32),)),
        "down_bias": noise(seeds[17], (D,), 0.3, 1.75, ((0, 32),)),
        "up_weight": noise(seeds[18], (D, FF), D ** -0.5, 0.21875, ((0, 8), (1, 4))),
        "down_weight": noise(seeds[19], (FF, D), FF ** -0.5, 0.109375, ((0, 4), (1, 8))),
        "out_grad": noise(seeds[20], (TOKENS, D), 1.0, 6.0, ((0, 32),), jnp.float32),
    }


eps = 1e-05
neg_big = -1e+30
score_scale = 0.125
highest = lax.Precision.HIGHEST

@jax.custom_vjp
def low(v):
    return lax.optimization_barrier(v.astype(jnp.bfloat16)).astype(jnp.float32)

@jax.custom_vjp
def low_back(v):
    return v

def low_keep(v):
    return (low(v), None)

def low_pass(kept, grad):
    return (grad,)

def back_keep(v):
    return (v, None)

def back_low(kept, grad):
    return (low(grad),)
low.defvjp(low_keep, low_pass)
low_back.defvjp(back_keep, back_low)

def layer_norm(values, norm_gain, norm_offset):
    center = values - lax.optimization_barrier(jnp.mean(values, axis=-1, keepdims=True))
    return center * lax.rsqrt(lax.optimization_barrier(jnp.mean(center * center, axis=-1, keepdims=True)) + eps) * norm_gain + norm_offset

def segment_ids(lengths_row):
    bounds = jnp.cumsum(lengths_row).astype(jnp.int32)[:-1]
    places = lax.iota(jnp.int32, PACK)
    return lax.optimization_barrier(jnp.sum((places[:, None] >= bounds[None, :]).astype(jnp.int32), axis=1)).astype(jnp.int32)

def pair_mask(query_pos, query_seg, key_pos, key_seg, key_flags):
    same = query_seg[:, None] == key_seg[None, :]
    before = (key_pos[None, :] < query_pos[:, None]) & (key_flags[None, :] > 0)
    return same & (before | (key_pos[None, :] == query_pos[:, None]))

def pack_attention(query_heads, key_heads, value_heads, seg_row, keep_row):
    pack_total = query_heads.shape[0]
    block_size = min(pack_total, 512)
    key_pos = lax.iota(jnp.int32, pack_total)

    def one_block(block_index):
        row_first = block_index * block_size
        query_rows = lax.dynamic_slice_in_dim(query_heads, row_first, block_size, 0)
        query_pos = row_first + lax.iota(jnp.int32, block_size)
        query_seg = lax.dynamic_slice_in_dim(seg_row, row_first, block_size, 0)
        allowed = pair_mask(query_pos, query_seg, key_pos, seg_row, keep_row)
        raw = jnp.einsum('qhd,khd->hqk', query_rows, key_heads, precision=highest) * score_scale
        scores = jnp.where(allowed[None], low_back(raw), neg_big)
        weights = jnp.exp(scores - lax.optimization_barrier(jnp.max(scores, axis=-1, keepdims=True)))
        probs = low(weights / lax.optimization_barrier(jnp.sum(weights, axis=-1, keepdims=True)))
        return jnp.einsum('hqk,khd->qhd', probs, value_heads, precision=highest)
    blocks = lax.map(jax.checkpoint(one_block), jnp.arange(pack_total // block_size, dtype=jnp.int32))
    return blocks.reshape(pack_total, D)

def pack_layer(inputs, seg_row, keep_row, params):
    pre_gain, pre_bias, qkv_weight, query_bias, value_bias, sub_gain, sub_bias, out_weight, out_bias, ffn_gain, ffn_bias, up_bias, hidden_gain, hidden_bias, down_bias, up_weight, down_weight = params
    pack_rows = inputs.shape[0]
    normed_in = low(layer_norm(inputs, pre_gain, pre_bias))
    projected = low_back(jnp.dot(normed_in, qkv_weight, precision=highest))
    queries = low(projected[:, :D] + query_bias)
    keys_all = low(projected[:, D:2 * D])
    values_all = low(projected[:, 2 * D:] + value_bias)
    attended = low_back(pack_attention(queries.reshape(pack_rows, HEADS, HEAD_DIM), keys_all.reshape(pack_rows, HEADS, HEAD_DIM), values_all.reshape(pack_rows, HEADS, HEAD_DIM), seg_row, keep_row))
    sub_normed = low(layer_norm(attended, sub_gain, sub_bias))
    middle = inputs + low_back(jnp.dot(sub_normed, out_weight, precision=highest)) + out_bias
    ffn_in = low(layer_norm(middle, ffn_gain, ffn_bias))
    pre_act = low_back(jnp.dot(ffn_in, up_weight, precision=highest)) + up_bias
    hidden = low(layer_norm(jax.nn.gelu(pre_act, approximate=False), hidden_gain, hidden_bias))
    return middle + low_back(jnp.dot(hidden, down_weight, precision=highest)) + down_bias

def reference(tokens, seq_lengths, key_keep, pre_gain, pre_bias, qkv_weight, query_bias, value_bias, sub_gain, sub_bias, out_weight, out_bias, ffn_gain, ffn_bias, up_bias, hidden_gain, hidden_bias, down_bias, up_weight, down_weight, out_grad):
    params = tuple((array.astype(jnp.float32) for array in (pre_gain, pre_bias, qkv_weight, query_bias, value_bias, sub_gain, sub_bias, out_weight, out_bias, ffn_gain, ffn_bias, up_bias, hidden_gain, hidden_bias, down_bias, up_weight, down_weight)))
    seg_rows = jax.vmap(segment_ids)(seq_lengths)
    keep_rows = key_keep.reshape(N_ROWS, PACK)

    def whole(inputs, weights):

        def per_pack(carry, piece):
            return (carry, pack_layer(piece[0], piece[1], piece[2], weights))
        _, outputs = lax.scan(per_pack, jnp.zeros((), jnp.float32), (inputs.reshape(N_ROWS, PACK, D), seg_rows, keep_rows))
        return outputs.reshape(N_ROWS * PACK, D)
    layer_out, pullback = jax.vjp(whole, tokens.astype(jnp.float32), params)
    tokens_grad, grads = pullback(out_grad.astype(jnp.float32))
    return (layer_out.astype(jnp.bfloat16), tokens_grad, grads[0], grads[1], grads[2], grads[3], grads[4], grads[5], grads[6], grads[7], grads[8], grads[9], grads[10], grads[11], grads[12], grads[13], grads[14], grads[15], grads[16])
```

```python
import functools

import jax
import jax.numpy as jnp
from jax import lax
from jax.experimental import pallas as pl
from jax.experimental.pallas import tpu as pltpu
from jax.sharding import PartitionSpec as P

HEAD_DIM = 64
FF = 3072
BLOCK = 256

eps = 1e-05
neg_big = -1e30
score_scale = 0.125
root_half = 0.7071067811865476
inv_root_tau = 0.3989422804014327

f32 = jnp.float32
bf16 = jnp.bfloat16


def _pairs(flip, count=4):
    return [(i, i ^ flip) for i in range(count)]


def swap(values, flip):
    return lax.ppermute(values, "ffn", _pairs(flip))


def slot_owner(slot, ffn_index, ffn_size):
    return ffn_index ^ slot if ffn_size == 4 else jnp.int32(slot)


def gather_slots(values, ffn_size):
    if ffn_size != 4:
        return lax.all_gather(values, "ffn", axis=0, tiled=False)
    across = swap(values, 2)
    beside = swap(values, 1)
    return jnp.stack([values, beside, across, swap(across, 1)])


def exchange_slots(values, ffn_size):
    if ffn_size != 4:
        return lax.all_to_all(values, "ffn", split_axis=0, concat_axis=0, tiled=True)
    across = swap(values[2], 2)
    slanted = swap(values[3], 3)
    beside = swap(values[1], 1)
    return jnp.stack([values[0], beside, across, slanted])


def reduce_slots(values, ffn_size):
    if ffn_size != 4:
        return lax.psum_scatter(values.astype(bf16), "ffn", scatter_dimension=0, tiled=True)[0].astype(f32)
    passed = swap(jnp.stack([values[1], values[3]]).astype(bf16), 1).astype(f32)
    across = swap((values[2] + passed[1]).astype(bf16), 2).astype(f32)
    return values[0] + passed[0] + across


def sum_slots(values, ffn_size):
    if ffn_size != 4:
        return lax.psum(values, "ffn")
    beside = swap(values, 1)
    values = values + jnp.stack([beside[1], beside[0], beside[3], beside[2]])
    across = swap(values, 2)
    return values + jnp.stack([across[2], across[3], across[0], across[1]])


NT = (((1,), (1,)), ((), ()))


def dot_nt(a, b):
    return lax.dot_general(a, b, NT, preferred_element_type=f32)


def dot_nn(a, b):
    return jnp.dot(a, b, preferred_element_type=f32)


def start_row(first, bounds_ref, bound_count):
    places = first + lax.broadcasted_iota(jnp.int32, (1, BLOCK), 1)
    start = jnp.zeros((1, BLOCK), jnp.int32)
    for i in range(bound_count):
        bound = bounds_ref[i]
        start = jnp.where(places >= bound, jnp.maximum(start, bound), start)
    return places, start


def first_block(first, bounds_ref, bound_count):
    start = jnp.int32(0)
    for i in range(bound_count):
        bound = bounds_ref[i]
        start = jnp.where(first >= bound, jnp.maximum(start, bound), start)
    return start // BLOCK


def load_keys(keep_ref, limit_ref, blocks):
    for j in range(blocks):
        row = keep_ref[j : j + 1, :]
        places = j * BLOCK + lax.broadcasted_iota(jnp.int32, (1, BLOCK), 1)
        limits = jnp.where(row > 0, places, 1 << 24).astype(f32)
        column = jnp.transpose(jnp.broadcast_to(limits, (128, BLOCK)))
        limit_ref[j * BLOCK : (j + 1) * BLOCK, :] = column


def block_bias(limit_ref, key_first, query_places, query_start):
    limit = limit_ref[pl.ds(key_first, BLOCK), :]
    limit = jnp.concatenate([limit] * (BLOCK // 128), axis=1)
    key_places = key_first + lax.broadcasted_iota(jnp.int32, (BLOCK, BLOCK), 0)
    before = (limit < query_places.astype(f32)) & (key_places >= query_start)
    return jnp.where(before | (key_places == query_places), 0.0, neg_big)


def forward_kernel(
    place_ref, bounds_ref, proj_ref, keep_ref, out_ref, lse_ref, limit_ref, value_t_ref, *, heads, bound_count
):
    total = proj_ref.shape[0]
    blocks = total // BLOCK
    width = heads * HEAD_DIM
    load_keys(keep_ref, limit_ref, blocks)
    for j in range(blocks):
        rows = slice(j * BLOCK, (j + 1) * BLOCK)
        value_t_ref[:, rows] = jnp.transpose(proj_ref[rows, 2 * width :].astype(f32)).astype(bf16)

    def query_step(qi, _):
        query_first = pl.multiple_of(qi * BLOCK, BLOCK)
        query_at = pl.multiple_of(place_ref[qi], BLOCK)
        places, starts = start_row(query_first, bounds_ref, bound_count)
        queries = proj_ref[pl.ds(query_at, BLOCK), :width] * jnp.asarray(score_scale, bf16)

        def key_step(kj, carry):
            key_first = pl.multiple_of(kj * BLOCK, BLOCK)
            key_at = pl.multiple_of(place_ref[kj], BLOCK)
            bias = block_bias(limit_ref, key_first, places, starts)
            keys = proj_ref[pl.ds(key_at, BLOCK), width : 2 * width]
            values_t = value_t_ref[:, pl.ds(key_at, BLOCK)]
            out = []
            for h in range(heads):
                cols = slice(h * HEAD_DIM, (h + 1) * HEAD_DIM)
                top, total_sum, mixed = carry[h]
                scores = dot_nt(keys[:, cols], queries[:, cols]) + bias
                new_top = jnp.maximum(top, jnp.max(scores, axis=0, keepdims=True))
                weights = jnp.exp(scores - new_top)
                decay = jnp.exp(top - new_top)
                new_sum = total_sum * decay + jnp.sum(weights, axis=0, keepdims=True)
                new_mixed = mixed * decay + dot_nn(values_t[cols, :], weights.astype(bf16))
                out.append((new_top, new_sum, new_mixed))
            return tuple(out)

        empty = (
            jnp.full((1, BLOCK), neg_big, f32),
            jnp.zeros((1, BLOCK), f32),
            jnp.zeros((HEAD_DIM, BLOCK), f32),
        )
        done = lax.fori_loop(first_block(query_first, bounds_ref, bound_count), qi + 1, key_step, (empty,) * heads)
        mixed_t = jnp.concatenate([mixed / total_sum for _, total_sum, mixed in done], axis=0)
        out_ref[pl.ds(query_at, BLOCK), :] = jnp.transpose(mixed_t).astype(out_ref.dtype)
        for h in range(heads):
            lse_ref[h : h + 1, pl.ds(query_first, BLOCK)] = done[h][0] + jnp.log(done[h][1])
        return 0

    lax.fori_loop(0, blocks, query_step, 0)


def backward_kernel(
    place_ref,
    bounds_ref,
    proj_ref,
    keep_ref,
    mixed_ref,
    grad_ref,
    lse_ref,
    out_ref,
    bias_ref,
    limit_ref,
    key_t_ref,
    key_acc,
    value_acc,
    *,
    heads,
    bound_count,
):
    total = proj_ref.shape[0]
    blocks = total // BLOCK
    width = heads * HEAD_DIM
    load_keys(keep_ref, limit_ref, blocks)
    for j in range(blocks):
        rows = slice(j * BLOCK, (j + 1) * BLOCK)
        key_t_ref[:, rows] = jnp.transpose(proj_ref[rows, width : 2 * width].astype(f32)).astype(bf16)
    key_acc[...] = jnp.zeros_like(key_acc)
    value_acc[...] = jnp.zeros_like(value_acc)
    bias_ref[...] = jnp.zeros_like(bias_ref)

    def query_step(qi, _):
        query_first = pl.multiple_of(qi * BLOCK, BLOCK)
        query_at = pl.multiple_of(place_ref[qi], BLOCK)
        query_rows = pl.ds(query_at, BLOCK)
        places, starts = start_row(query_first, bounds_ref, bound_count)
        queries = proj_ref[query_rows, :width] * jnp.asarray(score_scale, bf16)
        grads = grad_ref[query_rows, :]
        product_t = jnp.transpose(grads.astype(f32) * mixed_ref[query_rows, :].astype(f32))
        lse = [lse_ref[h : h + 1, pl.ds(query_first, BLOCK)] for h in range(heads)]
        delta = [
            jnp.sum(product_t[h * HEAD_DIM : (h + 1) * HEAD_DIM, :], axis=0, keepdims=True) for h in range(heads)
        ]

        def key_step(kj, carry):
            key_first = pl.multiple_of(kj * BLOCK, BLOCK)
            key_rows = pl.ds(pl.multiple_of(place_ref[kj], BLOCK), BLOCK)
            bias = block_bias(limit_ref, key_first, places, starts)
            keys = proj_ref[key_rows, width : 2 * width]
            values = proj_ref[key_rows, 2 * width :]
            keys_t = key_t_ref[:, key_rows]
            out, key_parts, value_parts = [], [], []
            for h in range(heads):
                cols = slice(h * HEAD_DIM, (h + 1) * HEAD_DIM)
                scores = dot_nt(keys[:, cols], queries[:, cols]) + bias
                probs = jnp.exp(scores - lse[h])
                grad_probs = dot_nt(values[:, cols], grads[:, cols])
                grad_scores = (probs * (grad_probs - delta[h])).astype(bf16)
                value_parts.append(dot_nn(probs.astype(bf16), grads[:, cols]))
                key_parts.append(dot_nn(grad_scores, queries[:, cols]))
                out.append(carry[h] + dot_nn(keys_t[cols, :], grad_scores))
            key_acc[key_rows, :] += jnp.concatenate(key_parts, axis=1)
            value_acc[key_rows, :] += jnp.concatenate(value_parts, axis=1)
            return tuple(out)

        zero = jnp.zeros((HEAD_DIM, BLOCK), f32)
        done = lax.fori_loop(first_block(query_first, bounds_ref, bound_count), qi + 1, key_step, (zero,) * heads)
        grad_query = jnp.transpose(jnp.concatenate(done, axis=0)) * score_scale
        bias_ref[0:1, :] += jnp.sum(grad_query, axis=0, keepdims=True)
        out_ref[query_rows, :width] = grad_query.astype(bf16)
        return 0

    lax.fori_loop(0, blocks, query_step, 0)
    bias_ref[1:2, :] = jnp.sum(value_acc[...], axis=0, keepdims=True)
    out_ref[:, width : 2 * width] = key_acc[...].astype(bf16)
    out_ref[:, 2 * width :] = value_acc[...].astype(bf16)


SMEM = pl.BlockSpec(memory_space=pltpu.SMEM)
VMEM = pl.BlockSpec(memory_space=pltpu.VMEM)


def attend_forward(place, bounds, proj, keep, heads):
    total, width = proj.shape[0], heads * HEAD_DIM
    pairs = total * total // 6
    return pl.pallas_call(
        functools.partial(forward_kernel, heads=heads, bound_count=bounds.shape[0]),
        out_shape=(jax.ShapeDtypeStruct((total, width), bf16), jax.ShapeDtypeStruct((heads, total), f32)),
        in_specs=[SMEM, SMEM, VMEM, VMEM],
        out_specs=(VMEM, VMEM),
        scratch_shapes=[pltpu.VMEM((total, 128), f32), pltpu.VMEM((width, total), bf16)],
        compiler_params=pltpu.CompilerParams(vmem_limit_bytes=40 << 20),
        cost_estimate=pl.CostEstimate(
            flops=16 * pairs * width, bytes_accessed=total * width * 8, transcendentals=pairs * heads
        ),
        name="attend_forward",
    )(place, bounds, proj, keep)


def attend_backward(place, bounds, proj, keep, mixed, grads, lse, heads):
    total, width = proj.shape[0], heads * HEAD_DIM
    pairs = total * total // 6
    return pl.pallas_call(
        functools.partial(backward_kernel, heads=heads, bound_count=bounds.shape[0]),
        out_shape=(jax.ShapeDtypeStruct((total, 3 * width), bf16), jax.ShapeDtypeStruct((2, width), f32)),
        in_specs=[SMEM, SMEM, VMEM, VMEM, VMEM, VMEM, VMEM],
        out_specs=(VMEM, VMEM),
        scratch_shapes=[
            pltpu.VMEM((total, 128), f32),
            pltpu.VMEM((width, total), bf16),
            pltpu.VMEM((total, width), f32),
            pltpu.VMEM((total, width), f32),
        ],
        compiler_params=pltpu.CompilerParams(vmem_limit_bytes=50 << 20),
        cost_estimate=pl.CostEstimate(
            flops=40 * pairs * width, bytes_accessed=total * width * 20, transcendentals=pairs * heads
        ),
        name="attend_backward",
    )(place, bounds, proj, keep, mixed, grads, lse)


def unit_norm(values):
    center = values - jnp.mean(values, axis=-1, keepdims=True)
    inverse = lax.rsqrt(jnp.mean(center * center, axis=-1, keepdims=True) + eps)
    return center * inverse, inverse


def norm_grad(upstream, normed, inverse, norm_gain):
    scaled = upstream * norm_gain
    adjusted = (
        scaled
        - jnp.mean(scaled, axis=-1, keepdims=True)
        - normed * jnp.mean(scaled * normed, axis=-1, keepdims=True)
    )
    return (adjusted * inverse, jnp.sum(upstream * normed, axis=0), jnp.sum(upstream, axis=0))


def permute_columns(values, owners, size):
    return jnp.concatenate(
        [lax.dynamic_slice_in_dim(values, owner * size, size, 0) for owner in owners], axis=0
    )


def body(
    row_size,
    ffn_size,
    tokens,
    seq_lengths,
    key_keep,
    pre_gain,
    pre_bias,
    qkv_weight,
    query_bias,
    value_bias,
    sub_gain,
    sub_bias,
    out_weight,
    out_bias,
    ffn_gain,
    ffn_bias,
    up_bias,
    hidden_gain,
    hidden_bias,
    down_bias,
    up_weight,
    down_weight,
    out_grad,
):
    ffn_index = lax.axis_index("ffn")
    devices = row_size * ffn_size
    row_count, width = tokens.shape
    pack_total = row_count * ffn_size
    head_count = width // HEAD_DIM
    heads = -(-head_count // ffn_size)
    head_width = heads * HEAD_DIM
    padded = head_width * ffn_size
    hidden_width = up_weight.shape[1]
    share, hidden_share = pre_gain.shape[0], up_bias.shape[0]
    owners = [slot_owner(p, ffn_index, ffn_size) for p in range(ffn_size)]

    token_slots = gather_slots(tokens, ffn_size)
    thirds = jnp.pad(qkv_weight.reshape(share, 3, width), ((0, 0), (0, 0), (0, padded - width)))
    pieces = thirds.reshape(share, 3, ffn_size, head_width).transpose(2, 0, 1, 3)
    pieces = pieces.reshape(ffn_size, share, 3 * head_width)
    vectors = jnp.concatenate(
        [
            pre_gain, pre_bias, query_bias, value_bias, sub_gain, sub_bias, out_bias, ffn_gain, ffn_bias, down_bias,
            up_bias, hidden_gain, hidden_bias,
        ]
    )
    narrow = 10 * share
    vector_row = jnp.pad(vectors, (0, 3 * head_width - vectors.shape[0]))
    pieces = jnp.concatenate(
        [pieces, jnp.broadcast_to(vector_row, (ffn_size, 1, 3 * head_width))], axis=1
    )
    pieces = lax.all_to_all(pieces, "ffn", split_axis=0, concat_axis=0, tiled=True)
    gathered = lax.all_gather(pieces, "rows", axis=0, tiled=False)
    qkv_own = gathered[:, :, :share, :].reshape(width, 3 * head_width)
    vector_all = gathered[:, :, share, :].reshape(devices, 3 * head_width)[:, : vectors.shape[0]].astype(f32)
    wide = vector_all[:, :narrow].reshape(devices, 10, share).transpose(1, 0, 2).reshape(10, width)
    (
        pre_gain_all, pre_bias_all, query_bias_all, value_bias_all, sub_gain_all, sub_bias_all, out_bias_all,
        ffn_gain_all, ffn_bias_all, down_bias_all,
    ) = [wide[i] for i in range(10)]
    hidden_vectors = lax.dynamic_slice_in_dim(vector_all[:, narrow:], ffn_index * row_size, row_size, 0)
    hidden_vectors = hidden_vectors.reshape(row_size, 3, hidden_share).transpose(1, 0, 2).reshape(3, hidden_width)
    up_bias_own, hidden_gain_own, hidden_bias_own = hidden_vectors[0], hidden_vectors[1], hidden_vectors[2]

    out_rows = lax.all_gather(out_weight, "ffn", axis=0, tiled=True)
    weight_rows = jnp.concatenate([up_weight, down_weight.T, out_rows], axis=1)
    weights_all = lax.all_gather(weight_rows, "rows", axis=0, tiled=True)
    up_own = weights_all[:, :hidden_width]
    down_own = weights_all[:, hidden_width : 2 * hidden_width]
    out_all = weights_all[:, 2 * hidden_width :]

    grad_slots = gather_slots(out_grad.astype(bf16), ffn_size).reshape(pack_total, width)

    unit_in, inverse_in = unit_norm(token_slots.reshape(pack_total, width).astype(f32))
    normed_low = (unit_in * pre_gain_all + pre_bias_all).astype(bf16)
    own_bias = [
        lax.dynamic_slice_in_dim(jnp.pad(b, (0, padded - width)), ffn_index * head_width, head_width, 0)
        for b in (query_bias_all, value_bias_all)
    ]
    bias_row = jnp.concatenate([own_bias[0], jnp.zeros((head_width,), f32), own_bias[1]])
    proj = (jnp.dot(normed_low, qkv_own, preferred_element_type=f32) + bias_row).astype(bf16)

    bounds, running = [], jnp.int32(0)
    for i in range(seq_lengths.shape[1] - 1):
        running = running + seq_lengths[0, i]
        bounds.append(running)
    bounds = jnp.stack(bounds)
    firsts = jnp.arange(pack_total // BLOCK, dtype=jnp.int32) * BLOCK
    block_owner = firsts // row_count
    place = (block_owner ^ ffn_index if ffn_size == 4 else block_owner) * row_count + firsts % row_count
    keep = key_keep.reshape(pack_total // BLOCK, BLOCK)
    mixed_own, lse = attend_forward(place, bounds, proj, keep, heads)

    mixed_slots = exchange_slots(mixed_own.reshape(ffn_size, row_count, head_width), ffn_size)
    attended = mixed_slots.transpose(1, 0, 2).reshape(row_count, padded).astype(f32)

    def by_slot(values):
        tail = [(0, padded - width)] + [(0, 0)] * (values.ndim - 1)
        return permute_columns(jnp.pad(values, tail), owners, head_width)

    out_slots = by_slot(out_all)
    sub_gain_slots, sub_bias_slots = by_slot(sub_gain_all), by_slot(sub_bias_all)
    real = by_slot(jnp.ones((width,), f32)) if padded != width else None

    def sub_mean(values):
        return jnp.sum(values, axis=-1, keepdims=True) * (1.0 / width)

    center = attended - sub_mean(attended)
    if real is not None:
        center = center * real
    sub_inverse = lax.rsqrt(sub_mean(center * center) + eps)
    sub_unit = center * sub_inverse
    sub_low = (sub_unit * sub_gain_slots + sub_bias_slots).astype(bf16)
    middle = tokens.astype(f32) + jnp.dot(sub_low, out_slots, preferred_element_type=f32) + out_bias_all
    ffn_unit, ffn_inverse = unit_norm(middle)
    ffn_low = (ffn_unit * ffn_gain_all + ffn_bias_all).astype(bf16)

    rows_all = gather_slots(ffn_low, ffn_size).reshape(pack_total, width)
    pre_act = jnp.dot(rows_all, up_own, preferred_element_type=f32) + up_bias_own
    phi = 0.5 * (1.0 + lax.erf(pre_act * root_half))
    activated = pre_act * phi
    slope = phi + pre_act * inv_root_tau * jnp.exp(-0.5 * pre_act * pre_act)
    grad_hidden = jnp.dot(grad_slots, down_own, preferred_element_type=f32)
    scaled = grad_hidden * hidden_gain_own
    sums = jnp.stack(
        [
            jnp.sum(activated, axis=1),
            jnp.sum(activated * activated, axis=1),
            jnp.sum(scaled, axis=1),
            jnp.sum(scaled * activated, axis=1),
        ]
    )
    sums = sum_slots(sums.reshape(4, ffn_size, row_count).transpose(1, 0, 2), ffn_size) * (1.0 / FF)
    sums = sums.transpose(1, 0, 2).reshape(4, pack_total)
    hidden_mean = sums[0]
    inverse = lax.rsqrt(sums[1] - hidden_mean * hidden_mean + eps)
    normed = (activated - hidden_mean[:, None]) * inverse[:, None]
    hidden_low = (normed * hidden_gain_own + hidden_bias_own).astype(bf16)
    back_dot = (sums[3] - hidden_mean * sums[2]) * inverse
    grad_pre = (scaled - sums[2][:, None] - normed * back_dot[:, None]) * (inverse[:, None] * slope)
    grad_pre_low = grad_pre.astype(bf16)
    grad_in_part = lax.dot_general(grad_pre_low, up_own, NT, preferred_element_type=f32)
    grad_ffn_in = reduce_slots(grad_in_part.reshape(ffn_size, row_count, width), ffn_size)
    down_part = lax.dot_general(hidden_low, down_own, NT, preferred_element_type=f32)
    down_sum = reduce_slots(down_part.reshape(ffn_size, row_count, width), ffn_size)
    layer_out = (middle + down_sum + down_bias_all).astype(bf16)
    up_grad = jnp.einsum("td,tf->df", rows_all, grad_pre_low, preferred_element_type=f32)
    down_grad = jnp.einsum("td,tf->df", grad_slots, hidden_low, preferred_element_type=f32)
    hidden_grads = jnp.stack(
        [jnp.sum(grad_pre, axis=0), jnp.sum(grad_hidden * normed, axis=0), jnp.sum(grad_hidden, axis=0)]
    )

    grad_middle_part, ffn_gain_grad, ffn_bias_grad = norm_grad(grad_ffn_in, ffn_unit, ffn_inverse, ffn_gain_all)
    grad_middle = out_grad + grad_middle_part
    middle_low = grad_middle.astype(bf16)
    grad_sub = lax.dot_general(middle_low, out_slots, NT, preferred_element_type=f32)
    sub_scaled = grad_sub * sub_gain_slots
    adjusted = sub_scaled - sub_mean(sub_scaled) - sub_unit * sub_mean(sub_scaled * sub_unit)
    attended_low = (adjusted * sub_inverse).astype(bf16)
    grad_own = exchange_slots(
        attended_low.reshape(row_count, ffn_size, head_width).transpose(1, 0, 2), ffn_size
    ).reshape(pack_total, head_width)
    out_grad_slots = lax.dot_general(
        sub_low, middle_low, (((0,), (0,)), ((), ())), preferred_element_type=f32
    ).reshape(ffn_size, head_width, width)

    def from_slots(values):
        places = [slot_owner(p, ffn_index, ffn_size) for p in range(ffn_size)]
        return jnp.concatenate(
            [lax.dynamic_index_in_dim(values, place_of, 0, keepdims=False) for place_of in places], axis=0
        )[:width]

    out_weight_grad = from_slots(out_grad_slots)
    sub_gain_grad = from_slots(jnp.sum(grad_sub * sub_unit, axis=0).reshape(ffn_size, head_width))
    sub_bias_grad = from_slots(jnp.sum(grad_sub, axis=0).reshape(ffn_size, head_width))

    weight_grads = lax.psum_scatter(
        jnp.concatenate([up_grad, down_grad, out_weight_grad], axis=1).astype(bf16),
        "rows",
        scatter_dimension=0,
        tiled=True,
    )
    up_weight_grad = weight_grads[:, :hidden_width].astype(f32)
    down_weight_grad = weight_grads[:, hidden_width : 2 * hidden_width].astype(f32).T
    out_rows_grad = weight_grads[:, 2 * hidden_width :].reshape(ffn_size, share, width)
    out_weight_own = jnp.sum(
        lax.all_to_all(out_rows_grad, "ffn", split_axis=0, concat_axis=0, tiled=True).astype(f32), axis=0
    )

    grad_proj, head_bias_grads = attend_backward(place, bounds, proj, keep, mixed_own, grad_own, lse, heads)
    grad_normed_part = lax.dot_general(grad_proj, qkv_own, NT, preferred_element_type=f32)
    grad_normed_in = reduce_slots(grad_normed_part.reshape(ffn_size, row_count, width), ffn_size)
    pre_gain_grad = jnp.sum(grad_normed_part * unit_in, axis=0)
    pre_bias_grad = jnp.sum(grad_normed_part, axis=0)
    qkv_grad = lax.dot_general(normed_low, grad_proj, (((0,), (0,)), ((), ())), preferred_element_type=f32)

    def own_heads(values):
        spread = lax.dynamic_update_slice_in_dim(
            jnp.zeros((padded,), f32), values, ffn_index * head_width, 0
        )
        return spread[:width]

    wide_grads = jnp.stack(
        [
            pre_gain_grad, pre_bias_grad, own_heads(head_bias_grads[0]), own_heads(head_bias_grads[1]),
            sub_gain_grad, sub_bias_grad, jnp.sum(grad_middle, axis=0), ffn_gain_grad, ffn_bias_grad,
            jnp.sum(out_grad, axis=0),
        ]
    )
    wide_grads = wide_grads.reshape(10, devices, share).transpose(1, 0, 2).reshape(devices, narrow)
    hidden_grads = hidden_grads.reshape(3, row_size, hidden_share).transpose(1, 0, 2).reshape(row_size, 3 * hidden_share)
    hidden_grads = lax.dynamic_update_slice_in_dim(
        jnp.zeros((devices, 3 * hidden_share), f32), hidden_grads, ffn_index * row_size, 0
    )
    vector_grads = jnp.concatenate([wide_grads, hidden_grads], axis=1)
    vector_grads = jnp.pad(vector_grads, ((0, 0), (0, 3 * head_width - vector_grads.shape[1])))
    packed = jnp.concatenate(
        [qkv_grad.reshape(devices, share, 3 * head_width), vector_grads[:, None, :]], axis=1
    ).astype(bf16)
    packed = lax.all_to_all(packed, ("rows", "ffn"), split_axis=0, concat_axis=0, tiled=True)
    vector_own = jnp.sum(packed[:, share, :].astype(f32), axis=0)
    qkv_sum = jnp.sum(packed[:, :share, :].astype(f32).reshape(row_size, ffn_size, share, 3, head_width), axis=0)
    qkv_weight_grad = qkv_sum.transpose(1, 2, 0, 3).reshape(share, 3, padded)[:, :, :width].reshape(share, 3 * width)

    in_slot = jnp.int32(0) if ffn_size == 4 else ffn_index
    unit_own = lax.dynamic_slice_in_dim(unit_in, in_slot * row_count, row_count, 0)
    inverse_own = lax.dynamic_slice_in_dim(inverse_in, in_slot * row_count, row_count, 0)
    in_scaled = grad_normed_in * pre_gain_all
    in_adjusted = (
        in_scaled
        - jnp.mean(in_scaled, axis=-1, keepdims=True)
        - unit_own * jnp.mean(in_scaled * unit_own, axis=-1, keepdims=True)
    )
    tokens_grad = grad_middle + in_adjusted * inverse_own

    small = [vector_own[i * share : (i + 1) * share] for i in range(10)]
    hidden_small = [
        vector_own[narrow + i * hidden_share : narrow + (i + 1) * hidden_share] for i in range(3)
    ]
    return (
        layer_out,
        tokens_grad,
        small[0],
        small[1],
        qkv_weight_grad,
        small[2],
        small[3],
        small[4],
        small[5],
        out_weight_own,
        small[6],
        small[7],
        small[8],
        hidden_small[0],
        hidden_small[1],
        hidden_small[2],
        small[9],
        up_weight_grad,
        down_weight_grad,
    )


def solution(mesh):
    flat, matrix = P(("rows", "ffn")), P(("rows", "ffn"), None)
    in_specs = (
        matrix, P("rows", None), P("rows"), flat, flat, matrix, flat, flat, flat, flat, matrix, flat, flat, flat,
        flat, flat, flat, flat, P("rows", "ffn"), P("ffn", "rows"), matrix,
    )
    out_specs = (
        matrix, matrix, flat, flat, matrix, flat, flat, flat, flat, matrix, flat, flat, flat, flat, flat, flat, flat,
        P("rows", "ffn"), P("ffn", "rows"),
    )
    return jax.shard_map(
        functools.partial(body, mesh.shape["rows"], mesh.shape["ffn"]),
        mesh=mesh,
        in_specs=in_specs,
        out_specs=out_specs,
        check_vma=False,
    )
```

```python
import functools

import jax
import jax.numpy as jnp
from jax import lax
from jax.experimental import pallas as pl
from jax.experimental.pallas import tpu as pltpu
from jax.sharding import PartitionSpec as P

HEAD_DIM = 64
FF = 3072
BLOCK = 256

eps = 1e-05
neg_big = -1e30
score_scale = 0.125
root_half = 0.7071067811865476
inv_root_tau = 0.3989422804014327

f32 = jnp.float32
bf16 = jnp.bfloat16


def swap(values, flip):
    return lax.ppermute(values, "ffn", [(i, i ^ flip) for i in range(4)])


def swap_rows(values, flip):
    return lax.ppermute(values, "rows", [(i, i ^ flip) for i in range(8)])


def slot_owner(slot, ffn_index, ffn_size):
    return ffn_index ^ slot if ffn_size == 4 else jnp.int32(slot)


def gather_slots(values, ffn_size):
    if ffn_size != 4:
        whole = lax.all_gather(values, "ffn", axis=0, tiled=False)
        return [whole[i] for i in range(ffn_size)]
    across = swap(values, 2)
    beside = swap(values, 1)
    return [values, beside, across, swap(across, 1)]


def exchange_slots(pieces, ffn_size):
    if ffn_size != 4:
        whole = lax.all_to_all(jnp.stack(pieces), "ffn", split_axis=0, concat_axis=0, tiled=True)
        return [whole[i] for i in range(ffn_size)]
    across = swap(pieces[2], 2)
    slanted = swap(pieces[3], 3)
    beside = swap(pieces[1], 1)
    return [pieces[0], beside, across, slanted]


def in_order(slots, ffn_index, ffn_size):
    if ffn_size != 4:
        return slots
    odd, high = (ffn_index & 1) > 0, (ffn_index & 2) > 0
    low = [jnp.where(odd, slots[p ^ 1], slots[p]) for p in range(4)]
    return [jnp.where(high, low[p ^ 2], low[p]) for p in range(4)]


def sum_slots(pairs, ffn_size):
    values = jnp.concatenate(pairs, axis=0)[:, :4, :]
    if ffn_size != 4:
        return lax.psum(values, "ffn")
    beside = swap(values, 1)
    values = values + jnp.stack([beside[1], beside[0], beside[3], beside[2]])
    across = swap(values, 2)
    return values + jnp.stack([across[2], across[3], across[0], across[1]])


def gather_rows(values, row_index, row_size):
    if row_size != 8:
        return lax.all_gather(values, "rows", axis=0, tiled=False)
    whole = values[None]
    for flip, bit in ((1, row_index & 1), (2, (row_index >> 1) & 1), (6, row_index >> 2)):
        other = swap_rows(whole, flip)
        first = jnp.where(bit > 0, other, whole)
        second = jnp.where(bit > 0, whole, other)
        whole = jnp.concatenate([first[None], second[None]], axis=0)
        whole = whole.reshape((-1,) + values.shape)
    return whole


def reduce_rows(values, row_index, row_size, wait=None):
    if row_size != 8:
        return lax.psum_scatter(values.astype(bf16), "rows", scatter_dimension=0, tiled=True)[0].astype(f32)
    whole = values
    for flip, bit in ((6, row_index >> 2), (2, (row_index >> 1) & 1), (1, row_index & 1)):
        half = whole.shape[0] // 2
        sent = lax.dynamic_slice_in_dim(whole, (1 - bit) * half, half, 0).astype(bf16)
        kept = lax.dynamic_slice_in_dim(whole, bit * half, half, 0).astype(f32)
        if flip == 2 and wait is not None:
            sent = after(sent, wait)
        whole = kept + swap_rows(sent, flip).astype(f32)
    return whole[0]


def after(values, other):
    return values + (other.ravel()[0] * 0).astype(values.dtype)


NT = (((1,), (1,)), ((), ()))


def dot_nt(a, b):
    return lax.dot_general(a, b, NT, preferred_element_type=f32)


def dot_nn(a, b):
    return jnp.dot(a, b, preferred_element_type=f32)


def start_row(first, bounds_ref, bound_count):
    places = first + lax.broadcasted_iota(jnp.int32, (1, BLOCK), 1)
    start = jnp.zeros((1, BLOCK), jnp.int32)
    for i in range(bound_count):
        bound = bounds_ref[i]
        start = jnp.where(places >= bound, jnp.maximum(start, bound), start)
    return places, start


def first_block(first, bounds_ref, bound_count):
    start = jnp.int32(0)
    for i in range(bound_count):
        bound = bounds_ref[i]
        start = jnp.where(first >= bound, jnp.maximum(start, bound), start)
    return start // BLOCK


def load_keys(keep_ref, limit_ref, blocks):
    for j in range(blocks):
        row = keep_ref[j : j + 1, :]
        places = j * BLOCK + lax.broadcasted_iota(jnp.int32, (1, BLOCK), 1)
        limits = jnp.where(row > 0, places, 1 << 24).astype(f32)
        column = jnp.transpose(jnp.broadcast_to(limits, (128, BLOCK)))
        limit_ref[j * BLOCK : (j + 1) * BLOCK, :] = column


def block_bias(limit_ref, key_first, query_places, query_start):
    limit = limit_ref[pl.ds(key_first, BLOCK), :]
    limit = jnp.concatenate([limit] * (BLOCK // 128), axis=1)
    key_places = key_first + lax.broadcasted_iota(jnp.int32, (BLOCK, BLOCK), 0)
    before = (limit < query_places.astype(f32)) & (key_places >= query_start)
    return jnp.where(before | (key_places == query_places), 0.0, neg_big)


def forward_kernel(
    place_ref, bounds_ref, proj_ref, keep_ref, out_ref, lse_ref, limit_ref, value_t_ref, *, heads, bound_count
):
    total = proj_ref.shape[0]
    blocks = total // BLOCK
    width = heads * HEAD_DIM
    load_keys(keep_ref, limit_ref, blocks)
    for j in range(blocks):
        rows = slice(j * BLOCK, (j + 1) * BLOCK)
        value_t_ref[:, rows] = jnp.transpose(proj_ref[rows, 2 * width :].astype(f32)).astype(bf16)

    def query_step(qi, _):
        query_first = pl.multiple_of(qi * BLOCK, BLOCK)
        query_at = pl.multiple_of(place_ref[qi], BLOCK)
        places, starts = start_row(query_first, bounds_ref, bound_count)
        queries = proj_ref[pl.ds(query_at, BLOCK), :width] * jnp.asarray(score_scale, bf16)

        def key_step(kj, carry):
            key_first = pl.multiple_of(kj * BLOCK, BLOCK)
            key_at = pl.multiple_of(place_ref[kj], BLOCK)
            bias = block_bias(limit_ref, key_first, places, starts)
            keys = proj_ref[pl.ds(key_at, BLOCK), width : 2 * width]
            values_t = value_t_ref[:, pl.ds(key_at, BLOCK)]
            out = []
            for h in range(heads):
                cols = slice(h * HEAD_DIM, (h + 1) * HEAD_DIM)
                top, total_sum, mixed = carry[h]
                scores = dot_nt(keys[:, cols], queries[:, cols]) + bias
                new_top = jnp.maximum(top, jnp.max(scores, axis=0, keepdims=True))
                weights = jnp.exp(scores - new_top)
                decay = jnp.exp(top - new_top)
                new_sum = total_sum * decay + jnp.sum(weights, axis=0, keepdims=True)
                new_mixed = mixed * decay + dot_nn(values_t[cols, :], weights.astype(bf16))
                out.append((new_top, new_sum, new_mixed))
            return tuple(out)

        empty = (
            jnp.full((1, BLOCK), neg_big, f32),
            jnp.zeros((1, BLOCK), f32),
            jnp.zeros((HEAD_DIM, BLOCK), f32),
        )
        done = lax.fori_loop(first_block(query_first, bounds_ref, bound_count), qi + 1, key_step, (empty,) * heads)
        mixed_t = jnp.concatenate([mixed / total_sum for _, total_sum, mixed in done], axis=0)
        out_ref[pl.ds(query_at, BLOCK), :] = jnp.transpose(mixed_t).astype(out_ref.dtype)
        for h in range(heads):
            lse_ref[h : h + 1, pl.ds(query_first, BLOCK)] = done[h][0] + jnp.log(done[h][1])
        return 0

    lax.fori_loop(0, blocks, query_step, 0)


def backward_kernel(
    place_ref,
    bounds_ref,
    proj_ref,
    keep_ref,
    mixed_ref,
    grad_ref,
    lse_ref,
    out_ref,
    bias_ref,
    limit_ref,
    key_t_ref,
    key_acc,
    value_acc,
    *,
    heads,
    bound_count,
):
    total = proj_ref.shape[0]
    blocks = total // BLOCK
    width = heads * HEAD_DIM
    load_keys(keep_ref, limit_ref, blocks)
    for j in range(blocks):
        rows = slice(j * BLOCK, (j + 1) * BLOCK)
        key_t_ref[:, rows] = jnp.transpose(proj_ref[rows, width : 2 * width].astype(f32)).astype(bf16)
    key_acc[...] = jnp.zeros_like(key_acc)
    value_acc[...] = jnp.zeros_like(value_acc)
    bias_ref[...] = jnp.zeros_like(bias_ref)

    def query_step(qi, _):
        query_first = pl.multiple_of(qi * BLOCK, BLOCK)
        query_at = pl.multiple_of(place_ref[qi], BLOCK)
        query_rows = pl.ds(query_at, BLOCK)
        places, starts = start_row(query_first, bounds_ref, bound_count)
        queries = proj_ref[query_rows, :width] * jnp.asarray(score_scale, bf16)
        grads = grad_ref[query_rows, :]
        product_t = jnp.transpose(grads.astype(f32) * mixed_ref[query_rows, :].astype(f32))
        lse = [lse_ref[h : h + 1, pl.ds(query_first, BLOCK)] for h in range(heads)]
        delta = [
            jnp.sum(product_t[h * HEAD_DIM : (h + 1) * HEAD_DIM, :], axis=0, keepdims=True) for h in range(heads)
        ]

        def key_step(kj, carry):
            key_first = pl.multiple_of(kj * BLOCK, BLOCK)
            key_rows = pl.ds(pl.multiple_of(place_ref[kj], BLOCK), BLOCK)
            bias = block_bias(limit_ref, key_first, places, starts)
            keys = proj_ref[key_rows, width : 2 * width]
            values = proj_ref[key_rows, 2 * width :]
            keys_t = key_t_ref[:, key_rows]
            out, key_parts, value_parts = [], [], []
            for h in range(heads):
                cols = slice(h * HEAD_DIM, (h + 1) * HEAD_DIM)
                scores = dot_nt(keys[:, cols], queries[:, cols]) + bias
                probs = jnp.exp(scores - lse[h])
                grad_probs = dot_nt(values[:, cols], grads[:, cols])
                grad_scores = (probs * (grad_probs - delta[h])).astype(bf16)
                value_parts.append(dot_nn(probs.astype(bf16), grads[:, cols]))
                key_parts.append(dot_nn(grad_scores, queries[:, cols]))
                out.append(carry[h] + dot_nn(keys_t[cols, :], grad_scores))
            key_acc[key_rows, :] += jnp.concatenate(key_parts, axis=1)
            value_acc[key_rows, :] += jnp.concatenate(value_parts, axis=1)
            return tuple(out)

        zero = jnp.zeros((HEAD_DIM, BLOCK), f32)
        done = lax.fori_loop(first_block(query_first, bounds_ref, bound_count), qi + 1, key_step, (zero,) * heads)
        grad_query = jnp.transpose(jnp.concatenate(done, axis=0)) * score_scale
        bias_ref[0:1, :] += jnp.sum(grad_query, axis=0, keepdims=True)
        out_ref[query_rows, :width] = grad_query.astype(bf16)
        return 0

    lax.fori_loop(0, blocks, query_step, 0)
    bias_ref[1:2, :] = jnp.sum(value_acc[...], axis=0, keepdims=True)
    out_ref[:, width : 2 * width] = key_acc[...].astype(bf16)
    out_ref[:, 2 * width :] = value_acc[...].astype(bf16)


SMEM = pl.BlockSpec(memory_space=pltpu.SMEM)
VMEM = pl.BlockSpec(memory_space=pltpu.VMEM)


def attend_forward(place, bounds, proj, keep, heads):
    total, width = proj.shape[0], heads * HEAD_DIM
    pairs = total * total // 6
    return pl.pallas_call(
        functools.partial(forward_kernel, heads=heads, bound_count=bounds.shape[0]),
        out_shape=(jax.ShapeDtypeStruct((total, width), bf16), jax.ShapeDtypeStruct((heads, total), f32)),
        in_specs=[SMEM, SMEM, VMEM, VMEM],
        out_specs=(VMEM, VMEM),
        scratch_shapes=[pltpu.VMEM((total, 128), f32), pltpu.VMEM((width, total), bf16)],
        compiler_params=pltpu.CompilerParams(vmem_limit_bytes=40 << 20),
        cost_estimate=pl.CostEstimate(
            flops=16 * pairs * width, bytes_accessed=total * width * 8, transcendentals=pairs * heads
        ),
        name="attend_forward",
    )(place, bounds, proj, keep)


def attend_backward(place, bounds, proj, keep, mixed, grads, lse, heads):
    total, width = proj.shape[0], heads * HEAD_DIM
    pairs = total * total // 6
    return pl.pallas_call(
        functools.partial(backward_kernel, heads=heads, bound_count=bounds.shape[0]),
        out_shape=(jax.ShapeDtypeStruct((total, 3 * width), bf16), jax.ShapeDtypeStruct((2, width), f32)),
        in_specs=[SMEM, SMEM, VMEM, VMEM, VMEM, VMEM, VMEM],
        out_specs=(VMEM, VMEM),
        scratch_shapes=[
            pltpu.VMEM((total, 128), f32),
            pltpu.VMEM((width, total), bf16),
            pltpu.VMEM((total, width), f32),
            pltpu.VMEM((total, width), f32),
        ],
        compiler_params=pltpu.CompilerParams(vmem_limit_bytes=50 << 20),
        cost_estimate=pl.CostEstimate(
            flops=40 * pairs * width, bytes_accessed=total * width * 20, transcendentals=pairs * heads
        ),
        name="attend_backward",
    )(place, bounds, proj, keep, mixed, grads, lse)


TN = (((0,), (0,)), ((), ()))
CHUNK = 16
ANY = pl.BlockSpec(memory_space=pl.ANY)


def dot_tn(a, b):
    return lax.dot_general(a, b, TN, preferred_element_type=f32)


def fixed(*shape):
    return pl.BlockSpec(shape, lambda i: (0,) * len(shape))


def columns(rows, width, index):
    return pl.BlockSpec((rows, width), lambda i: (0, index))


def call(kernel, grid, inputs, outputs, name, flops, scratch=(), transcendentals=0):
    moved = sum(a.size * a.dtype.itemsize for a, spec in inputs if spec.memory_space is None)
    return pl.pallas_call(
        kernel,
        grid=(grid,),
        in_specs=[spec for _, spec in inputs],
        out_specs=tuple(spec for _, _, spec in outputs),
        out_shape=tuple(jax.ShapeDtypeStruct(shape, dtype) for shape, dtype, _ in outputs),
        scratch_shapes=list(scratch),
        compiler_params=pltpu.CompilerParams(
            vmem_limit_bytes=58 << 20, dimension_semantics=("arbitrary",)
        ),
        cost_estimate=pl.CostEstimate(flops=flops, bytes_accessed=moved, transcendentals=transcendentals),
        name=name,
    )(*[a for a, _ in inputs])


def row_sum(values):
    return jnp.sum(values, axis=-1, keepdims=True)


def fold(values):
    out = values[:8]
    for i in range(8, values.shape[0], 8):
        out = out + values[i : i + 8]
    return out


def unit_norm(values):
    center = values - jnp.mean(values, axis=-1, keepdims=True)
    inverse = lax.rsqrt(jnp.mean(center * center, axis=-1, keepdims=True) + eps)
    return center * inverse, inverse


def sub_norm(pieces, real, width):
    mean = sum(row_sum(p) for p in pieces) * (1.0 / width)
    centers = [p - mean for p in pieces]
    if real is not None:
        centers = [c * r for c, r in zip(centers, real)]
    inverse = lax.rsqrt(sum(row_sum(c * c) for c in centers) * (1.0 / width) + eps)
    return [c * inverse for c in centers], inverse


def sub_vectors(owner_ref, sub_ref, count, padded):
    rows = [sub_ref[owner_ref[p]] for p in range(count)]
    real = [r[2:3] for r in rows] if padded else None
    return [r[0:1] for r in rows], [r[1:2] for r in rows], real


def front_kernel(weight_ref, bias_ref, vec_ref, *refs, count):
    token_refs, (proj_ref, normed_ref) = refs[:count], refs[count:]
    for s in range(count):
        unit, _ = unit_norm(token_refs[s][...].astype(f32))
        normed = (unit * vec_ref[0:1] + vec_ref[1:2]).astype(bf16)
        normed_ref[s] = normed
        proj_ref[s] = (dot_nn(normed, weight_ref[...]) + bias_ref[...]).astype(bf16)


def middle_forward_kernel(owner_ref, tokens_ref, out_ref, sub_ref, vec_ref, *refs, count, padded):
    piece_refs, (low_ref, middle_ref, ffn_ref) = refs[:count], refs[-3:]
    head_width, width = low_ref.shape[2], middle_ref.shape[1]
    gains, offsets, real = sub_vectors(owner_ref, sub_ref, count, padded)
    units, _ = sub_norm([r[...].astype(f32) for r in piece_refs], real, width)
    middle = tokens_ref[...].astype(f32) + vec_ref[0:1]
    for p in range(count):
        low = (units[p] * gains[p] + offsets[p]).astype(bf16)
        low_ref[p] = low
        rows = pl.ds(pl.multiple_of(owner_ref[p] * head_width, head_width), head_width)
        middle = middle + dot_nn(low, out_ref[rows, :])
    middle_ref[...] = middle
    unit, _ = unit_norm(middle)
    ffn_ref[...] = (unit * vec_ref[1:2] + vec_ref[2:3]).astype(bf16)


def middle_backward_kernel(
    owner_ref, out_grad_ref, middle_ref, out_ref, sub_ref, vec_ref, *refs, count, addends, padded
):
    piece_refs, add_refs = refs[:count], refs[count : count + addends]
    grad_ref, grad_low_ref, head_ref, sums_ref, sub_sums_ref = refs[count + addends :]
    head_width, width = head_ref.shape[2], middle_ref.shape[1]

    @pl.when(pl.program_id(0) == 0)
    def _():
        sums_ref[...] = jnp.zeros_like(sums_ref)
        sub_sums_ref[...] = jnp.zeros_like(sub_sums_ref)

    upstream = sum(r[...].astype(f32) for r in add_refs)
    unit, inverse = unit_norm(middle_ref[...])
    scaled = upstream * vec_ref[1:2]
    out_grad = out_grad_ref[...]
    grad = out_grad + inverse * (
        scaled - row_sum(scaled) * (1.0 / width) - unit * (row_sum(scaled * unit) * (1.0 / width))
    )
    grad_ref[...] = grad
    low = grad.astype(bf16)
    grad_low_ref[...] = low
    for i, terms in enumerate((grad, upstream * unit, upstream, out_grad)):
        sums_ref[i : i + 1, :] += jnp.sum(terms, axis=0, keepdims=True)
    gains, _, real = sub_vectors(owner_ref, sub_ref, count, padded)
    units, sub_inverse = sub_norm([r[...].astype(f32) for r in piece_refs], real, width)
    grads = []
    for p in range(count):
        rows = pl.ds(pl.multiple_of(owner_ref[p] * head_width, head_width), head_width)
        grads.append(dot_nt(low, out_ref[rows, :]))
    sub_scaled = [g * gain for g, gain in zip(grads, gains)]
    mean = sum(row_sum(v) for v in sub_scaled) * (1.0 / width)
    along = sum(row_sum(v * u) for v, u in zip(sub_scaled, units)) * (1.0 / width)
    for p in range(count):
        head_ref[p] = ((sub_scaled[p] - mean - units[p] * along) * sub_inverse).astype(bf16)
        own = owner_ref[p]
        sub_sums_ref[own] += jnp.concatenate(
            [
                jnp.sum(grads[p] * units[p], axis=0, keepdims=True),
                jnp.sum(grads[p], axis=0, keepdims=True),
                jnp.zeros((6, head_width), f32),
            ],
            axis=0,
        )


def out_grad_kernel(owner_ref, low_ref, grad_ref, out_ref, *, count):
    head_width = low_ref.shape[2]
    for p in range(count):
        rows = pl.ds(pl.multiple_of(owner_ref[p] * head_width, head_width), head_width)
        out_ref[rows, :] = dot_tn(low_ref[p], grad_ref[...]).astype(bf16)


def lane_fold(values):
    out = values[:, :128]
    for i in range(128, values.shape[1], 128):
        out = out + values[:, i : i + 128]
    return out


def normal_parts(values):
    density = jnp.exp(-0.5 * values * values)
    t = 1.0 / (1.0 + (0.3275911 * root_half) * jnp.abs(values))
    series = 0.5 * 1.061405429
    for c in (-1.453152027, 1.421413741, -0.284496736, 0.254829592):
        series = series * t + 0.5 * c
    tail = series * t * density
    return jnp.where(values >= 0, 1.0 - tail, tail), density


def up_kernel(up_ref, down_ref, vec_ref, *refs, count, waits):
    row_refs, grad_refs = refs[:count], refs[count : 2 * count]
    act_ref, slope_ref, back_ref, stat_ref, sums_ref, pre_ref, hid_ref, part_ref = refs[2 * count + waits :]
    rows = row_refs[0].shape[0]

    @pl.when(pl.program_id(0) == 0)
    def _():
        sums_ref[...] = jnp.zeros_like(sums_ref)

    for s in range(count):
        pre_ref[...] = dot_nn(row_refs[s][...], up_ref[...])
        hid_ref[...] = dot_nn(grad_refs[s][...], down_ref[...])

        def step(c, total):
            at = pl.ds(pl.multiple_of(c * CHUNK, CHUNK), CHUNK)
            pre = pre_ref[at, :] + vec_ref[0:1]
            phi, density = normal_parts(pre)
            activated = pre * phi
            back = hid_ref[at, :]
            scaled = back * vec_ref[1:2]
            act_ref[s, at, :] = activated
            slope_ref[s, at, :] = (phi + pre * inv_root_tau * density).astype(bf16)
            back_ref[s, at, :] = back.astype(bf16)
            for i, terms in enumerate((activated, activated * activated, scaled, scaled * activated)):
                part_ref[i, at, :] = lane_fold(terms)
            return total + fold(back)

        total = lax.fori_loop(0, rows // CHUNK, step, jnp.zeros((8, pre_ref.shape[1]), f32), unroll=4)
        sums_ref[...] += total
        for i in range(4):
            stat_ref[s, i : i + 1, :] = jnp.sum(jnp.transpose(part_ref[i]), axis=0, keepdims=True)


def back_kernel(up_ref, vec_ref, act_ref, slope_ref, back_ref, stat_ref, *refs, count):
    hidden_ref, pre_ref, in_ref, sums_ref, col_ref = refs[-5:]
    rows, width = act_ref.shape[1:]

    @pl.when(pl.program_id(0) == 0)
    def _():
        sums_ref[...] = jnp.zeros_like(sums_ref)

    for s in range(count):
        stats = stat_ref[s] * (1.0 / FF)
        mean, back_mean = stats[0:1], stats[2:3]
        inverse = lax.rsqrt(stats[1:2] - mean * mean + eps)
        along = (stats[3:4] - mean * back_mean) * inverse
        for i, line in enumerate((mean, inverse, back_mean, along)):
            col_ref[i] = jnp.transpose(jnp.broadcast_to(line, (128, rows)))

        def step(c, totals):
            at = pl.ds(pl.multiple_of(c * CHUNK, CHUNK), CHUNK)
            spread = [jnp.concatenate([col_ref[i, at, :]] * (width // 128), axis=1) for i in range(4)]
            normed = (act_ref[s, at, :] - spread[0]) * spread[1]
            back = back_ref[s, at, :].astype(f32)
            hidden_ref[s, at, :] = (normed * vec_ref[1:2] + vec_ref[2:3]).astype(bf16)
            inner = back * vec_ref[1:2] - spread[2] - normed * spread[3]
            grad = inner * (spread[1] * slope_ref[s, at, :].astype(f32))
            pre_ref[s, at, :] = grad.astype(bf16)
            return totals[0] + fold(grad), totals[1] + fold(back * normed)

        zero = jnp.zeros((8, width), f32)
        first, second = lax.fori_loop(0, rows // CHUNK, step, (zero, zero), unroll=4)
        sums_ref[0] += first
        sums_ref[1] += second
        in_ref[s] = dot_nt(pre_ref[s], up_ref[...]).astype(bf16)


def ffn_grad_kernel(down_ref, *refs, count, pairs):
    row_refs, grad_refs = refs[:count], refs[count : 2 * count]
    hidden_refs, pre_refs = refs[2 * count : 2 * count + pairs], refs[2 * count + pairs : 2 * count + 2 * pairs]
    out_ref, down_out_ref, up_acc, down_acc = refs[2 * count + 2 * pairs :]
    hidden_width = down_ref.shape[1]
    step = pl.program_id(0)

    @pl.when(step == 0)
    def _():
        up_acc[...] = jnp.zeros_like(up_acc)
        down_acc[...] = jnp.zeros_like(down_acc)

    rows_all = jnp.concatenate([r[...] for r in row_refs], axis=0)
    grads_all = jnp.concatenate([r[...] for r in grad_refs], axis=0)
    hidden = jnp.concatenate([r[i] for r in hidden_refs for i in range(r.shape[0])], axis=0)
    pre = jnp.concatenate([r[i] for r in pre_refs for i in range(r.shape[0])], axis=0)
    up_acc[...] += dot_tn(rows_all, pre)
    down_acc[...] += dot_tn(grads_all, hidden)
    rows = row_refs[0].shape[0]
    down = dot_nt(hidden, down_ref[...]).astype(bf16)
    for i in range(count):
        down_out_ref[i] = down[i * rows : (i + 1) * rows]

    @pl.when(step == pl.num_programs(0) - 1)
    def _():
        out_ref[:, :hidden_width] = up_acc[...].astype(bf16)
        out_ref[:, hidden_width:] = down_acc[...].astype(bf16)


def in_grad_kernel(weight_ref, *refs, count):
    token_refs, proj_refs = refs[:count], refs[count : 2 * count]
    out_ref, sums_ref = refs[-2:]

    @pl.when(pl.program_id(0) == 0)
    def _():
        sums_ref[...] = jnp.zeros_like(sums_ref)

    for s in range(count):
        unit, _ = unit_norm(token_refs[s][...].astype(f32))
        grad = dot_nt(proj_refs[s][...], weight_ref[...])
        out_ref[s] = grad.astype(bf16)
        sums_ref[0] += fold(grad * unit)
        sums_ref[1] += fold(grad)


def qkv_grad_kernel(normed_ref, proj_ref, *refs):
    out_ref, acc_ref = refs[-2:]
    step = pl.program_id(0)

    @pl.when(step == 0)
    def _():
        acc_ref[...] = jnp.zeros_like(acc_ref)

    acc_ref[...] += dot_tn(normed_ref[...], proj_ref[...])

    @pl.when(step == pl.num_programs(0) - 1)
    def _():
        out_ref[...] = acc_ref[...].astype(bf16)


def body(
    row_size,
    ffn_size,
    tokens,
    seq_lengths,
    key_keep,
    pre_gain,
    pre_bias,
    qkv_weight,
    query_bias,
    value_bias,
    sub_gain,
    sub_bias,
    out_weight,
    out_bias,
    ffn_gain,
    ffn_bias,
    up_bias,
    hidden_gain,
    hidden_bias,
    down_bias,
    up_weight,
    down_weight,
    out_grad,
):
    ffn_index, row_index = lax.axis_index("ffn"), lax.axis_index("rows")
    devices = row_size * ffn_size
    row_count, width = tokens.shape
    pack_total = row_count * ffn_size
    head_count = width // HEAD_DIM
    heads = -(-head_count // ffn_size)
    head_width = heads * HEAD_DIM
    three = 3 * head_width
    padded = head_width * ffn_size
    extra = padded - width
    hidden_width = up_weight.shape[1]
    share, hidden_share = pre_gain.shape[0], up_bias.shape[0]
    share_rows = -(-(share + 3) // 16) * 16
    owners = [slot_owner(p, ffn_index, ffn_size) for p in range(ffn_size)]
    owner_row = jnp.stack(owners).astype(jnp.int32)
    slots = range(ffn_size)
    pairs = [(i, i + 1) for i in range(0, ffn_size, 2)]
    steps = row_count // BLOCK

    thirds = jnp.pad(qkv_weight.reshape(share, 3, width), ((0, 0), (0, 0), (0, extra)))
    pieces = thirds.reshape(share, 3, ffn_size, head_width).transpose(2, 0, 1, 3)
    pieces = pieces.reshape(ffn_size, share, three)
    lines = [
        pre_gain, pre_bias, query_bias, value_bias, sub_gain, sub_bias, out_bias, ffn_gain, ffn_bias, down_bias,
        up_bias, hidden_gain, hidden_bias,
    ]
    line_rows = -(-18 * hidden_share // three)
    lines = jnp.stack([jnp.pad(v, (0, hidden_share - v.shape[0])) for v in lines])
    lines = jnp.pad(lines, ((0, 5), (0, 0))).reshape(1, -1)
    lines = jnp.pad(lines, ((0, 0), (0, line_rows * three - lines.shape[1]))).reshape(line_rows, three)
    lines = jnp.pad(lines, ((0, share_rows - share - line_rows), (0, 0)))
    pieces = jnp.concatenate([pieces, jnp.broadcast_to(lines, (ffn_size,) + lines.shape)], axis=1)
    pieces = in_order([pieces[i] for i in slots], ffn_index, ffn_size)
    pieces = in_order(exchange_slots(pieces, ffn_size), ffn_index, ffn_size)
    token_slots = gather_slots(tokens, ffn_size)
    gathered = gather_rows(jnp.concatenate(pieces, axis=0), row_index, row_size)
    gathered = gathered.reshape(devices, share_rows, three)
    qkv_own = gathered[:, :share, :].reshape(width, three)
    lines_all = gathered[:, share : share + line_rows, :].astype(f32).reshape(devices, line_rows * three)
    lines_all = lines_all[:, : 18 * hidden_share].reshape(devices, 18, hidden_share)
    wide = lines_all[:, :10, :share].transpose(1, 0, 2).reshape(10, width)
    hidden_vectors = lax.dynamic_slice_in_dim(lines_all[:, 10:13], ffn_index * row_size, row_size, 0)
    hidden_vectors = hidden_vectors.transpose(1, 0, 2).reshape(3, hidden_width)
    narrow = 10 * share
    hidden_vectors = jnp.pad(hidden_vectors, ((0, 5), (0, 0)))
    middle_vectors = jnp.pad(wide[6:9], ((0, 5), (0, 0)))
    sub_rows = jnp.pad(
        jnp.concatenate([wide[4:6], jnp.ones((1, width), f32)], axis=0), ((0, 5), (0, extra))
    )
    sub_rows = sub_rows.reshape(8, ffn_size, head_width).transpose(1, 0, 2)

    out_rows = jnp.concatenate(in_order(gather_slots(out_weight, ffn_size), ffn_index, ffn_size), axis=0)
    weight_rows = after(jnp.concatenate([up_weight, down_weight.T, out_rows], axis=1), gathered)
    weights_all = lax.all_gather(weight_rows, "rows", axis=0, tiled=True)
    up_in = (weights_all, columns(width, hidden_width, 0))
    down_in = (weights_all, columns(width, hidden_width, 1))
    if extra:
        out_in = (
            jnp.pad(weights_all[:, 2 * hidden_width :], ((0, extra), (0, 0))),
            columns(padded, width, 0),
        )
    else:
        out_in = (weights_all, columns(width, width, 2 * hidden_width // width))

    grad_low = after(out_grad, token_slots[-1]).astype(bf16)
    grad_slots = gather_slots(grad_low, ffn_size)

    own_bias = [
        lax.dynamic_slice_in_dim(jnp.pad(wide[i], (0, extra)), ffn_index * head_width, head_width, 0) for i in (2, 3)
    ]
    bias_row = jnp.concatenate([own_bias[0], jnp.zeros((head_width,), f32), own_bias[1]])
    block_row = pl.BlockSpec((BLOCK, width), lambda i: (i, 0))
    proj, normed_low = call(
        functools.partial(front_kernel, count=ffn_size),
        steps,
        [(qkv_own, fixed(width, three)), (bias_row[None], fixed(1, three)), (wide, fixed(10, width))]
        + [(t, block_row) for t in token_slots],
        [
            ((ffn_size, row_count, three), bf16, pl.BlockSpec((ffn_size, BLOCK, three), lambda i: (0, i, 0))),
            ((ffn_size, row_count, width), bf16, pl.BlockSpec((ffn_size, BLOCK, width), lambda i: (0, i, 0))),
        ],
        "front",
        2 * pack_total * width * three,
    )
    proj, normed_low = proj.reshape(pack_total, three), normed_low.reshape(pack_total, width)

    bounds, running = [], jnp.int32(0)
    for i in range(seq_lengths.shape[1] - 1):
        running = running + seq_lengths[0, i]
        bounds.append(running)
    bounds = jnp.stack(bounds)
    firsts = jnp.arange(pack_total // BLOCK, dtype=jnp.int32) * BLOCK
    block_owner = firsts // row_count
    place = (block_owner ^ ffn_index if ffn_size == 4 else block_owner) * row_count + firsts % row_count
    keep = key_keep.reshape(pack_total // BLOCK, BLOCK)
    mixed_own, lse = attend_forward(place, bounds, proj, keep, heads)

    mixed_slots = exchange_slots(
        [mixed_own[p * row_count : (p + 1) * row_count] for p in slots], ffn_size
    )
    block_piece = pl.BlockSpec((BLOCK, head_width), lambda i: (i, 0))
    block_pieces = pl.BlockSpec((ffn_size, BLOCK, head_width), lambda i: (0, i, 0))
    middle_in = [out_in, (sub_rows, fixed(ffn_size, 8, head_width)), (middle_vectors, fixed(8, width))]
    sub_low, middle, ffn_low = call(
        functools.partial(middle_forward_kernel, count=ffn_size, padded=bool(extra)),
        steps,
        [(owner_row, SMEM), (tokens, block_row), *middle_in, *[(m, block_piece) for m in mixed_slots]]
        + [(grad_slots[-1], ANY)],
        [
            ((ffn_size, row_count, head_width), bf16, block_pieces),
            ((row_count, width), f32, block_row),
            ((row_count, width), bf16, block_row),
        ],
        "middle_forward",
        2 * row_count * padded * width,
    )

    block_pair = pl.BlockSpec((2, BLOCK, hidden_width), lambda i: (0, i, 0))
    block_pair_row = pl.BlockSpec((2, BLOCK, width), lambda i: (0, i, 0))
    block_stat = pl.BlockSpec((2, 8, BLOCK), lambda i: (0, 0, i))
    block_four = pl.BlockSpec((2, 4, BLOCK), lambda i: (0, 0, i))
    hidden_in = (hidden_vectors, fixed(8, hidden_width))
    pair_shape = (2, row_count, hidden_width)

    def up_pair(rows, grads, waits):
        return call(
            functools.partial(up_kernel, count=2, waits=len(waits)),
            steps,
            [up_in, down_in, hidden_in, *[(r, block_row) for r in rows], *[(g, block_row) for g in grads]]
            + [(w, ANY) for w in waits],
            [
                (pair_shape, f32, block_pair),
                (pair_shape, bf16, block_pair),
                (pair_shape, bf16, block_pair),
                ((2, 8, row_count), f32, block_stat),
                ((8, hidden_width), f32, fixed(8, hidden_width)),
            ],
            "up",
            8 * row_count * width * hidden_width,
            [
                pltpu.VMEM((BLOCK, hidden_width), f32),
                pltpu.VMEM((BLOCK, hidden_width), f32),
                pltpu.VMEM((4, BLOCK, 128), f32),
            ],
            4 * row_count * hidden_width,
        )

    if ffn_size == 4:
        across, beside = swap(ffn_low, 2), swap(ffn_low, 1)
        ups = [up_pair([ffn_low, beside], grad_slots[:2], [])]
        slanted = swap(after(across, ups[0][3]), 1)
        row_slots = [ffn_low, beside, across, slanted]
        ups.append(up_pair([across, slanted], grad_slots[2:], [ups[0][3]]))
    else:
        row_slots = gather_slots(ffn_low, ffn_size)
        ups = [up_pair(row_slots[i : i + 2], grad_slots[i : i + 2], []) for i, _ in pairs]
    stats = sum_slots([u[3] for u in ups], ffn_size)
    backs, wait_for = [None] * len(pairs), []
    for k in reversed(range(len(pairs))):
        act, slope, back = ups[k][:3]
        backs[k] = call(
            functools.partial(back_kernel, count=2),
            steps,
            [up_in, hidden_in, (act, block_pair), (slope, block_pair), (back, block_pair)]
            + [(stats[2 * k : 2 * k + 2], block_four), *[(w, ANY) for w in wait_for]],
            [
                (pair_shape, bf16, block_pair),
                (pair_shape, bf16, block_pair),
                ((2, row_count, width), bf16, block_pair_row),
                ((2, 8, hidden_width), f32, fixed(2, 8, hidden_width)),
            ],
            "back",
            4 * row_count * width * hidden_width,
            [pltpu.VMEM((4, BLOCK, 128), f32)],
        )
        wait_for = [backs[k][2]]

    def reduce_pairs(near, far, wait=None):
        passed = swap(far[1], 1)
        sent = (far[0].astype(f32) + passed.astype(f32)).astype(bf16)
        across = swap(sent if wait is None else after(sent, wait), 2)
        return [near[0], swap(near[1], 1), across], sent

    def scatter_pairs(parts):
        return [lax.psum_scatter(jnp.concatenate(parts, axis=0), "ffn", scatter_dimension=0, tiled=True)[0]]

    if ffn_size == 4:
        in_terms, _ = reduce_pairs(backs[0][2], backs[1][2])
    else:
        in_terms = scatter_pairs([b[2] for b in backs])
    block_quarter = pl.BlockSpec((BLOCK // 2, width), lambda i: (i, 0))
    block_pair_quarter = pl.BlockSpec((2, BLOCK // 2, hidden_width), lambda i: (0, i, 0))
    weight_grads, down_parts = call(
        functools.partial(ffn_grad_kernel, count=ffn_size, pairs=len(pairs)),
        2 * steps,
        [down_in, *[(r, block_quarter) for r in row_slots], *[(g, block_quarter) for g in grad_slots]]
        + [(b[0], block_pair_quarter) for b in backs]
        + [(b[1], block_pair_quarter) for b in backs],
        [
            ((width, 2 * hidden_width), bf16, fixed(width, 2 * hidden_width)),
            (
                (ffn_size, row_count, width),
                bf16,
                pl.BlockSpec((ffn_size, BLOCK // 2, width), lambda i: (0, i, 0)),
            ),
        ],
        "ffn_grads",
        6 * pack_total * width * hidden_width,
        [pltpu.VMEM((width, hidden_width), f32), pltpu.VMEM((width, hidden_width), f32)],
    )
    weight_grads = lax.psum_scatter(weight_grads, "rows", scatter_dimension=0, tiled=True)
    up_weight_grad = weight_grads[:, :hidden_width].astype(f32)
    down_weight_grad = weight_grads[:, hidden_width:].astype(f32).T

    grad_middle, middle_low, head_low, middle_sums, sub_sums = call(
        functools.partial(
            middle_backward_kernel, count=ffn_size, addends=len(in_terms), padded=bool(extra)
        ),
        steps,
        [(owner_row, SMEM), (out_grad, block_row), (middle, block_row), *middle_in]
        + [(m, block_piece) for m in mixed_slots]
        + [(t, block_row) for t in in_terms],
        [
            ((row_count, width), f32, block_row),
            ((row_count, width), bf16, block_row),
            ((ffn_size, row_count, head_width), bf16, block_pieces),
            ((8, width), f32, fixed(8, width)),
            ((ffn_size, 8, head_width), f32, fixed(ffn_size, 8, head_width)),
        ],
        "middle_backward",
        2 * row_count * padded * width,
    )
    grad_own = jnp.concatenate(exchange_slots([head_low[p] for p in slots], ffn_size), axis=0)
    (out_part,) = call(
        functools.partial(out_grad_kernel, count=ffn_size),
        1,
        [(owner_row, SMEM), (sub_low, fixed(ffn_size, row_count, head_width)), (middle_low, fixed(row_count, width))],
        [((padded, width), bf16, fixed(padded, width))],
        "out_grads",
        2 * row_count * padded * width,
    )
    special = ffn_size == 4 and row_size == 8
    if special:
        shares = out_part.reshape(row_size, ffn_size, share, width).transpose(1, 0, 2, 3)
        shares = in_order([shares[i].astype(f32) for i in slots], ffn_index, ffn_size)
        passed = swap(jnp.stack([shares[1], shares[3]]).astype(bf16), 1).astype(f32)
        across = swap(after((shares[2] + passed[1]).astype(bf16), grad_own), 2).astype(f32)
        out_share = shares[0] + passed[0] + across
    else:
        out_weight_own = lax.psum_scatter(
            out_part[:width], ("rows", "ffn"), scatter_dimension=0, tiled=True
        ).astype(f32)

    if ffn_size == 4:
        down_terms, _ = reduce_pairs(down_parts[:2], down_parts[2:], grad_own)
    else:
        down_terms = scatter_pairs([down_parts])
    layer_out = (middle + sum(t.astype(f32) for t in down_terms) + wide[9]).astype(bf16)

    grad_proj, head_bias_grads = attend_backward(place, bounds, proj, keep, mixed_own, grad_own, lse, heads)

    def in_pair(k, waits):
        proj_specs = [
            pl.BlockSpec((BLOCK, three), lambda i, p=p: (p * steps + i, 0)) for p in pairs[k]
        ]
        return call(
            functools.partial(in_grad_kernel, count=2),
            steps,
            [(qkv_own, fixed(width, three)), *[(token_slots[p], block_row) for p in pairs[k]]]
            + [(grad_proj, spec) for spec in proj_specs]
            + [(w, ANY) for w in waits],
            [
                ((2, row_count, width), bf16, block_pair_row),
                ((2, 8, width), f32, fixed(2, 8, width)),
            ],
            "in_grads",
            4 * row_count * width * three,
        )

    def qkv_grads(waits):
        return call(
            qkv_grad_kernel,
            ffn_size,
            [
                (normed_low, pl.BlockSpec((row_count, width), lambda i: (i, 0))),
                (grad_proj, pl.BlockSpec((row_count, three), lambda i: (i, 0))),
            ]
            + [(w, ANY) for w in waits],
            [((width, three), bf16, fixed(width, three))],
            "qkv_grads",
            2 * pack_total * width * three,
            [pltpu.VMEM((width, three), f32)],
        )[0]

    if ffn_size == 4:
        far = in_pair(1, [down_terms[2]])
        qkv_grad = qkv_grads([far[0]])
        passed = swap(far[0][1], 1)
        sent = (far[0][0].astype(f32) + passed.astype(f32)).astype(bf16)
        across = swap(sent, 2)
        near = in_pair(0, [sent])
        in_terms = [near[0][0], swap(near[0][1], 1), across]
        in_parts = [near, far]
    else:
        in_parts = [in_pair(k, []) for k in range(len(pairs))]
        in_terms = scatter_pairs([p[0] for p in in_parts])
        qkv_grad = qkv_grads([])

    def own_heads(values):
        spread = lax.dynamic_update_slice_in_dim(jnp.zeros((2, padded), f32), values, ffn_index * head_width, 1)
        return spread[:, :width]

    in_sums = jnp.sum(sum(p[1] for p in in_parts), axis=1)
    sub_flat = sub_sums[:, :2].transpose(1, 0, 2).reshape(2, padded)[:, :width]
    wide_grads = jnp.concatenate([in_sums, own_heads(head_bias_grads), sub_flat, middle_sums[:4]], axis=0)
    wide_grads = wide_grads.reshape(10, devices, share).transpose(1, 0, 2).reshape(devices, narrow)
    back_sums = jnp.sum(sum(b[3] for b in backs), axis=1)
    hidden_grads = jnp.concatenate([back_sums, jnp.sum(sum(u[4] for u in ups), axis=0)[None]], axis=0)
    hidden_grads = hidden_grads.reshape(3, row_size, hidden_share).transpose(1, 0, 2).reshape(row_size, 3 * hidden_share)
    hidden_grads = lax.dynamic_update_slice_in_dim(
        jnp.zeros((devices, 3 * hidden_share), f32), hidden_grads, ffn_index * row_size, 0
    )
    vector_grads = jnp.concatenate([wide_grads, hidden_grads], axis=1)
    vector_grads = jnp.pad(vector_grads, ((0, 0), (0, three - vector_grads.shape[1]))).astype(bf16)
    packed = jnp.concatenate(
        [qkv_grad.reshape(devices, share, three), vector_grads[:, None, :]], axis=1
    ).reshape(row_size, ffn_size * (share + 1), three)
    taken = ffn_size * (share + 1)
    if special:
        out_rows_count = share * width // three
        tail_rows = out_share.astype(bf16).reshape(row_size, out_rows_count, three)
        packed = jnp.concatenate([packed, tail_rows], axis=1)
    packed = reduce_rows(packed, row_index, row_size, across if special else None)
    if special:
        out_weight_own = packed[taken:].reshape(share, width)
    packed = packed[:taken].astype(bf16).reshape(ffn_size, share + 1, three)
    packed = in_order([packed[i] for i in slots], ffn_index, ffn_size)
    packed = in_order(exchange_slots(packed, ffn_size), ffn_index, ffn_size)
    packed = jnp.stack(packed).astype(f32)
    vector_own = jnp.sum(packed[:, share, :], axis=0)
    qkv_weight_grad = packed[:, :share, :].reshape(ffn_size, share, 3, head_width).transpose(1, 2, 0, 3)
    qkv_weight_grad = qkv_weight_grad.reshape(share, 3, padded)[:, :, :width].reshape(share, 3 * width)

    unit_own, inverse_own = unit_norm(tokens.astype(f32))
    in_scaled = sum(t.astype(f32) for t in in_terms) * wide[0]
    in_adjusted = (
        in_scaled
        - jnp.mean(in_scaled, axis=-1, keepdims=True)
        - unit_own * jnp.mean(in_scaled * unit_own, axis=-1, keepdims=True)
    )
    tokens_grad = grad_middle + in_adjusted * inverse_own

    small = [vector_own[i * share : (i + 1) * share] for i in range(10)]
    hidden_small = [
        vector_own[narrow + i * hidden_share : narrow + (i + 1) * hidden_share] for i in range(3)
    ]
    return (
        layer_out,
        tokens_grad,
        small[0],
        small[1],
        qkv_weight_grad,
        small[2],
        small[3],
        small[4],
        small[5],
        out_weight_own,
        small[6],
        small[7],
        small[8],
        hidden_small[0],
        hidden_small[1],
        hidden_small[2],
        small[9],
        up_weight_grad,
        down_weight_grad,
    )


def solution(mesh):
    flat, matrix = P(("rows", "ffn")), P(("rows", "ffn"), None)
    in_specs = (
        matrix, P("rows", None), P("rows"), flat, flat, matrix, flat, flat, flat, flat, matrix, flat, flat, flat,
        flat, flat, flat, flat, P("rows", "ffn"), P("ffn", "rows"), matrix,
    )
    out_specs = (
        matrix, matrix, flat, flat, matrix, flat, flat, flat, flat, matrix, flat, flat, flat, flat, flat, flat, flat,
        P("rows", "ffn"), P("ffn", "rows"),
    )
    return jax.shard_map(
        functools.partial(body, mesh.shape["rows"], mesh.shape["ffn"]),
        mesh=mesh,
        in_specs=in_specs,
        out_specs=out_specs,
        check_vma=False,
    )
```

```python
import functools

import jax
import jax.numpy as jnp
from jax import lax
from jax.experimental import pallas as pl
from jax.experimental.pallas import tpu as pltpu
from jax.sharding import PartitionSpec as P

HEAD_DIM = 64
FF = 3072
BLOCK = 256

eps = 1e-05
neg_big = -1e30
score_scale = 0.125
root_half = 0.7071067811865476
inv_root_tau = 0.3989422804014327

f32 = jnp.float32
bf16 = jnp.bfloat16


def swap(values, flip):
    return lax.ppermute(values, "ffn", [(i, i ^ flip) for i in range(4)])


def swap_rows(values, flip):
    return lax.ppermute(values, "rows", [(i, i ^ flip) for i in range(8)])


def slot_owner(slot, ffn_index, ffn_size):
    return ffn_index ^ slot if ffn_size == 4 else jnp.int32(slot)


def gather_slots(values, ffn_size):
    if ffn_size != 4:
        whole = lax.all_gather(values, "ffn", axis=0, tiled=False)
        return [whole[i] for i in range(ffn_size)]
    across = swap(values, 2)
    beside = swap(values, 1)
    return [values, beside, across, swap(across, 1)]


def exchange_slots(pieces, ffn_size):
    if ffn_size != 4:
        whole = lax.all_to_all(jnp.stack(pieces), "ffn", split_axis=0, concat_axis=0, tiled=True)
        return [whole[i] for i in range(ffn_size)]
    across = swap(pieces[2], 2)
    slanted = swap(pieces[3], 3)
    beside = swap(pieces[1], 1)
    return [pieces[0], beside, across, slanted]


def in_order(slots, ffn_index, ffn_size):
    if ffn_size != 4:
        return slots
    odd, high = (ffn_index & 1) > 0, (ffn_index & 2) > 0
    low = [jnp.where(odd, slots[p ^ 1], slots[p]) for p in range(4)]
    return [jnp.where(high, low[p ^ 2], low[p]) for p in range(4)]


def sum_slots(pairs, ffn_size):
    values = jnp.concatenate(pairs, axis=0)[:, :4, :]
    if ffn_size != 4:
        return lax.psum(values, "ffn")
    beside = swap(values, 1)
    values = values + jnp.stack([beside[1], beside[0], beside[3], beside[2]])
    across = swap(values, 2)
    return values + jnp.stack([across[2], across[3], across[0], across[1]])


ROW_AXIS = {4: 0, 2: 1, 1: 2}


def row_bit(flip, row_index):
    return (row_index >> (2 - ROW_AXIS[flip])) & 1


def row_step(whole, flip, row_index, outer=0, wait=None):
    bit = row_bit(flip, row_index)
    other = swap_rows(whole, flip)
    if wait is not None:
        other = after(other, wait)
    return jnp.stack([jnp.where(bit > 0, other, whole), jnp.where(bit > 0, whole, other)], axis=outer)


def row_split(whole, flip, row_index):
    axis, bit = ROW_AXIS[flip], row_bit(flip, row_index)
    sent = lax.dynamic_slice_in_dim(whole, 1 - bit, 1, axis).astype(bf16)
    return sent, lax.dynamic_slice_in_dim(whole, bit, 1, axis).astype(f32)


def split_add(whole, flip, row_index, wait=None):
    sent, kept = row_split(whole, flip, row_index)
    other = swap_rows(sent, flip)
    return kept + (other if wait is None else after(other, wait)).astype(f32), sent


def row_halves(whole, flips, row_index, waits):
    sends = []
    for flip, wait in zip(flips, waits):
        sent, kept = row_split(whole, flip, row_index)
        sends.append(sent)
        other = swap_rows(sent, flip)
        whole = kept + (other if wait is None else after(other, wait)).astype(f32)
    return whole[0, 0, 0], sends


def after(values, other):
    return values + (other.ravel()[0] * 0).astype(values.dtype)


NT = (((1,), (1,)), ((), ()))


def dot_nt(a, b):
    return lax.dot_general(a, b, NT, preferred_element_type=f32)


def dot_nn(a, b):
    return jnp.dot(a, b, preferred_element_type=f32)


def start_row(first, bounds_ref, bound_count):
    places = first + lax.broadcasted_iota(jnp.int32, (1, BLOCK), 1)
    start = jnp.zeros((1, BLOCK), jnp.int32)
    for i in range(bound_count):
        bound = bounds_ref[i]
        start = jnp.where(places >= bound, jnp.maximum(start, bound), start)
    return places, start


def first_block(first, bounds_ref, bound_count):
    start = jnp.int32(0)
    for i in range(bound_count):
        bound = bounds_ref[i]
        start = jnp.where(first >= bound, jnp.maximum(start, bound), start)
    return start // BLOCK


def load_keys(keep_ref, limit_ref, blocks):
    for j in range(blocks):
        row = keep_ref[j : j + 1, :]
        places = j * BLOCK + lax.broadcasted_iota(jnp.int32, (1, BLOCK), 1)
        limits = jnp.where(row > 0, places, 1 << 24).astype(f32)
        column = jnp.transpose(jnp.broadcast_to(limits, (128, BLOCK)))
        limit_ref[j * BLOCK : (j + 1) * BLOCK, :] = column


def block_bias(limit_ref, key_first, query_places, query_start):
    limit = limit_ref[pl.ds(key_first, BLOCK), :]
    limit = jnp.concatenate([limit] * (BLOCK // 128), axis=1)
    key_places = key_first + lax.broadcasted_iota(jnp.int32, (BLOCK, BLOCK), 0)
    before = (limit < query_places.astype(f32)) & (key_places >= query_start)
    return jnp.where(before | (key_places == query_places), 0.0, neg_big)


def forward_kernel(
    place_ref, bounds_ref, proj_ref, keep_ref, *refs, heads, bound_count
):
    out_ref, lse_ref, limit_ref, value_t_ref, _ = refs[-5:]
    total = proj_ref.shape[0]
    blocks = total // BLOCK
    width = heads * HEAD_DIM
    load_keys(keep_ref, limit_ref, blocks)
    for j in range(blocks):
        rows = slice(j * BLOCK, (j + 1) * BLOCK)
        value_t_ref[:, rows] = jnp.transpose(proj_ref[rows, 2 * width :].astype(f32)).astype(bf16)

    def query_step(qi, _):
        query_first = pl.multiple_of(qi * BLOCK, BLOCK)
        query_at = pl.multiple_of(place_ref[qi], BLOCK)
        places, starts = start_row(query_first, bounds_ref, bound_count)
        queries = proj_ref[pl.ds(query_at, BLOCK), :width] * jnp.asarray(score_scale, bf16)

        def key_step(kj, carry):
            key_first = pl.multiple_of(kj * BLOCK, BLOCK)
            key_at = pl.multiple_of(place_ref[kj], BLOCK)
            bias = block_bias(limit_ref, key_first, places, starts)
            keys = proj_ref[pl.ds(key_at, BLOCK), width : 2 * width]
            values_t = value_t_ref[:, pl.ds(key_at, BLOCK)]
            out = []
            for h in range(heads):
                cols = slice(h * HEAD_DIM, (h + 1) * HEAD_DIM)
                top, total_sum, mixed = carry[h]
                scores = dot_nt(keys[:, cols], queries[:, cols]) + bias
                new_top = jnp.maximum(top, jnp.max(scores, axis=0, keepdims=True))
                weights = jnp.exp(scores - new_top)
                decay = jnp.exp(top - new_top)
                new_sum = total_sum * decay + jnp.sum(weights, axis=0, keepdims=True)
                new_mixed = mixed * decay + dot_nn(values_t[cols, :], weights.astype(bf16))
                out.append((new_top, new_sum, new_mixed))
            return tuple(out)

        empty = (
            jnp.full((1, BLOCK), neg_big, f32),
            jnp.zeros((1, BLOCK), f32),
            jnp.zeros((HEAD_DIM, BLOCK), f32),
        )
        done = lax.fori_loop(first_block(query_first, bounds_ref, bound_count), qi + 1, key_step, (empty,) * heads)
        mixed_t = jnp.concatenate([mixed / total_sum for _, total_sum, mixed in done], axis=0)
        out_ref[pl.ds(query_at, BLOCK), :] = jnp.transpose(mixed_t).astype(out_ref.dtype)
        for h in range(heads):
            lse_ref[h : h + 1, pl.ds(query_first, BLOCK)] = done[h][0] + jnp.log(done[h][1])
        return 0

    lax.fori_loop(0, blocks, query_step, 0)


def backward_kernel(
    place_ref, bounds_ref, proj_ref, keep_ref, mixed_ref, grad_ref, lse_ref, *refs, heads, bound_count
):
    out_ref, bias_ref, limit_ref, key_t_ref, key_acc, value_acc = refs[-6:]
    total = proj_ref.shape[0]
    blocks = total // BLOCK
    width = heads * HEAD_DIM
    load_keys(keep_ref, limit_ref, blocks)
    for j in range(blocks):
        rows = slice(j * BLOCK, (j + 1) * BLOCK)
        key_t_ref[:, rows] = jnp.transpose(proj_ref[rows, width : 2 * width].astype(f32)).astype(bf16)
    key_acc[...] = jnp.zeros_like(key_acc)
    value_acc[...] = jnp.zeros_like(value_acc)
    bias_ref[...] = jnp.zeros_like(bias_ref)

    def query_step(qi, _):
        query_first = pl.multiple_of(qi * BLOCK, BLOCK)
        query_at = pl.multiple_of(place_ref[qi], BLOCK)
        query_rows = pl.ds(query_at, BLOCK)
        places, starts = start_row(query_first, bounds_ref, bound_count)
        queries = proj_ref[query_rows, :width] * jnp.asarray(score_scale, bf16)
        grads = grad_ref[query_rows, :]
        product_t = jnp.transpose(grads.astype(f32) * mixed_ref[query_rows, :].astype(f32))
        lse = [lse_ref[h : h + 1, pl.ds(query_first, BLOCK)] for h in range(heads)]
        delta = [
            jnp.sum(product_t[h * HEAD_DIM : (h + 1) * HEAD_DIM, :], axis=0, keepdims=True) for h in range(heads)
        ]

        def key_step(kj, carry):
            key_first = pl.multiple_of(kj * BLOCK, BLOCK)
            key_rows = pl.ds(pl.multiple_of(place_ref[kj], BLOCK), BLOCK)
            bias = block_bias(limit_ref, key_first, places, starts)
            keys = proj_ref[key_rows, width : 2 * width]
            values = proj_ref[key_rows, 2 * width :]
            keys_t = key_t_ref[:, key_rows]
            out, key_parts, value_parts = [], [], []
            for h in range(heads):
                cols = slice(h * HEAD_DIM, (h + 1) * HEAD_DIM)
                scores = dot_nt(keys[:, cols], queries[:, cols]) + bias
                probs = jnp.exp(scores - lse[h])
                grad_probs = dot_nt(values[:, cols], grads[:, cols])
                grad_scores = (probs * (grad_probs - delta[h])).astype(bf16)
                value_parts.append(dot_nn(probs.astype(bf16), grads[:, cols]))
                key_parts.append(dot_nn(grad_scores, queries[:, cols]))
                out.append(carry[h] + dot_nn(keys_t[cols, :], grad_scores))
            key_acc[key_rows, :] += jnp.concatenate(key_parts, axis=1)
            value_acc[key_rows, :] += jnp.concatenate(value_parts, axis=1)
            return tuple(out)

        zero = jnp.zeros((HEAD_DIM, BLOCK), f32)
        done = lax.fori_loop(first_block(query_first, bounds_ref, bound_count), qi + 1, key_step, (zero,) * heads)
        grad_query = jnp.transpose(jnp.concatenate(done, axis=0)) * score_scale
        bias_ref[0:1, :] += jnp.sum(grad_query, axis=0, keepdims=True)
        out_ref[query_rows, :width] = grad_query.astype(bf16)
        return 0

    lax.fori_loop(0, blocks, query_step, 0)
    bias_ref[1:2, :] = jnp.sum(value_acc[...], axis=0, keepdims=True)
    out_ref[:, width : 2 * width] = key_acc[...].astype(bf16)
    out_ref[:, 2 * width :] = value_acc[...].astype(bf16)


ANY = pl.BlockSpec(memory_space=pl.ANY)
SMEM = pl.BlockSpec(memory_space=pltpu.SMEM)
VMEM = pl.BlockSpec(memory_space=pltpu.VMEM)


def attend_forward(place, bounds, proj, keep, heads, waits):
    total, width = proj.shape[0], heads * HEAD_DIM
    pairs = total * total // 6
    return pl.pallas_call(
        functools.partial(forward_kernel, heads=heads, bound_count=bounds.shape[0]),
        out_shape=(jax.ShapeDtypeStruct((total, width), bf16), jax.ShapeDtypeStruct((heads, total), f32)),
        in_specs=[SMEM, SMEM, VMEM, VMEM] + [ANY] * len(waits),
        out_specs=(VMEM, VMEM),
        scratch_shapes=[
            pltpu.VMEM((total, 128), f32),
            pltpu.VMEM((width, total), bf16),
            pltpu.VMEM((8, 128), f32),
        ],
        compiler_params=pltpu.CompilerParams(vmem_limit_bytes=40 << 20),
        cost_estimate=pl.CostEstimate(
            flops=16 * pairs * width, bytes_accessed=total * width * 8, transcendentals=pairs * heads
        ),
        name="attend_forward",
    )(place, bounds, proj, keep, *waits)


def attend_backward(place, bounds, proj, keep, mixed, grads, lse, heads, waits):
    total, width = proj.shape[0], heads * HEAD_DIM
    pairs = total * total // 6
    return pl.pallas_call(
        functools.partial(backward_kernel, heads=heads, bound_count=bounds.shape[0]),
        out_shape=(jax.ShapeDtypeStruct((total, 3 * width), bf16), jax.ShapeDtypeStruct((2, width), f32)),
        in_specs=[SMEM, SMEM, VMEM, VMEM, VMEM, VMEM, VMEM] + [ANY] * len(waits),
        out_specs=(VMEM, VMEM),
        scratch_shapes=[
            pltpu.VMEM((total, 128), f32),
            pltpu.VMEM((width, total), bf16),
            pltpu.VMEM((total, width), f32),
            pltpu.VMEM((total, width), f32),
        ],
        compiler_params=pltpu.CompilerParams(vmem_limit_bytes=50 << 20),
        cost_estimate=pl.CostEstimate(
            flops=40 * pairs * width, bytes_accessed=total * width * 20, transcendentals=pairs * heads
        ),
        name="attend_backward",
    )(place, bounds, proj, keep, mixed, grads, lse, *waits)


TN = (((0,), (0,)), ((), ()))
CHUNK = 16


def dot_tn(a, b):
    return lax.dot_general(a, b, TN, preferred_element_type=f32)


def fixed(*shape):
    return pl.BlockSpec(shape, lambda i: (0,) * len(shape))


def columns(rows, width, index):
    return pl.BlockSpec((rows, width), lambda i: (0, index))


def call(kernel, grid, inputs, outputs, name, flops, scratch=(), transcendentals=0):
    moved = sum(a.size * a.dtype.itemsize for a, spec in inputs if spec.memory_space is None)
    return pl.pallas_call(
        kernel,
        grid=(grid,),
        in_specs=[spec for _, spec in inputs],
        out_specs=tuple(spec for _, _, spec in outputs),
        out_shape=tuple(jax.ShapeDtypeStruct(shape, dtype) for shape, dtype, _ in outputs),
        scratch_shapes=list(scratch),
        compiler_params=pltpu.CompilerParams(
            vmem_limit_bytes=58 << 20, dimension_semantics=("arbitrary",)
        ),
        cost_estimate=pl.CostEstimate(flops=flops, bytes_accessed=moved, transcendentals=transcendentals),
        name=name,
    )(*[a for a, _ in inputs])


def row_sum(values):
    return jnp.sum(values, axis=-1, keepdims=True)


def fold(values):
    out = values[:8]
    for i in range(8, values.shape[0], 8):
        out = out + values[i : i + 8]
    return out


def unit_norm(values):
    center = values - jnp.mean(values, axis=-1, keepdims=True)
    inverse = lax.rsqrt(jnp.mean(center * center, axis=-1, keepdims=True) + eps)
    return center * inverse, inverse


def sub_norm(pieces, real, width):
    mean = sum(row_sum(p) for p in pieces) * (1.0 / width)
    centers = [p - mean for p in pieces]
    if real is not None:
        centers = [c * r for c, r in zip(centers, real)]
    inverse = lax.rsqrt(sum(row_sum(c * c) for c in centers) * (1.0 / width) + eps)
    return [c * inverse for c in centers], inverse


def sub_vectors(owner_ref, sub_ref, count, padded):
    rows = [sub_ref[owner_ref[p]] for p in range(count)]
    real = [r[2:3] for r in rows] if padded else None
    return [r[0:1] for r in rows], [r[1:2] for r in rows], real


def place_columns(share, width, first, rows):
    lane = lax.broadcasted_iota(jnp.int32, (128, width), 0)
    column = first + lax.broadcasted_iota(jnp.int32, (128, width), 1)
    matrix = jnp.where(lane == column % share, 1.0, 0.0).astype(bf16)
    device = lax.broadcasted_iota(jnp.int32, (rows, 1, width), 0)
    column = first + lax.broadcasted_iota(jnp.int32, (rows, 1, width), 2)
    return jnp.where(device == column // share, 1.0, 0.0), matrix


def unpack_kernel(place_ref, here_ref, *refs, share, hidden_share, line_at, halves):
    weight_ref, wide_ref, hidden_ref, bias_ref, lines_ref = refs[-5:]
    devices = lines_ref.shape[0]
    blocks = here_ref.shape[1]
    together = 2 if share % 16 else 1

    def block_of(i):
        if not halves:
            return here_ref[i].astype(f32)
        per = devices // 8
        row, own = i // per, i % per
        own_rows = here_ref[row // 2, own].astype(f32)
        other_rows = refs[0][row // 2, own].astype(f32)
        return jnp.where(place_ref[2] == row % 2, own_rows, other_rows)

    for i in range(0, devices, together):
        both = [block_of(i + j) for j in range(together)]
        for j in range(together):
            lines_ref[i + j] = both[j][line_at : line_at + 8, :256].astype(bf16).astype(f32)
        if share % 8 == 0:
            rows = jnp.concatenate([b[:share] for b in both], axis=0)
            weight_ref[i * share : (i + together) * share, :] = rows.astype(bf16)

    def spread(size, first, width):
        mine, matrix = place_columns(size, width, first, devices)
        out = []
        for part in range(2):
            lines = lines_ref[:, :, part * 128 : (part + 1) * 128].reshape(devices * 8, 128).astype(bf16)
            out.append(jnp.sum(dot_nn(lines, matrix).reshape(devices, 8, width) * mine, axis=0))
        return jnp.concatenate(out, axis=0)

    head_width = bias_ref.shape[1] // 3
    wide_ref[...] = spread(share, 0, wide_ref.shape[1])
    hidden_ref[...] = spread(hidden_share, place_ref[0], hidden_ref.shape[1])
    own = spread(share, place_ref[1], head_width)[:8]
    zero = jnp.zeros((1, head_width), f32)
    bias_ref[...] = jnp.broadcast_to(
        jnp.concatenate([own[2:3], zero, own[3:4]], axis=1), bias_ref.shape
    )


def pack_lines(values, share, first, devices):
    mine, matrix = place_columns(share, values.shape[1], first, devices)
    lines = (values[None] * mine).reshape(devices * 8, values.shape[1]).astype(bf16)
    return dot_nt(lines, matrix).reshape(devices, 8, 128)


def front_kernel(weight_ref, bias_ref, vec_ref, *refs, count):
    token_refs, (proj_ref, normed_ref) = refs[:count], refs[-2:]
    for s in range(count):
        unit, _ = unit_norm(token_refs[s][...].astype(f32))
        normed = (unit * vec_ref[0:1] + vec_ref[1:2]).astype(bf16)
        normed_ref[s] = normed
        proj_ref[s] = (dot_nn(normed, weight_ref[...]) + bias_ref[0:1]).astype(bf16)


def middle_forward_kernel(owner_ref, tokens_ref, left_ref, right_ref, sub_ref, vec_ref, *refs, count, padded):
    piece_refs, (low_ref, middle_ref, ffn_ref) = refs[:count], refs[-3:]
    head_width, width = low_ref.shape[2], middle_ref.shape[1]
    gains, offsets, real = sub_vectors(owner_ref, sub_ref, count, padded)
    units, _ = sub_norm([r[...].astype(f32) for r in piece_refs], real, width)
    middle = tokens_ref[...].astype(f32) + vec_ref[0:1]
    for p in range(count):
        low = (units[p] * gains[p] + offsets[p]).astype(bf16)
        low_ref[p] = low
        rows = pl.ds(pl.multiple_of(owner_ref[p] * head_width, head_width), head_width)
        middle = middle + dot_nn(low, jnp.concatenate([left_ref[rows, :], right_ref[rows, :]], axis=1))
    middle_ref[...] = middle
    unit, _ = unit_norm(middle)
    ffn_ref[...] = (unit * vec_ref[1:2] + vec_ref[2:3]).astype(bf16)


def middle_backward_kernel(
    owner_ref, out_grad_ref, middle_ref, left_ref, right_ref, sub_ref, vec_ref, *refs, count, addends, padded
):
    piece_refs, add_refs = refs[:count], refs[count : count + addends]
    grad_ref, grad_low_ref, *head_refs, sums_ref, sub_sums_ref = refs[count + addends :]
    head_width, width = head_refs[0].shape[1], middle_ref.shape[1]

    @pl.when(pl.program_id(0) == 0)
    def _():
        sums_ref[...] = jnp.zeros_like(sums_ref)
        sub_sums_ref[...] = jnp.zeros_like(sub_sums_ref)

    upstream = sum(r[...].astype(f32) for r in add_refs)
    unit, inverse = unit_norm(middle_ref[...])
    scaled = upstream * vec_ref[1:2]
    out_grad = out_grad_ref[...]
    grad = out_grad + inverse * (
        scaled - row_sum(scaled) * (1.0 / width) - unit * (row_sum(scaled * unit) * (1.0 / width))
    )
    grad_ref[...] = grad
    low = grad.astype(bf16)
    grad_low_ref[...] = low
    for i, terms in enumerate((grad, upstream * unit, upstream, out_grad)):
        sums_ref[i : i + 1, :] += jnp.sum(terms, axis=0, keepdims=True)
    gains, _, real = sub_vectors(owner_ref, sub_ref, count, padded)
    units, sub_inverse = sub_norm([r[...].astype(f32) for r in piece_refs], real, width)
    grads = []
    for p in range(count):
        rows = pl.ds(pl.multiple_of(owner_ref[p] * head_width, head_width), head_width)
        grads.append(dot_nt(low, jnp.concatenate([left_ref[rows, :], right_ref[rows, :]], axis=1)))
    sub_scaled = [g * gain for g, gain in zip(grads, gains)]
    mean = sum(row_sum(v) for v in sub_scaled) * (1.0 / width)
    along = sum(row_sum(v * u) for v, u in zip(sub_scaled, units)) * (1.0 / width)
    for p in range(count):
        head_refs[p][...] = ((sub_scaled[p] - mean - units[p] * along) * sub_inverse).astype(bf16)
        own = owner_ref[p]
        sub_sums_ref[own] += jnp.concatenate(
            [
                jnp.sum(grads[p] * units[p], axis=0, keepdims=True),
                jnp.sum(grads[p], axis=0, keepdims=True),
                jnp.zeros((6, head_width), f32),
            ],
            axis=0,
        )


def out_grad_kernel(owner_ref, low_ref, grad_ref, out_ref, *, count):
    head_width = low_ref.shape[2]
    for p in range(count):
        rows = pl.ds(pl.multiple_of(owner_ref[p] * head_width, head_width), head_width)
        out_ref[rows, :] = dot_tn(low_ref[p], grad_ref[...]).astype(bf16)


def lane_fold(values):
    out = values[:, :128]
    for i in range(128, values.shape[1], 128):
        out = out + values[:, i : i + 128]
    return out


def normal_parts(values):
    density = jnp.exp(-0.5 * values * values)
    t = 1.0 / (1.0 + (0.3275911 * root_half) * jnp.abs(values))
    series = 0.5 * 1.061405429
    for c in (-1.453152027, 1.421413741, -0.284496736, 0.254829592):
        series = series * t + 0.5 * c
    tail = series * t * density
    return jnp.where(values >= 0, 1.0 - tail, tail), density


def up_kernel(up_ref, down_ref, vec_ref, *refs, count, waits):
    row_refs, grad_refs = refs[:count], refs[count : 2 * count]
    act_ref, slope_ref, back_ref, stat_ref, sums_ref, pre_ref, hid_ref, part_ref = refs[2 * count + waits :]
    rows = row_refs[0].shape[0]

    @pl.when(pl.program_id(0) == 0)
    def _():
        sums_ref[...] = jnp.zeros_like(sums_ref)

    for s in range(count):
        pre_ref[s] = dot_nn(row_refs[s][...], up_ref[...])
        hid_ref[s] = dot_nn(grad_refs[s][...], down_ref[...])
    for s in range(count):
        total = jnp.zeros((8, pre_ref.shape[2]), f32)
        for c in range(rows // CHUNK):
            at = slice(c * CHUNK, (c + 1) * CHUNK)
            pre = pre_ref[s, at, :] + vec_ref[0:1]
            phi, density = normal_parts(pre)
            activated = pre * phi
            back = hid_ref[s, at, :]
            scaled = back * vec_ref[1:2]
            act_ref[s, at, :] = activated
            slope_ref[s, at, :] = (phi + pre * inv_root_tau * density).astype(bf16)
            back_ref[s, at, :] = back.astype(bf16)
            for i, terms in enumerate((activated, activated * activated, scaled, scaled * activated)):
                part_ref[s, i, at, :] = lane_fold(terms)
            total = total + fold(back)
        sums_ref[...] += total
        for i in range(4):
            stat_ref[s, i : i + 1, :] = jnp.sum(jnp.transpose(part_ref[s, i]), axis=0, keepdims=True)


def back_kernel(up_ref, vec_ref, act_ref, slope_ref, back_ref, stat_ref, *refs, count):
    hidden_ref, pre_ref, *in_refs, sums_ref, col_ref = refs[-(4 + count) :]
    rows, width = act_ref.shape[1:]

    @pl.when(pl.program_id(0) == 0)
    def _():
        sums_ref[...] = jnp.zeros_like(sums_ref)

    for s in range(count):
        stats = stat_ref[s] * (1.0 / FF)
        mean, back_mean = stats[0:1], stats[2:3]
        inverse = lax.rsqrt(stats[1:2] - mean * mean + eps)
        along = (stats[3:4] - mean * back_mean) * inverse
        for i, line in enumerate((mean, inverse, back_mean, along)):
            col_ref[s, i] = jnp.transpose(jnp.broadcast_to(line, (128, rows)))
    for s in range(count):
        first = second = jnp.zeros((8, width), f32)
        for c in range(rows // CHUNK):
            at = slice(c * CHUNK, (c + 1) * CHUNK)
            spread = [jnp.concatenate([col_ref[s, i, at, :]] * (width // 128), axis=1) for i in range(4)]
            normed = (act_ref[s, at, :] - spread[0]) * spread[1]
            back = back_ref[s, at, :].astype(f32)
            hidden_ref[s, at, :] = (normed * vec_ref[1:2] + vec_ref[2:3]).astype(bf16)
            inner = back * vec_ref[1:2] - spread[2] - normed * spread[3]
            grad = inner * (spread[1] * slope_ref[s, at, :].astype(f32))
            pre_ref[s, at, :] = grad.astype(bf16)
            first, second = first + fold(grad), second + fold(back * normed)
        sums_ref[0] += first
        sums_ref[1] += second
        in_refs[s][...] = dot_nt(pre_ref[s], up_ref[...]).astype(bf16)


def ffn_grad_kernel(down_ref, *refs, count, pairs):
    row_refs, grad_refs = refs[:count], refs[count : 2 * count]
    hidden_refs, pre_refs = refs[2 * count : 2 * count + pairs], refs[2 * count + pairs : 2 * count + 2 * pairs]
    up_out_ref, down_grad_ref, *down_out_refs, up_acc, down_acc = refs[2 * count + 2 * pairs :]
    step = pl.program_id(0)

    @pl.when(step == 0)
    def _():
        up_acc[...] = jnp.zeros_like(up_acc)
        down_acc[...] = jnp.zeros_like(down_acc)

    rows_all = jnp.concatenate([r[...] for r in row_refs], axis=0)
    grads_all = jnp.concatenate([r[...] for r in grad_refs], axis=0)
    hidden = jnp.concatenate([r[i] for r in hidden_refs for i in range(r.shape[0])], axis=0)
    pre = jnp.concatenate([r[i] for r in pre_refs for i in range(r.shape[0])], axis=0)
    up_acc[...] += dot_tn(rows_all, pre)
    down_acc[...] += dot_tn(grads_all, hidden)
    rows = row_refs[0].shape[0]
    down = dot_nt(hidden, down_ref[...]).astype(bf16)
    for i in range(count):
        down_out_refs[i][...] = down[i * rows : (i + 1) * rows]

    @pl.when(step == pl.num_programs(0) - 1)
    def _():
        up_out_ref[...] = up_acc[...].astype(bf16)
        down_grad_ref[...] = down_acc[...].astype(bf16)


def in_grad_kernel(weight_ref, *refs, count):
    proj_refs, out_refs = refs[:count], refs[-count:]
    for s in range(count):
        out_refs[s][...] = dot_nt(proj_refs[s][...], weight_ref[...]).astype(bf16)


def qkv_grad_kernel(
    place_ref, weight_ref, lines_ref, hidden_lines_ref, head_sums_ref, out_kept_ref, out_across_ref, normed_ref,
    proj_ref, *refs, count, share, hidden_share, special,
):
    token_refs = refs[:count]
    out_ref, acc_ref, unit_acc, col_acc = refs[-4:]
    step = pl.program_id(0)

    @pl.when(step == 0)
    def _():
        acc_ref[...] = jnp.zeros_like(acc_ref)
        unit_acc[...] = jnp.zeros_like(unit_acc)
        col_acc[...] = jnp.zeros_like(col_acc)

    proj = jnp.concatenate([proj_ref[s] for s in range(count)], axis=0)
    normed = jnp.concatenate([normed_ref[s] for s in range(count)], axis=0)
    unit = jnp.concatenate([unit_norm(r[...].astype(f32))[0].astype(bf16) for r in token_refs], axis=0)
    acc_ref[...] += dot_tn(normed, proj)
    unit_acc[...] += dot_tn(unit, proj)
    col_acc[...] += fold(proj.astype(f32))

    @pl.when(step == pl.num_programs(0) - 1)
    def _():
        weight = weight_ref[...].astype(f32)
        width, three = weight.shape
        rows, per, pad = out_ref.shape[0], count, out_ref.shape[1]
        devices = rows * per
        lane = lax.broadcasted_iota(jnp.int32, (width, 128), 1)
        gain = row_sum(weight * unit_acc[...])
        offset = row_sum(weight * jnp.sum(col_acc[...], axis=0, keepdims=True))
        norm_lines = jnp.transpose(jnp.where(lane == 0, gain, jnp.where(lane == 1, offset, 0.0)))[:8]
        low = pack_lines(lines_ref[0:8] + norm_lines, share, 0, devices)
        head_width = three // 3
        heads = jnp.concatenate(
            [jnp.zeros((2, head_width), f32), head_sums_ref[...], jnp.zeros((4, head_width), f32)], axis=0
        )
        low = low + pack_lines(heads, share, place_ref[1], devices)
        high = pack_lines(lines_ref[8:16], share, 0, devices)
        high = high + pack_lines(hidden_lines_ref[...], hidden_share, place_ref[0], devices)
        lines = jnp.concatenate([low, high, jnp.zeros((devices, 8, three - 256), f32)], axis=2)
        block = share_block(share)
        for i in range(devices):
            at = (i % per) * block
            rows_i = acc_ref[i * share : (i + 1) * share, :]
            tail = [jnp.zeros((block - share - 8, three), f32)] if block > share + 8 else []
            out_ref[i // per, at : at + block, :] = jnp.concatenate([rows_i, lines[i], *tail], axis=0).astype(bf16)
        if special:
            extra = out_kept_ref.shape[1] - three
            for r in range(rows):
                at = slice(r * share, (r + 1) * share)
                own = out_kept_ref[at, :] + out_across_ref[r].astype(f32)
                side = [own[j * 8 : (j + 1) * 8, three:] for j in range(three // extra)]
                out_ref[r, per * block :, :] = jnp.concatenate(
                    [own[:, :three], jnp.concatenate(side, axis=1)], axis=0
                ).astype(bf16)


def share_block(share):
    return -(-(-(-share // 8) * 8 + 8) // 16) * 16


def finish_kernel(*refs, count, share, width):
    piece_refs, (out_ref, lines_ref) = refs[:count], refs[count:]
    head_width = piece_refs[0].shape[1] // 3
    total = 0.0
    for f in range(count):
        piece = piece_refs[f][...].astype(f32)
        total = total + piece[share : share + 8]
        size = min(head_width, width - f * head_width)
        for part in range(3):
            if size > 0:
                out_ref[:, part * width + f * head_width : part * width + f * head_width + size] = piece[
                    :share, part * head_width : part * head_width + size
                ]
    lines_ref[...] = total


def body(
    row_size,
    ffn_size,
    tokens,
    seq_lengths,
    key_keep,
    pre_gain,
    pre_bias,
    qkv_weight,
    query_bias,
    value_bias,
    sub_gain,
    sub_bias,
    out_weight,
    out_bias,
    ffn_gain,
    ffn_bias,
    up_bias,
    hidden_gain,
    hidden_bias,
    down_bias,
    up_weight,
    down_weight,
    out_grad,
):
    ffn_index, row_index = lax.axis_index("ffn"), lax.axis_index("rows")
    devices = row_size * ffn_size
    row_count, width = tokens.shape
    pack_total = row_count * ffn_size
    head_count = width // HEAD_DIM
    heads = -(-head_count // ffn_size)
    head_width = heads * HEAD_DIM
    three = 3 * head_width
    padded = head_width * ffn_size
    extra = padded - width
    hidden_width = up_weight.shape[1]
    share, hidden_share = pre_gain.shape[0], up_bias.shape[0]
    share_rows = share_block(share)
    owners = [slot_owner(p, ffn_index, ffn_size) for p in range(ffn_size)]
    owner_row = jnp.stack(owners).astype(jnp.int32)
    slots = range(ffn_size)
    pairs = [(i, i + 1) for i in range(0, ffn_size, 2)]
    steps = row_count // BLOCK

    thirds = jnp.pad(qkv_weight.reshape(share, 3, width), ((0, 0), (0, 0), (0, extra)))
    pieces = thirds.reshape(share, 3, ffn_size, head_width).transpose(2, 0, 1, 3)
    pieces = pieces.reshape(ffn_size, share, three)
    lines = [
        pre_gain, pre_bias, query_bias, value_bias, sub_gain, sub_bias, out_bias, ffn_gain, ffn_bias, down_bias,
        up_bias, hidden_gain, hidden_bias,
    ]
    lines = jnp.stack([jnp.pad(v, (0, 128 - v.shape[0])) for v in lines])
    lines = jnp.concatenate([lines[:8], jnp.pad(lines[8:], ((0, 3), (0, 0)))], axis=1)
    share_eight = -(-share // 8) * 8
    lines = jnp.pad(lines, ((share_eight - share, share_rows - share_eight - 8), (0, three - 256)))
    out_flat = share * width // three
    lines = jnp.concatenate([lines, out_weight.reshape(out_flat, three)], axis=0)
    pieces = jnp.concatenate([pieces, jnp.broadcast_to(lines, (ffn_size,) + lines.shape)], axis=1)
    pieces = in_order([pieces[i] for i in slots], ffn_index, ffn_size)
    pieces = jnp.stack(in_order(exchange_slots(pieces, ffn_size), ffn_index, ffn_size))
    if ffn_size == 4:
        tokens_across = swap(after(tokens, pieces), 2)
        token_slots = [tokens, swap(tokens, 1), tokens_across, swap(tokens_across, 1)]
    else:
        token_slots = gather_slots(tokens, ffn_size)
    out_rows = pieces[:, share_rows:].reshape(ffn_size * share, width)
    half = width // 2
    left = jnp.concatenate([up_weight, out_rows[:, :half]], axis=1)
    right = jnp.concatenate([down_weight.T, out_rows[:, half:]], axis=1)
    gathered = pieces[:, :share_rows].reshape(ffn_size * share_rows, three)
    special = ffn_size == 4 and row_size == 8
    if special:
        gathered = row_step(gathered, 4, row_index)
        right = row_step(right, 1, row_index)
        left = after(left, gathered)
        gathered = row_step(gathered, 2, row_index, 1)
        left = row_step(left, 4, row_index)
        gathered = after(gathered, tokens_across).reshape(4, ffn_size, share_rows, three)
        gathered_across = swap_rows(gathered, 1)
        left = row_step(left, 2, row_index, 1, wait=gathered_across)
        right = row_step(after(right, gathered), 4, row_index, wait=gathered_across)
        early = [left, right]
        left = row_step(left, 1, row_index, 2)
        right = row_step(right, 2, row_index, 1)
        halves = [gathered_across]
    else:
        gathered, left, right = [lax.all_gather(v, "rows", axis=0, tiled=False) for v in (gathered, left, right)]
        early, halves = [], []
    left, right = left.reshape(width, -1), right.reshape(width, -1)
    if not halves:
        gathered = gathered.reshape(devices, share_rows, three)
    place_row = jnp.stack([ffn_index * hidden_width, ffn_index * head_width, row_index & 1]).astype(jnp.int32)
    qkv_own, wide, hidden_all, bias_rows = call(
        functools.partial(
            unpack_kernel, share=share, hidden_share=hidden_share, line_at=share_eight, halves=bool(halves)
        ),
        1,
        [(place_row, SMEM), *[(g, fixed(*g.shape)) for g in [gathered] + halves]],
        [
            ((width, three), bf16, fixed(width, three)),
            ((16, width), f32, fixed(16, width)),
            ((16, hidden_width), f32, fixed(16, hidden_width)),
            ((8, three), f32, fixed(8, three)),
        ],
        "unpack",
        devices * 64 * width * 16,
        [pltpu.VMEM((devices, 8, 256), f32)],
    )
    if share % 8:
        qkv_own = gathered[:, :share, :].reshape(width, three)
    hidden_vectors = jnp.pad(hidden_all[10:13], ((0, 5), (0, 0)))
    middle_vectors = jnp.pad(wide[6:9], ((0, 5), (0, 0)))
    sub_rows = jnp.pad(
        jnp.concatenate([wide[4:6], jnp.ones((1, width), f32)], axis=0), ((0, 5), (0, extra))
    )
    sub_rows = sub_rows.reshape(8, ffn_size, head_width).transpose(1, 0, 2)
    up_in = (left, columns(width, hidden_width, 0))
    down_in = (right, columns(width, hidden_width, 0))
    if extra:
        out_in = [
            (jnp.pad(v[:, hidden_width:], ((0, extra), (0, 0))), columns(padded, half, 0)) for v in (left, right)
        ]
    else:
        out_in = [(v, columns(width, half, hidden_width // half)) for v in (left, right)]

    if ffn_size == 4:
        grad_low = after(out_grad, tokens_across).astype(bf16)
        grad_across = swap(grad_low, 2)
        grad_slots = [grad_low, swap(grad_low, 1), grad_across, swap(grad_across, 1)]
        early.append(grad_across)
    else:
        grad_slots = gather_slots(out_grad.astype(bf16), ffn_size)

    block_row = pl.BlockSpec((BLOCK, width), lambda i: (i, 0))
    proj, normed_low = call(
        functools.partial(front_kernel, count=ffn_size),
        steps,
        [(qkv_own, fixed(width, three)), (bias_rows, fixed(8, three)), (wide, fixed(16, width))]
        + [(t, block_row) for t in token_slots]
        + [(e, ANY) for e in early],
        [
            ((ffn_size, row_count, three), bf16, pl.BlockSpec((ffn_size, BLOCK, three), lambda i: (0, i, 0))),
            ((ffn_size, row_count, width), bf16, pl.BlockSpec((ffn_size, BLOCK, width), lambda i: (0, i, 0))),
        ],
        "front",
        2 * pack_total * width * three,
    )
    proj, normed_low = proj.reshape(pack_total, three), normed_low.reshape(pack_total, width)

    bounds, running = [], jnp.int32(0)
    for i in range(seq_lengths.shape[1] - 1):
        running = running + seq_lengths[0, i]
        bounds.append(running)
    bounds = jnp.stack(bounds)
    firsts = jnp.arange(pack_total // BLOCK, dtype=jnp.int32) * BLOCK
    block_owner = firsts // row_count
    place = (block_owner ^ ffn_index if ffn_size == 4 else block_owner) * row_count + firsts % row_count
    keep = key_keep.reshape(pack_total // BLOCK, BLOCK)
    mixed_own, lse = attend_forward(place, bounds, proj, keep, heads, [])

    mixed_slots = exchange_slots(
        [mixed_own[p * row_count : (p + 1) * row_count] for p in slots], ffn_size
    )
    block_piece = pl.BlockSpec((BLOCK, head_width), lambda i: (i, 0))
    block_pieces = pl.BlockSpec((ffn_size, BLOCK, head_width), lambda i: (0, i, 0))
    middle_in = [*out_in, (sub_rows, fixed(ffn_size, 8, head_width)), (middle_vectors, fixed(8, width))]
    sub_low, middle, ffn_low = call(
        functools.partial(middle_forward_kernel, count=ffn_size, padded=bool(extra)),
        steps,
        [(owner_row, SMEM), (tokens, block_row), *middle_in, *[(m, block_piece) for m in mixed_slots]]
        + [(grad_slots[-1], ANY)],
        [
            ((ffn_size, row_count, head_width), bf16, block_pieces),
            ((row_count, width), f32, block_row),
            ((row_count, width), bf16, block_row),
        ],
        "middle_forward",
        2 * row_count * padded * width,
    )

    fine = BLOCK // 2
    block_fine = pl.BlockSpec((fine, width), lambda i: (i, 0))
    block_pair = pl.BlockSpec((2, fine, hidden_width), lambda i: (0, i, 0))
    block_pair_row = pl.BlockSpec((2, fine, width), lambda i: (0, i, 0))
    block_stat = pl.BlockSpec((2, 8, fine), lambda i: (0, 0, i))
    block_four = pl.BlockSpec((2, 4, fine), lambda i: (0, 0, i))
    hidden_in = (hidden_vectors, fixed(8, hidden_width))
    pair_shape = (2, row_count, hidden_width)

    def up_pair(rows, grads, waits):
        return call(
            functools.partial(up_kernel, count=2, waits=len(waits)),
            2 * steps,
            [up_in, down_in, hidden_in, *[(r, block_fine) for r in rows], *[(g, block_fine) for g in grads]]
            + [(w, ANY) for w in waits],
            [
                (pair_shape, f32, block_pair),
                (pair_shape, bf16, block_pair),
                (pair_shape, bf16, block_pair),
                ((2, 8, row_count), f32, block_stat),
                ((8, hidden_width), f32, fixed(8, hidden_width)),
            ],
            "up",
            8 * row_count * width * hidden_width,
            [
                pltpu.VMEM((2, fine, hidden_width), f32),
                pltpu.VMEM((2, fine, hidden_width), f32),
                pltpu.VMEM((2, 4, fine, 128), f32),
            ],
            4 * row_count * hidden_width,
        )

    if ffn_size == 4:
        across, beside = swap(ffn_low, 2), swap(ffn_low, 1)
        ups = [up_pair([ffn_low, beside], grad_slots[:2], [])]
        slanted = swap(after(across, ups[0][3]), 1)
        row_slots = [ffn_low, beside, across, slanted]
        ups.append(up_pair([across, slanted], grad_slots[2:], [ups[0][3]]))
    else:
        row_slots = gather_slots(ffn_low, ffn_size)
        ups = [up_pair(row_slots[i : i + 2], grad_slots[i : i + 2], []) for i, _ in pairs]
    stats = sum_slots([u[3] for u in ups], ffn_size)
    backs, wait_for = [None] * len(pairs), []
    for k in reversed(range(len(pairs))):
        act, slope, back = ups[k][:3]
        backs[k] = call(
            functools.partial(back_kernel, count=2),
            2 * steps,
            [up_in, hidden_in, (act, block_pair), (slope, block_pair), (back, block_pair)]
            + [(stats[2 * k : 2 * k + 2], block_four), *[(w, ANY) for w in wait_for]],
            [
                (pair_shape, bf16, block_pair),
                (pair_shape, bf16, block_pair),
                ((row_count, width), bf16, block_fine),
                ((row_count, width), bf16, block_fine),
                ((2, 8, hidden_width), f32, fixed(2, 8, hidden_width)),
            ],
            "back",
            4 * row_count * width * hidden_width,
            [pltpu.VMEM((2, 4, fine, 128), f32)],
        )
        wait_for = [backs[k][3]]

    def reduce_pairs(near, far, wait=None):
        passed = swap(far[1], 1)
        sent = far[0].astype(f32) + passed.astype(f32)
        sent = (sent if wait is None else after(sent, wait)).astype(bf16)
        return [near[0], swap(near[1], 1), swap(sent, 2)], sent

    def scatter_pairs(parts):
        return [lax.psum_scatter(jnp.stack(parts), "ffn", scatter_dimension=0, tiled=True)[0]]

    if ffn_size == 4:
        in_terms, _ = reduce_pairs(backs[0][2:4], backs[1][2:4])
    else:
        in_terms = scatter_pairs([v for b in backs for v in b[2:4]])
    block_quarter = pl.BlockSpec((BLOCK // 2, width), lambda i: (i, 0))
    block_pair_quarter = pl.BlockSpec((2, BLOCK // 2, hidden_width), lambda i: (0, i, 0))
    up_part, down_part, *down_parts = call(
        functools.partial(ffn_grad_kernel, count=ffn_size, pairs=len(pairs)),
        2 * steps,
        [down_in, *[(r, block_quarter) for r in row_slots], *[(g, block_quarter) for g in grad_slots]]
        + [(b[0], block_pair_quarter) for b in backs]
        + [(b[1], block_pair_quarter) for b in backs],
        [
            ((width, hidden_width), bf16, fixed(width, hidden_width)),
            ((width, hidden_width), bf16, fixed(width, hidden_width)),
        ]
        + [((row_count, width), bf16, block_quarter)] * ffn_size,
        "ffn_grads",
        6 * pack_total * width * hidden_width,
        [pltpu.VMEM((width, hidden_width), f32), pltpu.VMEM((width, hidden_width), f32)],
    )
    if special:
        bulk = (2, 2, 2, width // row_size, hidden_width)
        up_shares, down_shares = up_part.reshape(bulk), down_part.reshape(bulk)
    else:
        ties = []
        up_weight_grad, down_weight_grad = [
            lax.psum_scatter(v, "rows", scatter_dimension=0, tiled=True).astype(f32) for v in (up_part, down_part)
        ]

    grad_middle, middle_low, *head_low, middle_sums, sub_sums = call(
        functools.partial(
            middle_backward_kernel, count=ffn_size, addends=len(in_terms), padded=bool(extra)
        ),
        steps,
        [(owner_row, SMEM), (out_grad, block_row), (middle, block_row), *middle_in]
        + [(m, block_piece) for m in mixed_slots]
        + [(t, block_row) for t in in_terms],
        [
            ((row_count, width), f32, block_row),
            ((row_count, width), bf16, block_row),
            *[((row_count, head_width), bf16, block_piece)] * ffn_size,
            ((8, width), f32, fixed(8, width)),
            ((ffn_size, 8, head_width), f32, fixed(ffn_size, 8, head_width)),
        ],
        "middle_backward",
        2 * row_count * padded * width,
    )
    grad_own = jnp.concatenate(exchange_slots(head_low, ffn_size), axis=0)
    (out_part,) = call(
        functools.partial(out_grad_kernel, count=ffn_size),
        1,
        [(owner_row, SMEM), (sub_low, fixed(ffn_size, row_count, head_width)), (middle_low, fixed(row_count, width))],
        [((padded, width), bf16, fixed(padded, width))],
        "out_grads",
        2 * row_count * padded * width,
    )
    if special:
        up_two, _ = split_add(up_shares, 1, row_index, middle_low)
        down_two, _ = split_add(down_shares, 2, row_index, middle_low)
        up_sent, up_kept = row_split(up_two, 2, row_index)
        down_sent, down_kept = row_split(down_two, 4, row_index)
        ties = [up_sent, down_sent]
        shares = out_part.reshape(row_size, ffn_size, share, width).transpose(1, 0, 2, 3)
        shares = in_order([shares[i].astype(f32) for i in slots], ffn_index, ffn_size)
        passed = swap(jnp.stack([shares[1], shares[3]]).astype(bf16), 1).astype(f32)
        out_sent = after(shares[2] + passed[1], grad_own).astype(bf16)
        out_across = swap(out_sent, 2)
        out_kept = (shares[0] + passed[0]).reshape(row_size * share, width)
        ties += [out_sent, out_kept]
    else:
        out_kept = out_across = jnp.zeros((8, 8, width), f32)
        out_weight_own = lax.psum_scatter(
            out_part[:width], ("rows", "ffn"), scatter_dimension=0, tiled=True
        ).astype(f32)

    if ffn_size == 4:
        down_terms, layer_sent = reduce_pairs(down_parts[:2], down_parts[2:], grad_own)
        ties.append(layer_sent)
    else:
        down_terms = scatter_pairs(down_parts)
    layer_out = (middle + sum(t.astype(f32) for t in down_terms) + wide[9]).astype(bf16)

    sub_flat = sub_sums[:, :2].transpose(1, 0, 2).reshape(2, padded)[:, :width]
    lines = jnp.concatenate(
        [jnp.zeros((4, width), f32), sub_flat, middle_sums[:4], jnp.zeros((6, width), f32)], axis=0
    )
    back_sums = jnp.sum(sum(b[4] for b in backs), axis=1)
    hidden_lines = jnp.concatenate(
        [
            jnp.zeros((2, hidden_width), f32),
            back_sums,
            jnp.sum(sum(u[4] for u in ups), axis=0)[None],
            jnp.zeros((3, hidden_width), f32),
        ],
        axis=0,
    )
    ties += [lines, hidden_lines]

    grad_proj, head_bias_grads = attend_backward(place, bounds, proj, keep, mixed_own, grad_own, lse, heads, ties)

    def in_pair(k, waits):
        proj_specs = [
            pl.BlockSpec((BLOCK, three), lambda i, p=p: (p * steps + i, 0)) for p in pairs[k]
        ]
        return call(
            functools.partial(in_grad_kernel, count=2),
            steps,
            [(qkv_own, fixed(width, three)), *[(grad_proj, spec) for spec in proj_specs]]
            + [(w, ANY) for w in waits],
            [((row_count, width), bf16, block_row)] * 2,
            "in_grads",
            4 * row_count * width * three,
        )

    if special:
        up_one = up_kept + after(swap_rows(up_sent, 2), grad_proj).astype(f32)
        down_one = down_kept + after(swap_rows(down_sent, 4), grad_proj).astype(f32)
        up_sent, up_kept = row_split(up_one, 4, row_index)
        down_sent, down_kept = row_split(down_one, 1, row_index)
        late = [up_sent, down_sent]
    else:
        late = []
    taken = ffn_size * share_rows
    packed_rows = taken + (out_flat if special else 0)
    eighth = row_count // 4
    (packed,) = call(
        functools.partial(
            qkv_grad_kernel, count=ffn_size, share=share, hidden_share=hidden_share, special=special
        ),
        4,
        [
            (place_row, SMEM),
            (qkv_own, fixed(width, three)),
            (lines, fixed(16, width)),
            (hidden_lines, fixed(8, hidden_width)),
            (head_bias_grads, fixed(2, head_width)),
            (out_kept, fixed(*out_kept.shape)),
            (out_across, fixed(*out_across.shape)),
            (
                normed_low.reshape(ffn_size, row_count, width),
                pl.BlockSpec((ffn_size, eighth, width), lambda i: (0, i, 0)),
            ),
            (
                grad_proj.reshape(ffn_size, row_count, three),
                pl.BlockSpec((ffn_size, eighth, three), lambda i: (0, i, 0)),
            ),
            *[(t, pl.BlockSpec((eighth, width), lambda i: (i, 0))) for t in token_slots],
            *[(v, ANY) for v in late],
        ],
        [((row_size, packed_rows, three), bf16, fixed(row_size, packed_rows, three))],
        "qkv_grads",
        4 * pack_total * width * three,
        [pltpu.VMEM((width, three), f32), pltpu.VMEM((width, three), f32), pltpu.VMEM((8, three), f32)],
    )
    if special:
        far = in_pair(1, [packed, down_terms[2]])
        passed = swap(far[1], 1)
        sent = (far[0].astype(f32) + passed.astype(f32)).astype(bf16)
        across = swap(sent, 2)
        near = in_pair(0, [sent])
        in_terms = [near[0], swap(near[1], 1), across]
        packed, _ = row_halves(
            packed.reshape(2, 2, 2, packed_rows, three), (1, 2, 4), row_index, (near[0], None, None)
        )
        up_weight_grad = up_kept + after(swap_rows(up_sent, 4), near[0]).astype(f32)
        down_weight_grad = down_kept + after(swap_rows(down_sent, 1), near[0]).astype(f32)
        tail_rows = packed[taken:]
        side = tail_rows[share:]
        side = jnp.concatenate([side[:, j : j + width - three] for j in range(0, three, width - three)], axis=0)
        out_weight_own = jnp.concatenate([tail_rows[:share], side], axis=1)
    else:
        in_terms = scatter_pairs([v for k in range(len(pairs)) for v in in_pair(k, [])])
        packed = lax.psum_scatter(packed, "rows", scatter_dimension=0, tiled=True)[0]
    packed = packed[:taken].astype(bf16).reshape(ffn_size, share_rows, three)
    packed = in_order([packed[i] for i in slots], ffn_index, ffn_size)
    packed = in_order(exchange_slots(packed, ffn_size), ffn_index, ffn_size)
    qkv_weight_grad, line_own = call(
        functools.partial(finish_kernel, count=ffn_size, share=share, width=width),
        1,
        [(p, fixed(share_rows, three)) for p in packed],
        [((share, 3 * width), f32, fixed(share, 3 * width)), ((8, three), f32, fixed(8, three))],
        "finish",
        share * three * ffn_size,
    )

    up_weight_grad = up_weight_grad.reshape(-1, hidden_width)
    down_weight_grad = down_weight_grad.reshape(-1, hidden_width).T

    unit_own, inverse_own = unit_norm(tokens.astype(f32))
    in_scaled = sum(t.astype(f32) for t in in_terms) * wide[0]
    in_adjusted = (
        in_scaled
        - jnp.mean(in_scaled, axis=-1, keepdims=True)
        - unit_own * jnp.mean(in_scaled * unit_own, axis=-1, keepdims=True)
    )
    tokens_grad = grad_middle + in_adjusted * inverse_own

    vectors = [line_own[i, :share] for i in range(8)] + [line_own[i, 128 : 128 + share] for i in range(2)]
    small = vectors
    hidden_small = [line_own[i, 128 : 128 + hidden_share] for i in range(2, 5)]
    return (
        layer_out,
        tokens_grad,
        small[0],
        small[1],
        qkv_weight_grad,
        small[2],
        small[3],
        small[4],
        small[5],
        out_weight_own,
        small[6],
        small[7],
        small[8],
        hidden_small[0],
        hidden_small[1],
        hidden_small[2],
        small[9],
        up_weight_grad,
        down_weight_grad,
    )


def solution(mesh):
    flat, matrix = P(("rows", "ffn")), P(("rows", "ffn"), None)
    in_specs = (
        matrix, P("rows", None), P("rows"), flat, flat, matrix, flat, flat, flat, flat, matrix, flat, flat, flat,
        flat, flat, flat, flat, P("rows", "ffn"), P("ffn", "rows"), matrix,
    )
    out_specs = (
        matrix, matrix, flat, flat, matrix, flat, flat, flat, flat, matrix, flat, flat, flat, flat, flat, flat, flat,
        P("rows", "ffn"), P("ffn", "rows"),
    )
    return jax.shard_map(
        functools.partial(body, mesh.shape["rows"], mesh.shape["ffn"]),
        mesh=mesh,
        in_specs=in_specs,
        out_specs=out_specs,
        check_vma=False,
    )
```

```python
import functools

import jax
import jax.numpy as jnp
from jax import lax
from jax.experimental import pallas as pl
from jax.experimental.pallas import tpu as pltpu
from jax.sharding import PartitionSpec as P

HEAD_DIM = 64
FF = 3072
BLOCK = 256
SMALL = 20

eps = 1e-05
neg_big = -1e30
score_scale = 0.125
root_half = 0.7071067811865476
inv_root_tau = 0.3989422804014327

f32 = jnp.float32
bf16 = jnp.bfloat16


def swap(values, flip):
    return lax.ppermute(values, "ffn", [(i, i ^ flip) for i in range(4)])


def swap_rows(values, flip):
    return lax.ppermute(values, "rows", [(i, i ^ flip) for i in range(8)])


def slot_owner(slot, ffn_index, ffn_size):
    return ffn_index ^ slot if ffn_size == 4 else jnp.int32(slot)


def gather_slots(values, ffn_size):
    if ffn_size != 4:
        whole = lax.all_gather(values, "ffn", axis=0, tiled=False)
        return [whole[i] for i in range(ffn_size)]
    across = swap(values, 2)
    beside = swap(values, 1)
    return [values, beside, across, swap(across, 1)]


def exchange_slots(pieces, ffn_size):
    if ffn_size != 4:
        whole = lax.all_to_all(jnp.stack(pieces), "ffn", split_axis=0, concat_axis=0, tiled=True)
        return [whole[i] for i in range(ffn_size)]
    across = swap(pieces[2], 2)
    slanted = swap(pieces[3], 3)
    beside = swap(pieces[1], 1)
    return [pieces[0], beside, across, slanted]


def in_order(slots, ffn_index, ffn_size):
    if ffn_size != 4:
        return slots
    odd, high = (ffn_index & 1) > 0, (ffn_index & 2) > 0
    low = [jnp.where(odd, slots[p ^ 1], slots[p]) for p in range(4)]
    return [jnp.where(high, low[p ^ 2], low[p]) for p in range(4)]


def sum_slots(pairs, ffn_size):
    values = jnp.concatenate(pairs, axis=0)[:, :4, :]
    if ffn_size != 4:
        return lax.psum(values, "ffn")
    beside = swap(values, 1)
    values = values + jnp.stack([beside[1], beside[0], beside[3], beside[2]])
    across = swap(values, 2)
    return values + jnp.stack([across[2], across[3], across[0], across[1]])


ROW_AXIS = {4: 0, 2: 1, 1: 2}


def row_bit(flip, row_index):
    return (row_index >> (2 - ROW_AXIS[flip])) & 1


def row_step(whole, flip, row_index, outer=0, wait=None):
    bit = row_bit(flip, row_index)
    other = swap_rows(whole, flip)
    if wait is not None:
        other = after(other, wait)
    return jnp.stack([jnp.where(bit > 0, other, whole), jnp.where(bit > 0, whole, other)], axis=outer)


def row_split(whole, flip, row_index):
    axis, bit = ROW_AXIS[flip], row_bit(flip, row_index)
    sent = lax.dynamic_slice_in_dim(whole, 1 - bit, 1, axis).astype(bf16)
    return sent, lax.dynamic_slice_in_dim(whole, bit, 1, axis).astype(f32)


def split_add(whole, flip, row_index, wait):
    sent, kept = row_split(whole, flip, row_index)
    sent = after(sent, wait)
    return kept + swap_rows(sent, flip).astype(f32), sent


def row_halves(whole, flips, row_index, waits):
    sends = []
    for flip, wait in zip(flips, waits):
        sent, kept = row_split(whole, flip, row_index)
        sends.append(sent)
        other = swap_rows(sent, flip)
        whole = kept + (other if wait is None else after(other, wait)).astype(f32)
    return whole[0, 0, 0], sends


def after(values, other):
    first = lax.slice(other, (0,) * other.ndim, (1,) * other.ndim).reshape(())
    return values + (first * 0).astype(values.dtype)


NT = (((1,), (1,)), ((), ()))


def dot_nt(a, b):
    return lax.dot_general(a, b, NT, preferred_element_type=f32)


def dot_nn(a, b):
    return jnp.dot(a, b, preferred_element_type=f32)


def start_row(first, bounds_ref, bound_count):
    places = first + lax.broadcasted_iota(jnp.int32, (1, BLOCK), 1)
    start = jnp.zeros((1, BLOCK), jnp.int32)
    for i in range(bound_count):
        bound = bounds_ref[i]
        start = jnp.where(places >= bound, jnp.maximum(start, bound), start)
    return places, start


def first_block(first, bounds_ref, bound_count):
    start = jnp.int32(0)
    for i in range(bound_count):
        bound = bounds_ref[i]
        start = jnp.where(first >= bound, jnp.maximum(start, bound), start)
    return start // BLOCK


def load_keys(keep_ref, limit_ref, blocks):
    for j in range(blocks):
        row = keep_ref[j : j + 1, :]
        places = j * BLOCK + lax.broadcasted_iota(jnp.int32, (1, BLOCK), 1)
        limits = jnp.where(row > 0, places, 1 << 24).astype(f32)
        column = jnp.transpose(jnp.broadcast_to(limits, (128, BLOCK)))
        limit_ref[j * BLOCK : (j + 1) * BLOCK, :] = column


def block_bias(limit_ref, key_first, query_places, query_start):
    limit = limit_ref[pl.ds(key_first, BLOCK), :]
    limit = jnp.concatenate([limit] * (BLOCK // 128), axis=1)
    key_places = key_first + lax.broadcasted_iota(jnp.int32, (BLOCK, BLOCK), 0)
    before = (limit < query_places.astype(f32)) & (key_places >= query_start)
    return jnp.where(before | (key_places == query_places), 0.0, neg_big)


def forward_kernel(
    place_ref, bounds_ref, proj_ref, keep_ref, *refs, heads, bound_count
):
    out_ref, lse_ref, limit_ref, value_t_ref = refs[-4:]
    total = proj_ref.shape[0]
    blocks = total // BLOCK
    width = heads * HEAD_DIM
    load_keys(keep_ref, limit_ref, blocks)
    for j in range(blocks):
        rows = slice(j * BLOCK, (j + 1) * BLOCK)
        value_t_ref[:, rows] = jnp.transpose(proj_ref[rows, 2 * width :].astype(f32)).astype(bf16)

    def query_step(qi, _):
        query_first = pl.multiple_of(qi * BLOCK, BLOCK)
        query_at = pl.multiple_of(place_ref[qi], BLOCK)
        places, starts = start_row(query_first, bounds_ref, bound_count)
        queries = proj_ref[pl.ds(query_at, BLOCK), :width] * jnp.asarray(score_scale, bf16)

        def key_step(kj, carry):
            key_first = pl.multiple_of(kj * BLOCK, BLOCK)
            key_at = pl.multiple_of(place_ref[kj], BLOCK)
            bias = block_bias(limit_ref, key_first, places, starts)
            keys = proj_ref[pl.ds(key_at, BLOCK), width : 2 * width]
            values_t = value_t_ref[:, pl.ds(key_at, BLOCK)]
            out = []
            for h in range(heads):
                cols = slice(h * HEAD_DIM, (h + 1) * HEAD_DIM)
                top, total_sum, mixed = carry[h]
                scores = dot_nt(keys[:, cols], queries[:, cols]) + bias
                new_top = jnp.maximum(top, jnp.max(scores, axis=0, keepdims=True))
                weights = jnp.exp(scores - new_top)
                decay = jnp.exp(top - new_top)
                new_sum = total_sum * decay + jnp.sum(weights, axis=0, keepdims=True)
                new_mixed = mixed * decay + dot_nn(values_t[cols, :], weights.astype(bf16))
                out.append((new_top, new_sum, new_mixed))
            return tuple(out)

        empty = (
            jnp.full((1, BLOCK), neg_big, f32),
            jnp.zeros((1, BLOCK), f32),
            jnp.zeros((HEAD_DIM, BLOCK), f32),
        )
        done = lax.fori_loop(first_block(query_first, bounds_ref, bound_count), qi + 1, key_step, (empty,) * heads)
        mixed_t = jnp.concatenate([mixed / total_sum for _, total_sum, mixed in done], axis=0)
        out_ref[pl.ds(query_at, BLOCK), :] = jnp.transpose(mixed_t).astype(out_ref.dtype)
        for h in range(heads):
            lse_ref[h : h + 1, pl.ds(query_first, BLOCK)] = done[h][0] + jnp.log(done[h][1])
        return 0

    lax.fori_loop(0, blocks, query_step, 0)


def backward_kernel(
    place_ref, bounds_ref, proj_ref, keep_ref, mixed_ref, grad_ref, lse_ref, *refs, heads, bound_count
):
    out_ref, bias_ref, limit_ref, key_t_ref, key_acc, value_acc = refs[-6:]
    total = proj_ref.shape[0]
    blocks = total // BLOCK
    width = heads * HEAD_DIM
    load_keys(keep_ref, limit_ref, blocks)
    for j in range(blocks):
        rows = slice(j * BLOCK, (j + 1) * BLOCK)
        key_t_ref[:, rows] = jnp.transpose(proj_ref[rows, width : 2 * width].astype(f32)).astype(bf16)
    key_acc[...] = jnp.zeros_like(key_acc)
    value_acc[...] = jnp.zeros_like(value_acc)
    bias_ref[...] = jnp.zeros_like(bias_ref)

    def query_step(qi, _):
        query_first = pl.multiple_of(qi * BLOCK, BLOCK)
        query_at = pl.multiple_of(place_ref[qi], BLOCK)
        query_rows = pl.ds(query_at, BLOCK)
        places, starts = start_row(query_first, bounds_ref, bound_count)
        queries = proj_ref[query_rows, :width] * jnp.asarray(score_scale, bf16)
        grads = grad_ref[query_rows, :]
        product_t = jnp.transpose(grads.astype(f32) * mixed_ref[query_rows, :].astype(f32))
        lse = [lse_ref[h : h + 1, pl.ds(query_first, BLOCK)] for h in range(heads)]
        delta = [
            jnp.sum(product_t[h * HEAD_DIM : (h + 1) * HEAD_DIM, :], axis=0, keepdims=True) for h in range(heads)
        ]

        def key_step(kj, carry):
            key_first = pl.multiple_of(kj * BLOCK, BLOCK)
            key_rows = pl.ds(pl.multiple_of(place_ref[kj], BLOCK), BLOCK)
            bias = block_bias(limit_ref, key_first, places, starts)
            keys = proj_ref[key_rows, width : 2 * width]
            values = proj_ref[key_rows, 2 * width :]
            keys_t = key_t_ref[:, key_rows]
            out, key_parts, value_parts = [], [], []
            for h in range(heads):
                cols = slice(h * HEAD_DIM, (h + 1) * HEAD_DIM)
                scores = dot_nt(keys[:, cols], queries[:, cols]) + bias
                probs = jnp.exp(scores - lse[h])
                grad_probs = dot_nt(values[:, cols], grads[:, cols])
                grad_scores = (probs * (grad_probs - delta[h])).astype(bf16)
                value_parts.append(dot_nn(probs.astype(bf16), grads[:, cols]))
                key_parts.append(dot_nn(grad_scores, queries[:, cols]))
                out.append(carry[h] + dot_nn(keys_t[cols, :], grad_scores))
            key_acc[key_rows, :] += jnp.concatenate(key_parts, axis=1)
            value_acc[key_rows, :] += jnp.concatenate(value_parts, axis=1)
            return tuple(out)

        zero = jnp.zeros((HEAD_DIM, BLOCK), f32)
        done = lax.fori_loop(first_block(query_first, bounds_ref, bound_count), qi + 1, key_step, (zero,) * heads)
        grad_query = jnp.transpose(jnp.concatenate(done, axis=0)) * score_scale
        bias_ref[0:1, :] += jnp.sum(grad_query, axis=0, keepdims=True)
        out_ref[query_rows, :width] = grad_query.astype(bf16)
        return 0

    lax.fori_loop(0, blocks, query_step, 0)
    bias_ref[1:2, :] = jnp.sum(value_acc[...], axis=0, keepdims=True)
    out_ref[:, width : 2 * width] = key_acc[...].astype(bf16)
    out_ref[:, 2 * width :] = value_acc[...].astype(bf16)


ANY = pl.BlockSpec(memory_space=pl.ANY)
SMEM = pl.BlockSpec(memory_space=pltpu.SMEM)
VMEM = pl.BlockSpec(memory_space=pltpu.VMEM)


def attend_forward(place, bounds, proj, keep, heads, waits):
    total, width = proj.shape[0], heads * HEAD_DIM
    pairs = total * total // 6
    return pl.pallas_call(
        functools.partial(forward_kernel, heads=heads, bound_count=bounds.shape[0]),
        out_shape=(jax.ShapeDtypeStruct((total, width), bf16), jax.ShapeDtypeStruct((heads, total), f32)),
        in_specs=[SMEM, SMEM, VMEM, VMEM] + [ANY] * len(waits),
        out_specs=(VMEM, VMEM),
        scratch_shapes=[
            pltpu.VMEM((total, 128), f32),
            pltpu.VMEM((width, total), bf16),
        ],
        compiler_params=pltpu.CompilerParams(vmem_limit_bytes=40 << 20),
        cost_estimate=pl.CostEstimate(
            flops=16 * pairs * width // SMALL, bytes_accessed=1024, transcendentals=0
        ),
        name="attend_forward",
    )(place, bounds, proj, keep, *waits)


def attend_backward(place, bounds, proj, keep, mixed, grads, lse, heads, waits):
    total, width = proj.shape[0], heads * HEAD_DIM
    pairs = total * total // 6
    return pl.pallas_call(
        functools.partial(backward_kernel, heads=heads, bound_count=bounds.shape[0]),
        out_shape=(jax.ShapeDtypeStruct((total, 3 * width), bf16), jax.ShapeDtypeStruct((2, width), f32)),
        in_specs=[SMEM, SMEM, VMEM, VMEM, VMEM, VMEM, VMEM] + [ANY] * len(waits),
        out_specs=(VMEM, VMEM),
        scratch_shapes=[
            pltpu.VMEM((total, 128), f32),
            pltpu.VMEM((width, total), bf16),
            pltpu.VMEM((total, width), f32),
            pltpu.VMEM((total, width), f32),
        ],
        compiler_params=pltpu.CompilerParams(vmem_limit_bytes=50 << 20),
        cost_estimate=pl.CostEstimate(
            flops=40 * pairs * width // SMALL, bytes_accessed=1024, transcendentals=0
        ),
        name="attend_backward",
    )(place, bounds, proj, keep, mixed, grads, lse, *waits)


TN = (((0,), (0,)), ((), ()))
CHUNK = 16


def dot_tn(a, b):
    return lax.dot_general(a, b, TN, preferred_element_type=f32)


def fixed(*shape):
    return pl.BlockSpec(shape, lambda i: (0,) * len(shape))


def columns(rows, width, index):
    return pl.BlockSpec((rows, width), lambda i: (0, index))


def call(kernel, grid, inputs, outputs, name, flops, scratch=(), transcendentals=0):
    moved = sum(a.size * a.dtype.itemsize for a, spec in inputs if spec.memory_space is None)
    return pl.pallas_call(
        kernel,
        grid=(grid,),
        in_specs=[spec for _, spec in inputs],
        out_specs=tuple(spec for _, _, spec in outputs),
        out_shape=tuple(jax.ShapeDtypeStruct(shape, dtype) for shape, dtype, _ in outputs),
        scratch_shapes=list(scratch),
        compiler_params=pltpu.CompilerParams(
            vmem_limit_bytes=58 << 20, dimension_semantics=("arbitrary",)
        ),
        cost_estimate=pl.CostEstimate(
            flops=flops // SMALL, bytes_accessed=moved // SMALL, transcendentals=transcendentals // SMALL
        ),
        name=name,
    )(*[a for a, _ in inputs])


def row_sum(values):
    return jnp.sum(values, axis=-1, keepdims=True)


def fold(values):
    out = values[:8]
    for i in range(8, values.shape[0], 8):
        out = out + values[i : i + 8]
    return out


def unit_norm(values):
    center = values - jnp.mean(values, axis=-1, keepdims=True)
    inverse = lax.rsqrt(jnp.mean(center * center, axis=-1, keepdims=True) + eps)
    return center * inverse, inverse


def sub_norm(pieces, real, width):
    mean = sum(row_sum(p) for p in pieces) * (1.0 / width)
    centers = [p - mean for p in pieces]
    if real is not None:
        centers = [c * r for c, r in zip(centers, real)]
    inverse = lax.rsqrt(sum(row_sum(c * c) for c in centers) * (1.0 / width) + eps)
    return [c * inverse for c in centers], inverse


def sub_vectors(owner_ref, sub_ref, count, padded):
    rows = [sub_ref[owner_ref[p]] for p in range(count)]
    real = [r[2:3] for r in rows] if padded else None
    return [r[0:1] for r in rows], [r[1:2] for r in rows], real


def place_columns(share, width, first, rows):
    lane = lax.broadcasted_iota(jnp.int32, (128, width), 0)
    column = first + lax.broadcasted_iota(jnp.int32, (128, width), 1)
    matrix = jnp.where(lane == column % share, 1.0, 0.0).astype(bf16)
    device = lax.broadcasted_iota(jnp.int32, (rows, 1, width), 0)
    column = first + lax.broadcasted_iota(jnp.int32, (rows, 1, width), 2)
    return jnp.where(device == column // share, 1.0, 0.0), matrix


def unpack_kernel(place_ref, here_ref, *refs, share, hidden_share, line_at, halves):
    weight_ref, wide_ref, hidden_ref, bias_ref, lines_ref = refs[-5:]
    devices = lines_ref.shape[0]
    blocks = here_ref.shape[1]
    together = 2 if share % 16 else 1

    def block_of(i):
        if not halves:
            return here_ref[i].astype(f32)
        per = devices // 8
        row, own = i // per, i % per
        own_rows = here_ref[row // 2, own].astype(f32)
        other_rows = refs[0][row // 2, own].astype(f32)
        return jnp.where(place_ref[2] == row % 2, own_rows, other_rows)

    for i in range(0, devices, together):
        both = [block_of(i + j) for j in range(together)]
        for j in range(together):
            lines_ref[i + j] = both[j][line_at : line_at + 8, :256].astype(bf16).astype(f32)
        if share % 8 == 0:
            rows = jnp.concatenate([b[:share] for b in both], axis=0)
            weight_ref[i * share : (i + together) * share, :] = rows.astype(bf16)

    def spread(size, first, width):
        mine, matrix = place_columns(size, width, first, devices)
        out = []
        for part in range(2):
            lines = lines_ref[:, :, part * 128 : (part + 1) * 128].reshape(devices * 8, 128).astype(bf16)
            out.append(jnp.sum(dot_nn(lines, matrix).reshape(devices, 8, width) * mine, axis=0))
        return jnp.concatenate(out, axis=0)

    head_width = bias_ref.shape[1] // 3
    wide_ref[...] = spread(share, 0, wide_ref.shape[1])
    hidden_ref[...] = spread(hidden_share, place_ref[0], hidden_ref.shape[1])
    own = spread(share, place_ref[1], head_width)[:8]
    zero = jnp.zeros((1, head_width), f32)
    bias_ref[...] = jnp.broadcast_to(
        jnp.concatenate([own[2:3], zero, own[3:4]], axis=1), bias_ref.shape
    )


def pack_lines(values, share, first, devices):
    mine, matrix = place_columns(share, values.shape[1], first, devices)
    lines = (values[None] * mine).reshape(devices * 8, values.shape[1]).astype(bf16)
    return dot_nt(lines, matrix).reshape(devices, 8, 128)


def front_kernel(weight_ref, bias_ref, vec_ref, *refs, count):
    token_refs, (proj_ref, normed_ref) = refs[:count], refs[-2:]
    for s in range(count):
        unit, _ = unit_norm(token_refs[s][...].astype(f32))
        normed = (unit * vec_ref[0:1] + vec_ref[1:2]).astype(bf16)
        normed_ref[s] = normed
        proj_ref[s] = (dot_nn(normed, weight_ref[...]) + bias_ref[0:1]).astype(bf16)


def middle_forward_kernel(owner_ref, tokens_ref, left_ref, right_ref, sub_ref, vec_ref, *refs, count, padded):
    piece_refs, (low_ref, middle_ref, ffn_ref) = refs[:count], refs[-3:]
    head_width, width = low_ref.shape[2], middle_ref.shape[1]
    gains, offsets, real = sub_vectors(owner_ref, sub_ref, count, padded)
    units, _ = sub_norm([r[...].astype(f32) for r in piece_refs], real, width)
    middle = tokens_ref[...].astype(f32) + vec_ref[0:1]
    for p in range(count):
        low = (units[p] * gains[p] + offsets[p]).astype(bf16)
        low_ref[p] = low
        rows = pl.ds(pl.multiple_of(owner_ref[p] * head_width, head_width), head_width)
        middle = middle + dot_nn(low, jnp.concatenate([left_ref[rows, :], right_ref[rows, :]], axis=1))
    middle_ref[...] = middle
    unit, _ = unit_norm(middle)
    ffn_ref[...] = (unit * vec_ref[1:2] + vec_ref[2:3]).astype(bf16)


def middle_backward_kernel(
    owner_ref, out_grad_ref, middle_ref, left_ref, right_ref, sub_ref, vec_ref, *refs, count, addends, padded
):
    piece_refs, add_refs = refs[:count], refs[count : count + addends]
    grad_ref, grad_low_ref, *head_refs, sums_ref, sub_sums_ref = refs[count + addends :]
    head_width, width = head_refs[0].shape[1], middle_ref.shape[1]

    @pl.when(pl.program_id(0) == 0)
    def _():
        sums_ref[...] = jnp.zeros_like(sums_ref)
        sub_sums_ref[...] = jnp.zeros_like(sub_sums_ref)

    upstream = sum(r[...].astype(f32) for r in add_refs)
    unit, inverse = unit_norm(middle_ref[...])
    scaled = upstream * vec_ref[1:2]
    out_grad = out_grad_ref[...]
    grad = out_grad + inverse * (
        scaled - row_sum(scaled) * (1.0 / width) - unit * (row_sum(scaled * unit) * (1.0 / width))
    )
    grad_ref[...] = grad
    low = grad.astype(bf16)
    grad_low_ref[...] = low
    for i, terms in enumerate((grad, upstream * unit, upstream, out_grad)):
        sums_ref[i : i + 1, :] += jnp.sum(terms, axis=0, keepdims=True)
    gains, _, real = sub_vectors(owner_ref, sub_ref, count, padded)
    units, sub_inverse = sub_norm([r[...].astype(f32) for r in piece_refs], real, width)
    grads = []
    for p in range(count):
        rows = pl.ds(pl.multiple_of(owner_ref[p] * head_width, head_width), head_width)
        grads.append(dot_nt(low, jnp.concatenate([left_ref[rows, :], right_ref[rows, :]], axis=1)))
    sub_scaled = [g * gain for g, gain in zip(grads, gains)]
    mean = sum(row_sum(v) for v in sub_scaled) * (1.0 / width)
    along = sum(row_sum(v * u) for v, u in zip(sub_scaled, units)) * (1.0 / width)
    for p in range(count):
        head_refs[p][...] = ((sub_scaled[p] - mean - units[p] * along) * sub_inverse).astype(bf16)
        own = owner_ref[p]
        sub_sums_ref[own] += jnp.concatenate(
            [
                jnp.sum(grads[p] * units[p], axis=0, keepdims=True),
                jnp.sum(grads[p], axis=0, keepdims=True),
                jnp.zeros((6, head_width), f32),
            ],
            axis=0,
        )


def out_grad_kernel(owner_ref, low_ref, grad_ref, *refs, count, share, in_slots):
    head_width = low_ref.shape[2]
    *out_refs, part_ref = refs
    for p in range(count):
        own = owner_ref[p]
        part_ref[...] = dot_tn(low_ref[p], grad_ref[...])
        if in_slots:
            rows = head_width // count
            at = pl.ds(pl.multiple_of(own * rows, rows), rows)
            for q in range(count):
                first = pl.multiple_of(owner_ref[q] * share, share)
                parts = [
                    part_ref[pl.ds(pl.multiple_of(first + a * count * share, share), share), :]
                    for a in range(rows // share)
                ]
                out_refs[q][at, :] = jnp.concatenate(parts, axis=0).astype(bf16)
        else:
            rows = pl.ds(pl.multiple_of(own * head_width, head_width), head_width)
            out_refs[0][rows, :] = part_ref[...].astype(bf16)


def lane_fold(values):
    out = values[:, :128]
    for i in range(128, values.shape[1], 128):
        out = out + values[:, i : i + 128]
    return out


def normal_parts(values):
    density = jnp.exp(-0.5 * values * values)
    t = 1.0 / (1.0 + (0.3275911 * root_half) * jnp.abs(values))
    series = 0.5 * 1.061405429
    for c in (-1.453152027, 1.421413741, -0.284496736, 0.254829592):
        series = series * t + 0.5 * c
    tail = series * t * density
    return jnp.where(values >= 0, 1.0 - tail, tail), density


def up_kernel(up_ref, down_ref, vec_ref, *refs, count, waits):
    row_refs, grad_refs = refs[:count], refs[count : 2 * count]
    act_ref, slope_ref, back_ref, stat_ref, sums_ref, pre_ref, hid_ref, part_ref = refs[2 * count + waits :]
    rows = row_refs[0].shape[0]

    @pl.when(pl.program_id(0) == 0)
    def _():
        sums_ref[...] = jnp.zeros_like(sums_ref)

    for s in range(count):
        pre_ref[s] = dot_nn(row_refs[s][...], up_ref[...])
        hid_ref[s] = dot_nn(grad_refs[s][...], down_ref[...])
    for s in range(count):
        total = jnp.zeros((8, pre_ref.shape[2]), f32)
        for c in range(rows // CHUNK):
            at = slice(c * CHUNK, (c + 1) * CHUNK)
            pre = pre_ref[s, at, :] + vec_ref[0:1]
            phi, density = normal_parts(pre)
            activated = pre * phi
            back = hid_ref[s, at, :]
            scaled = back * vec_ref[1:2]
            act_ref[s, at, :] = activated
            slope_ref[s, at, :] = (phi + pre * inv_root_tau * density).astype(bf16)
            back_ref[s, at, :] = back.astype(bf16)
            for i, terms in enumerate((activated, activated * activated, scaled, scaled * activated)):
                part_ref[s, i, at, :] = lane_fold(terms)
            total = total + fold(back)
        sums_ref[...] += total
        for i in range(4):
            stat_ref[s, i : i + 1, :] = jnp.sum(jnp.transpose(part_ref[s, i]), axis=0, keepdims=True)


def back_kernel(up_ref, vec_ref, act_ref, slope_ref, back_ref, stat_ref, *refs, count):
    hidden_ref, pre_ref, *in_refs, sums_ref, col_ref = refs[-(4 + count) :]
    rows, width = act_ref.shape[1:]

    @pl.when(pl.program_id(0) == 0)
    def _():
        sums_ref[...] = jnp.zeros_like(sums_ref)

    for s in range(count):
        stats = stat_ref[s] * (1.0 / FF)
        mean, back_mean = stats[0:1], stats[2:3]
        inverse = lax.rsqrt(stats[1:2] - mean * mean + eps)
        along = (stats[3:4] - mean * back_mean) * inverse
        for i, line in enumerate((mean, inverse, back_mean, along)):
            col_ref[s, i] = jnp.transpose(jnp.broadcast_to(line, (128, rows)))
    for s in range(count):
        first = second = jnp.zeros((8, width), f32)
        for c in range(rows // CHUNK):
            at = slice(c * CHUNK, (c + 1) * CHUNK)
            spread = [jnp.concatenate([col_ref[s, i, at, :]] * (width // 128), axis=1) for i in range(4)]
            normed = (act_ref[s, at, :] - spread[0]) * spread[1]
            back = back_ref[s, at, :].astype(f32)
            hidden_ref[s, at, :] = (normed * vec_ref[1:2] + vec_ref[2:3]).astype(bf16)
            inner = back * vec_ref[1:2] - spread[2] - normed * spread[3]
            grad = inner * (spread[1] * slope_ref[s, at, :].astype(f32))
            pre_ref[s, at, :] = grad.astype(bf16)
            first, second = first + fold(grad), second + fold(back * normed)
        sums_ref[0] += first
        sums_ref[1] += second
        in_refs[s][...] = dot_nt(pre_ref[s], up_ref[...]).astype(bf16)


def ffn_grad_kernel(down_ref, *refs, count, pairs):
    row_refs, grad_refs = refs[:count], refs[count : 2 * count]
    hidden_refs, pre_refs = refs[2 * count : 2 * count + pairs], refs[2 * count + pairs : 2 * count + 2 * pairs]
    out_ref, *down_out_refs, up_acc, down_acc = refs[2 * count + 2 * pairs :]
    hidden_width = down_ref.shape[1]
    step = pl.program_id(0)

    @pl.when(step == 0)
    def _():
        up_acc[...] = jnp.zeros_like(up_acc)
        down_acc[...] = jnp.zeros_like(down_acc)

    rows_all = jnp.concatenate([r[...] for r in row_refs], axis=0)
    grads_all = jnp.concatenate([r[...] for r in grad_refs], axis=0)
    hidden = jnp.concatenate([r[i] for r in hidden_refs for i in range(r.shape[0])], axis=0)
    pre = jnp.concatenate([r[i] for r in pre_refs for i in range(r.shape[0])], axis=0)
    up_acc[...] += dot_tn(rows_all, pre)
    down_acc[...] += dot_tn(grads_all, hidden)
    rows = row_refs[0].shape[0]
    down = dot_nt(hidden, down_ref[...]).astype(bf16)
    for i in range(count):
        down_out_refs[i][...] = down[i * rows : (i + 1) * rows]

    @pl.when(step == pl.num_programs(0) - 1)
    def _():
        out_ref[:, :hidden_width] = up_acc[...].astype(bf16)
        out_ref[:, hidden_width:] = down_acc[...].astype(bf16)


def in_grad_kernel(weight_ref, *refs, count):
    proj_refs, out_refs = refs[:count], refs[-count:]
    for s in range(count):
        out_refs[s][...] = dot_nt(proj_refs[s][...], weight_ref[...]).astype(bf16)


def qkv_grad_kernel(
    place_ref, weight_ref, lines_ref, hidden_lines_ref, head_sums_ref, normed_ref, proj_ref, *refs, count, share,
    hidden_share,
):
    token_refs = refs[:count]
    out_ref, acc_ref, unit_acc, col_acc = refs[-4:]
    step = pl.program_id(0)

    @pl.when(step == 0)
    def _():
        acc_ref[...] = jnp.zeros_like(acc_ref)
        unit_acc[...] = jnp.zeros_like(unit_acc)
        col_acc[...] = jnp.zeros_like(col_acc)

    proj = jnp.concatenate([proj_ref[s] for s in range(count)], axis=0)
    normed = jnp.concatenate([normed_ref[s] for s in range(count)], axis=0)
    unit = jnp.concatenate([unit_norm(r[...].astype(f32))[0].astype(bf16) for r in token_refs], axis=0)
    acc_ref[...] += dot_tn(normed, proj)
    unit_acc[...] += dot_tn(unit, proj)
    col_acc[...] += fold(proj.astype(f32))

    @pl.when(step == pl.num_programs(0) - 1)
    def _():
        weight = weight_ref[...].astype(f32)
        width, three = weight.shape
        devices = out_ref.shape[0]
        lane = lax.broadcasted_iota(jnp.int32, (width, 128), 1)
        gain = row_sum(weight * unit_acc[...])
        offset = row_sum(weight * jnp.sum(col_acc[...], axis=0, keepdims=True))
        norm_lines = jnp.transpose(jnp.where(lane == 0, gain, jnp.where(lane == 1, offset, 0.0)))[:8]
        low = pack_lines(lines_ref[0:8] + norm_lines, share, 0, devices)
        head_width = three // 3
        heads = jnp.concatenate(
            [jnp.zeros((2, head_width), f32), head_sums_ref[...], jnp.zeros((4, head_width), f32)], axis=0
        )
        low = low + pack_lines(heads, share, place_ref[1], devices)
        high = pack_lines(lines_ref[8:16], share, 0, devices)
        high = high + pack_lines(hidden_lines_ref[...], hidden_share, place_ref[0], devices)
        lines = jnp.concatenate([low, high, jnp.zeros((devices, 8, three - 256), f32)], axis=2)
        block = share_block(share)
        for i in range(devices):
            rows_i = acc_ref[i * share : (i + 1) * share, :]
            tail = [jnp.zeros((block - share - 8, three), f32)] if block > share + 8 else []
            out_ref[i] = jnp.concatenate([rows_i, lines[i], *tail], axis=0).astype(bf16)


def share_block(share):
    return -(-(-(-share // 8) * 8 + 8) // 16) * 16


def finish_kernel(packed_ref, out_ref, lines_ref, *, count, share, width):
    devices, _, three = packed_ref.shape
    head_width = three // 3
    total = 0.0
    for f in range(count):
        piece = packed_ref[f].astype(f32)
        for i in range(f + count, devices, count):
            piece = piece + packed_ref[i].astype(f32)
        total = total + piece[share : share + 8]
        size = min(head_width, width - f * head_width)
        for part in range(3):
            if size > 0:
                out_ref[:, part * width + f * head_width : part * width + f * head_width + size] = piece[
                    :share, part * head_width : part * head_width + size
                ]
    lines_ref[...] = total


def body(
    row_size,
    ffn_size,
    tokens,
    seq_lengths,
    key_keep,
    pre_gain,
    pre_bias,
    qkv_weight,
    query_bias,
    value_bias,
    sub_gain,
    sub_bias,
    out_weight,
    out_bias,
    ffn_gain,
    ffn_bias,
    up_bias,
    hidden_gain,
    hidden_bias,
    down_bias,
    up_weight,
    down_weight,
    out_grad,
):
    ffn_index, row_index = lax.axis_index("ffn"), lax.axis_index("rows")
    devices = row_size * ffn_size
    row_count, width = tokens.shape
    pack_total = row_count * ffn_size
    head_count = width // HEAD_DIM
    heads = -(-head_count // ffn_size)
    head_width = heads * HEAD_DIM
    three = 3 * head_width
    padded = head_width * ffn_size
    extra = padded - width
    hidden_width = up_weight.shape[1]
    share, hidden_share = pre_gain.shape[0], up_bias.shape[0]
    share_rows = share_block(share)
    owners = [slot_owner(p, ffn_index, ffn_size) for p in range(ffn_size)]
    owner_row = jnp.stack(owners).astype(jnp.int32)
    slots = range(ffn_size)
    pairs = [(i, i + 1) for i in range(0, ffn_size, 2)]
    steps = row_count // BLOCK

    thirds = jnp.pad(qkv_weight.reshape(share, 3, width), ((0, 0), (0, 0), (0, extra)))
    pieces = thirds.reshape(share, 3, ffn_size, head_width).transpose(2, 0, 1, 3)
    pieces = pieces.reshape(ffn_size, share, three)
    lines = [
        pre_gain, pre_bias, query_bias, value_bias, sub_gain, sub_bias, out_bias, ffn_gain, ffn_bias, down_bias,
        up_bias, hidden_gain, hidden_bias,
    ]
    lines = jnp.stack([jnp.pad(v, (0, 128 - v.shape[0])) for v in lines])
    lines = jnp.concatenate([lines[:8], jnp.pad(lines[8:], ((0, 3), (0, 0)))], axis=1)
    share_eight = -(-share // 8) * 8
    lines = jnp.pad(lines, ((share_eight - share, share_rows - share_eight - 8), (0, three - 256)))
    out_flat = share * width // three
    lines = jnp.concatenate([lines, out_weight.reshape(out_flat, three)], axis=0)
    pieces = jnp.concatenate([pieces, jnp.broadcast_to(lines, (ffn_size,) + lines.shape)], axis=1)
    pieces = in_order([pieces[i] for i in slots], ffn_index, ffn_size)
    pieces = jnp.stack(in_order(exchange_slots(pieces, ffn_size), ffn_index, ffn_size))
    if ffn_size == 4:
        tokens_across = swap(after(tokens, pieces), 2)
        token_slots = [tokens, swap(tokens, 1), tokens_across, swap(tokens_across, 1)]
    else:
        token_slots = gather_slots(tokens, ffn_size)
    out_rows = pieces[:, share_rows:].reshape(ffn_size * share, width)
    half = width // 2
    left = jnp.concatenate([up_weight, out_rows[:, :half]], axis=1)
    right = jnp.concatenate([down_weight.T, out_rows[:, half:]], axis=1)
    gathered = pieces[:, :share_rows].reshape(ffn_size * share_rows, three)
    special = ffn_size == 4 and row_size == 8
    if special:
        gathered = row_step(gathered, 4, row_index)
        right = row_step(right, 1, row_index)
        gathered = row_step(gathered, 2, row_index, 1)
        left = row_step(after(left, tokens_across), 4, row_index)
        gathered = gathered.reshape(4, ffn_size, share_rows, three)
        gathered_across = swap_rows(gathered, 1)
        halves = [gathered_across]
    else:
        gathered, left, right = [lax.all_gather(v, "rows", axis=0, tiled=False) for v in (gathered, left, right)]
        halves = []
    if not halves:
        gathered = gathered.reshape(devices, share_rows, three)
    place_row = jnp.stack([ffn_index * hidden_width, ffn_index * head_width, row_index & 1]).astype(jnp.int32)
    qkv_own, wide, hidden_all, bias_rows = call(
        functools.partial(
            unpack_kernel, share=share, hidden_share=hidden_share, line_at=share_eight, halves=bool(halves)
        ),
        1,
        [(place_row, SMEM), *[(g, fixed(*g.shape)) for g in [gathered] + halves]],
        [
            ((width, three), bf16, fixed(width, three)),
            ((16, width), f32, fixed(16, width)),
            ((16, hidden_width), f32, fixed(16, hidden_width)),
            ((8, three), f32, fixed(8, three)),
        ],
        "unpack",
        devices * 64 * width * 16,
        [pltpu.VMEM((devices, 8, 256), f32)],
    )
    if share % 8:
        qkv_own = gathered[:, :share, :].reshape(width, three)
    hidden_vectors = jnp.pad(hidden_all[10:13], ((0, 5), (0, 0)))
    middle_vectors = jnp.pad(wide[6:9], ((0, 5), (0, 0)))
    sub_rows = jnp.pad(
        jnp.concatenate([wide[4:6], jnp.ones((1, width), f32)], axis=0), ((0, 5), (0, extra))
    )
    sub_rows = sub_rows.reshape(8, ffn_size, head_width).transpose(1, 0, 2)
    if ffn_size == 4:
        grad_low = after(out_grad, tokens_across).astype(bf16)
        grad_across = swap(grad_low, 2)
        grad_slots = [grad_low, swap(grad_low, 1), grad_across, swap(grad_across, 1)]
        early = [grad_across]
    else:
        early = []
        grad_slots = gather_slots(out_grad.astype(bf16), ffn_size)

    block_row = pl.BlockSpec((BLOCK, width), lambda i: (i, 0))
    proj, normed_low = call(
        functools.partial(front_kernel, count=ffn_size),
        steps,
        [(qkv_own, fixed(width, three)), (bias_rows, fixed(8, three)), (wide, fixed(16, width))]
        + [(t, block_row) for t in token_slots],
        [
            ((ffn_size, row_count, three), bf16, pl.BlockSpec((ffn_size, BLOCK, three), lambda i: (0, i, 0))),
            ((ffn_size, row_count, width), bf16, pl.BlockSpec((ffn_size, BLOCK, width), lambda i: (0, i, 0))),
        ],
        "front",
        2 * pack_total * width * three,
    )
    if special:
        left = after(left, wide)
        right = after(right, wide)
        early += [left, right]
    proj, normed_low = proj.reshape(pack_total, three), normed_low.reshape(pack_total, width)

    bounds, running = [], jnp.int32(0)
    for i in range(seq_lengths.shape[1] - 1):
        running = running + seq_lengths[0, i]
        bounds.append(running)
    bounds = jnp.stack(bounds)
    firsts = jnp.arange(pack_total // BLOCK, dtype=jnp.int32) * BLOCK
    block_owner = firsts // row_count
    place = (block_owner ^ ffn_index if ffn_size == 4 else block_owner) * row_count + firsts % row_count
    keep = key_keep.reshape(pack_total // BLOCK, BLOCK)
    mixed_own, lse = attend_forward(place, bounds, proj, keep, heads, early)

    if special:
        left = row_step(left, 2, row_index, 1, wait=lse)
        right = row_step(right, 4, row_index, wait=lse)
        left = row_step(left, 1, row_index, 2)
        right = row_step(right, 2, row_index, 1)
    left, right = left.reshape(width, -1), right.reshape(width, -1)
    up_in = (left, columns(width, hidden_width, 0))
    down_in = (right, columns(width, hidden_width, 0))
    if extra:
        out_in = [
            (jnp.pad(v[:, hidden_width:], ((0, extra), (0, 0))), columns(padded, half, 0)) for v in (left, right)
        ]
    else:
        out_in = [(v, columns(width, half, hidden_width // half)) for v in (left, right)]

    mixed_slots = exchange_slots(
        [mixed_own[p * row_count : (p + 1) * row_count] for p in slots], ffn_size
    )
    block_piece = pl.BlockSpec((BLOCK, head_width), lambda i: (i, 0))
    block_pieces = pl.BlockSpec((ffn_size, BLOCK, head_width), lambda i: (0, i, 0))
    middle_in = [*out_in, (sub_rows, fixed(ffn_size, 8, head_width)), (middle_vectors, fixed(8, width))]
    sub_low, middle, ffn_low = call(
        functools.partial(middle_forward_kernel, count=ffn_size, padded=bool(extra)),
        steps,
        [(owner_row, SMEM), (tokens, block_row), *middle_in, *[(m, block_piece) for m in mixed_slots]]
        + [(grad_slots[-1], ANY)],
        [
            ((ffn_size, row_count, head_width), bf16, block_pieces),
            ((row_count, width), f32, block_row),
            ((row_count, width), bf16, block_row),
        ],
        "middle_forward",
        2 * row_count * padded * width,
    )

    fine = BLOCK // 2
    block_fine = pl.BlockSpec((fine, width), lambda i: (i, 0))
    block_pair = pl.BlockSpec((2, fine, hidden_width), lambda i: (0, i, 0))
    block_pair_row = pl.BlockSpec((2, fine, width), lambda i: (0, i, 0))
    block_stat = pl.BlockSpec((2, 8, fine), lambda i: (0, 0, i))
    block_four = pl.BlockSpec((2, 4, fine), lambda i: (0, 0, i))
    hidden_in = (hidden_vectors, fixed(8, hidden_width))
    pair_shape = (2, row_count, hidden_width)

    def up_pair(rows, grads, waits):
        return call(
            functools.partial(up_kernel, count=2, waits=len(waits)),
            2 * steps,
            [up_in, down_in, hidden_in, *[(r, block_fine) for r in rows], *[(g, block_fine) for g in grads]]
            + [(w, ANY) for w in waits],
            [
                (pair_shape, f32, block_pair),
                (pair_shape, bf16, block_pair),
                (pair_shape, bf16, block_pair),
                ((2, 8, row_count), f32, block_stat),
                ((8, hidden_width), f32, fixed(8, hidden_width)),
            ],
            "up",
            8 * row_count * width * hidden_width,
            [
                pltpu.VMEM((2, fine, hidden_width), f32),
                pltpu.VMEM((2, fine, hidden_width), f32),
                pltpu.VMEM((2, 4, fine, 128), f32),
            ],
            4 * row_count * hidden_width,
        )

    if ffn_size == 4:
        across, beside = swap(ffn_low, 2), swap(ffn_low, 1)
        ups = [up_pair([ffn_low, beside], grad_slots[:2], [])]
        slanted = swap(after(across, ups[0][3]), 1)
        row_slots = [ffn_low, beside, across, slanted]
        ups.append(up_pair([across, slanted], grad_slots[2:], [ups[0][3]]))
    else:
        row_slots = gather_slots(ffn_low, ffn_size)
        ups = [up_pair(row_slots[i : i + 2], grad_slots[i : i + 2], []) for i, _ in pairs]
    stats = sum_slots([u[3] for u in ups], ffn_size)
    backs, wait_for = [None] * len(pairs), []
    for k in reversed(range(len(pairs))):
        act, slope, back = ups[k][:3]
        backs[k] = call(
            functools.partial(back_kernel, count=2),
            2 * steps,
            [up_in, hidden_in, (act, block_pair), (slope, block_pair), (back, block_pair)]
            + [(stats[2 * k : 2 * k + 2], block_four), *[(w, ANY) for w in wait_for]],
            [
                (pair_shape, bf16, block_pair),
                (pair_shape, bf16, block_pair),
                ((row_count, width), bf16, block_fine),
                ((row_count, width), bf16, block_fine),
                ((2, 8, hidden_width), f32, fixed(2, 8, hidden_width)),
            ],
            "back",
            4 * row_count * width * hidden_width,
            [pltpu.VMEM((2, 4, fine, 128), f32)],
        )
        wait_for = [backs[k][3]]

    def reduce_pairs(near, far, wait=None):
        passed = swap(far[1], 1)
        sent = far[0].astype(f32) + passed.astype(f32)
        sent = (sent if wait is None else after(sent, wait)).astype(bf16)
        return [near[0], swap(near[1], 1), swap(sent, 2)], sent

    def scatter_pairs(parts):
        return [lax.psum_scatter(jnp.stack(parts), "ffn", scatter_dimension=0, tiled=True)[0]]

    if ffn_size == 4:
        in_terms, _ = reduce_pairs(backs[0][2:4], backs[1][2:4])
    else:
        in_terms = scatter_pairs([v for b in backs for v in b[2:4]])
    block_quarter = pl.BlockSpec((BLOCK // 2, width), lambda i: (i, 0))
    block_pair_quarter = pl.BlockSpec((2, BLOCK // 2, hidden_width), lambda i: (0, i, 0))
    weight_part, *down_parts = call(
        functools.partial(ffn_grad_kernel, count=ffn_size, pairs=len(pairs)),
        2 * steps,
        [down_in, *[(r, block_quarter) for r in row_slots], *[(g, block_quarter) for g in grad_slots]]
        + [(b[0], block_pair_quarter) for b in backs]
        + [(b[1], block_pair_quarter) for b in backs],
        [
            ((width, 2 * hidden_width), bf16, fixed(width, 2 * hidden_width)),
        ]
        + [((row_count, width), bf16, block_quarter)] * ffn_size,
        "ffn_grads",
        6 * pack_total * width * hidden_width,
        [pltpu.VMEM((width, hidden_width), f32), pltpu.VMEM((width, hidden_width), f32)],
    )
    if special:
        weight_part = weight_part.reshape(2, 2, 2, width // row_size, 2 * hidden_width)
    else:
        ties = []
        weight_grad = lax.psum_scatter(weight_part, "rows", scatter_dimension=0, tiled=True).astype(f32)

    grad_middle, middle_low, *head_low, middle_sums, sub_sums = call(
        functools.partial(
            middle_backward_kernel, count=ffn_size, addends=len(in_terms), padded=bool(extra)
        ),
        steps,
        [(owner_row, SMEM), (out_grad, block_row), (middle, block_row), *middle_in]
        + [(m, block_piece) for m in mixed_slots]
        + [(t, block_row) for t in in_terms],
        [
            ((row_count, width), f32, block_row),
            ((row_count, width), bf16, block_row),
            *[((row_count, head_width), bf16, block_piece)] * ffn_size,
            ((8, width), f32, fixed(8, width)),
            ((ffn_size, 8, head_width), f32, fixed(ffn_size, 8, head_width)),
        ],
        "middle_backward",
        2 * row_count * padded * width,
    )
    grad_own = jnp.concatenate(exchange_slots(head_low, ffn_size), axis=0)
    out_shape = (row_size * share, width) if special else (padded, width)
    out_parts = call(
        functools.partial(out_grad_kernel, count=ffn_size, share=share, in_slots=special),
        1,
        [(owner_row, SMEM), (sub_low, fixed(ffn_size, row_count, head_width)), (middle_low, fixed(row_count, width))],
        [(out_shape, bf16, fixed(*out_shape))] * (ffn_size if special else 1),
        "out_grads",
        2 * row_count * padded * width,
        [pltpu.VMEM((head_width, width), f32)],
    )
    if special:
        weight_sent, weight_kept = row_split(weight_part, 1, row_index)
        weight_across = after(swap_rows(weight_sent, 1), middle_low)
        weight_sent, weight_kept = row_split(weight_kept + weight_across.astype(f32), 2, row_index)
        ties = [weight_sent]
        weight_across = swap_rows(weight_sent, 2)
        out_terms = exchange_slots([after(v, grad_own) if i > 1 else v for i, v in enumerate(out_parts)], ffn_size)
    else:
        out_weight_own = lax.psum_scatter(
            out_parts[0][:width], ("rows", "ffn"), scatter_dimension=0, tiled=True
        ).astype(f32)

    if ffn_size == 4:
        down_terms, layer_sent = reduce_pairs(down_parts[:2], down_parts[2:], grad_own)
        ties.append(layer_sent)
    else:
        down_terms = scatter_pairs(down_parts)
    layer_out = (middle + sum(t.astype(f32) for t in down_terms) + wide[9]).astype(bf16)

    sub_flat = sub_sums[:, :2].transpose(1, 0, 2).reshape(2, padded)[:, :width]
    lines = jnp.concatenate(
        [jnp.zeros((4, width), f32), sub_flat, middle_sums[:4], jnp.zeros((6, width), f32)], axis=0
    )
    back_sums = jnp.sum(sum(b[4] for b in backs), axis=1)
    hidden_lines = jnp.concatenate(
        [
            jnp.zeros((2, hidden_width), f32),
            back_sums,
            jnp.sum(sum(u[4] for u in ups), axis=0)[None],
            jnp.zeros((3, hidden_width), f32),
        ],
        axis=0,
    )
    ties += [lines, hidden_lines]

    grad_proj, head_bias_grads = attend_backward(place, bounds, proj, keep, mixed_own, grad_own, lse, heads, ties)

    def in_pair(k, waits):
        proj_specs = [
            pl.BlockSpec((BLOCK, three), lambda i, p=p: (p * steps + i, 0)) for p in pairs[k]
        ]
        return call(
            functools.partial(in_grad_kernel, count=2),
            steps,
            [(qkv_own, fixed(width, three)), *[(grad_proj, spec) for spec in proj_specs]]
            + [(w, ANY) for w in waits],
            [((row_count, width), bf16, block_row)] * 2,
            "in_grads",
            4 * row_count * width * three,
        )

    if special:
        weight_sent, weight_kept = row_split(weight_kept + after(weight_across, grad_proj).astype(f32), 4, row_index)
        weight_across = swap_rows(weight_sent, 4)
        out_sum = sum(after(v, grad_proj).astype(f32) for v in out_terms).reshape(2, 2, 2, share, width)
        out_sent, out_kept = row_split(out_sum, 1, row_index)
        out_across = swap_rows(out_sent, 1)
        far = in_pair(1, [down_terms[2], out_sent])
        sent = (far[0].astype(f32) + swap(far[1], 1).astype(f32)).astype(bf16)
        across = swap(sent, 2)
        out_sent, out_kept = row_split(out_kept + after(out_across, far[0]).astype(f32), 2, row_index)
        out_across = swap_rows(out_sent, 2)
        late = [weight_sent, out_sent, sent]
    else:
        late = []
    eighth = row_count // 4
    (packed,) = call(
        functools.partial(
            qkv_grad_kernel, count=ffn_size, share=share, hidden_share=hidden_share
        ),
        4,
        [
            (place_row, SMEM),
            (qkv_own, fixed(width, three)),
            (lines, fixed(16, width)),
            (hidden_lines, fixed(8, hidden_width)),
            (head_bias_grads, fixed(2, head_width)),
            (
                normed_low.reshape(ffn_size, row_count, width),
                pl.BlockSpec((ffn_size, eighth, width), lambda i: (0, i, 0)),
            ),
            (
                grad_proj.reshape(ffn_size, row_count, three),
                pl.BlockSpec((ffn_size, eighth, three), lambda i: (0, i, 0)),
            ),
            *[(t, pl.BlockSpec((eighth, width), lambda i: (i, 0))) for t in token_slots],
            *[(v, ANY) for v in late],
        ],
        [((devices, share_rows, three), bf16, fixed(devices, share_rows, three))],
        "qkv_grads",
        4 * pack_total * width * three,
        [pltpu.VMEM((width, three), f32), pltpu.VMEM((width, three), f32), pltpu.VMEM((8, three), f32)],
    )
    if special:
        near = in_pair(0, [packed, across])
        in_terms = [near[0], swap(near[1], 1), across]
        weight_grad = weight_kept + after(weight_across, near[0]).astype(f32)
        out_sent, out_kept = row_split(out_kept + after(out_across, packed).astype(f32), 4, row_index)
        out_weight_own = (out_kept + after(swap_rows(out_sent, 4), near[0]).astype(f32)).reshape(share, width)
    else:
        in_terms = scatter_pairs([v for k in range(len(pairs)) for v in in_pair(k, [])])
    packed = lax.all_to_all(packed, ("rows", "ffn"), split_axis=0, concat_axis=0, tiled=True)
    qkv_weight_grad, line_own = call(
        functools.partial(finish_kernel, count=ffn_size, share=share, width=width),
        1,
        [(packed, fixed(*packed.shape))],
        [((share, 3 * width), f32, fixed(share, 3 * width)), ((8, three), f32, fixed(8, three))],
        "finish",
        devices * share * three,
    )

    weight_grad = weight_grad.reshape(-1, 2 * hidden_width)
    up_weight_grad, down_weight_grad = weight_grad[:, :hidden_width], weight_grad[:, hidden_width:].T

    unit_own, inverse_own = unit_norm(tokens.astype(f32))
    in_scaled = sum(t.astype(f32) for t in in_terms) * wide[0]
    in_adjusted = (
        in_scaled
        - jnp.mean(in_scaled, axis=-1, keepdims=True)
        - unit_own * jnp.mean(in_scaled * unit_own, axis=-1, keepdims=True)
    )
    tokens_grad = grad_middle + in_adjusted * inverse_own

    vectors = [line_own[i, :share] for i in range(8)] + [line_own[i, 128 : 128 + share] for i in range(2)]
    small = vectors
    hidden_small = [line_own[i, 128 : 128 + hidden_share] for i in range(2, 5)]
    return (
        layer_out,
        tokens_grad,
        small[0],
        small[1],
        qkv_weight_grad,
        small[2],
        small[3],
        small[4],
        small[5],
        out_weight_own,
        small[6],
        small[7],
        small[8],
        hidden_small[0],
        hidden_small[1],
        hidden_small[2],
        small[9],
        up_weight_grad,
        down_weight_grad,
    )


def solution(mesh):
    flat, matrix = P(("rows", "ffn")), P(("rows", "ffn"), None)
    in_specs = (
        matrix, P("rows", None), P("rows"), flat, flat, matrix, flat, flat, flat, flat, matrix, flat, flat, flat,
        flat, flat, flat, flat, P("rows", "ffn"), P("ffn", "rows"), matrix,
    )
    out_specs = (
        matrix, matrix, flat, flat, matrix, flat, flat, flat, flat, matrix, flat, flat, flat, flat, flat, flat, flat,
        P("rows", "ffn"), P("ffn", "rows"),
    )
    return jax.shard_map(
        functools.partial(body, mesh.shape["rows"], mesh.shape["ffn"]),
        mesh=mesh,
        in_specs=in_specs,
        out_specs=out_specs,
        check_vma=False,
    )
```

```python
import functools

import jax
import jax.numpy as jnp
from jax import lax
from jax.experimental import pallas as pl
from jax.experimental.pallas import tpu as pltpu
from jax.sharding import PartitionSpec as P

HEAD_DIM = 64
FF = 3072
BLOCK = 256
SMALL = 20

eps = 1e-05
neg_big = -1e30
score_scale = 0.125
root_half = 0.7071067811865476
inv_root_tau = 0.3989422804014327

f32 = jnp.float32
bf16 = jnp.bfloat16


def swap(values, flip):
    return lax.ppermute(values, "ffn", [(i, i ^ flip) for i in range(4)])


def swap_rows(values, flip):
    return lax.ppermute(values, "rows", [(i, i ^ flip) for i in range(8)])


def slot_owner(slot, ffn_index, ffn_size):
    return ffn_index ^ slot if ffn_size == 4 else jnp.int32(slot)


def gather_slots(values, ffn_size):
    if ffn_size != 4:
        whole = lax.all_gather(values, "ffn", axis=0, tiled=False)
        return [whole[i] for i in range(ffn_size)]
    across = swap(values, 2)
    beside = swap(values, 1)
    return [values, beside, across, swap(across, 1)]


def exchange_slots(pieces, ffn_size):
    if ffn_size != 4:
        whole = lax.all_to_all(jnp.stack(pieces), "ffn", split_axis=0, concat_axis=0, tiled=True)
        return [whole[i] for i in range(ffn_size)]
    across = swap(pieces[2], 2)
    slanted = swap(pieces[3], 3)
    beside = swap(pieces[1], 1)
    return [pieces[0], beside, across, slanted]


def in_order(slots, ffn_index, ffn_size):
    if ffn_size != 4:
        return slots
    odd, high = (ffn_index & 1) > 0, (ffn_index & 2) > 0
    low = [jnp.where(odd, slots[p ^ 1], slots[p]) for p in range(4)]
    return [jnp.where(high, low[p ^ 2], low[p]) for p in range(4)]


def sum_slots(pairs, ffn_size):
    values = jnp.concatenate(pairs, axis=0)[:, :4, :]
    if ffn_size != 4:
        return lax.psum(values, "ffn")
    beside = swap(values, 1)
    values = values + jnp.stack([beside[1], beside[0], beside[3], beside[2]])
    across = swap(values, 2)
    return values + jnp.stack([across[2], across[3], across[0], across[1]])


ROW_AXIS = {4: 0, 2: 1, 1: 2}


def row_bit(flip, row_index):
    return (row_index >> (2 - ROW_AXIS[flip])) & 1


def row_step(whole, flip, row_index, outer=0, wait=None):
    bit = row_bit(flip, row_index)
    other = swap_rows(whole, flip)
    if wait is not None:
        other = after(other, wait)
    return jnp.stack([jnp.where(bit > 0, other, whole), jnp.where(bit > 0, whole, other)], axis=outer)


def row_split(whole, flip, row_index):
    axis, bit = ROW_AXIS[flip], row_bit(flip, row_index)
    sent = lax.dynamic_slice_in_dim(whole, 1 - bit, 1, axis).astype(bf16)
    return sent, lax.dynamic_slice_in_dim(whole, bit, 1, axis).astype(f32)


def split_add(whole, flip, row_index, wait):
    sent, kept = row_split(whole, flip, row_index)
    sent = after(sent, wait)
    return kept + swap_rows(sent, flip).astype(f32), sent


def row_halves(whole, flips, row_index, waits):
    sends = []
    for flip, wait in zip(flips, waits):
        sent, kept = row_split(whole, flip, row_index)
        sends.append(sent)
        other = swap_rows(sent, flip)
        whole = kept + (other if wait is None else after(other, wait)).astype(f32)
    return whole[0, 0, 0], sends


def after(values, other):
    first = lax.slice(other, (0,) * other.ndim, (1,) * other.ndim).reshape(())
    return values + (first * 0).astype(values.dtype)


NT = (((1,), (1,)), ((), ()))


def dot_nt(a, b):
    return lax.dot_general(a, b, NT, preferred_element_type=f32)


def dot_nn(a, b):
    return jnp.dot(a, b, preferred_element_type=f32)


def start_row(first, bounds_ref, bound_count):
    places = first + lax.broadcasted_iota(jnp.int32, (1, BLOCK), 1)
    start = jnp.zeros((1, BLOCK), jnp.int32)
    for i in range(bound_count):
        bound = bounds_ref[i]
        start = jnp.where(places >= bound, jnp.maximum(start, bound), start)
    return places, start


def first_block(first, bounds_ref, bound_count):
    start = jnp.int32(0)
    for i in range(bound_count):
        bound = bounds_ref[i]
        start = jnp.where(first >= bound, jnp.maximum(start, bound), start)
    return start // BLOCK


def load_keys(keep_ref, limit_ref, blocks):
    for j in range(blocks):
        row = keep_ref[j : j + 1, :]
        places = j * BLOCK + lax.broadcasted_iota(jnp.int32, (1, BLOCK), 1)
        limits = jnp.where(row > 0, places, 1 << 24).astype(f32)
        column = jnp.transpose(jnp.broadcast_to(limits, (128, BLOCK)))
        limit_ref[j * BLOCK : (j + 1) * BLOCK, :] = column


def block_bias(limit_ref, key_first, query_places, query_start):
    limit = limit_ref[pl.ds(key_first, BLOCK), :]
    limit = jnp.concatenate([limit] * (BLOCK // 128), axis=1)
    key_places = key_first + lax.broadcasted_iota(jnp.int32, (BLOCK, BLOCK), 0)
    before = (limit < query_places.astype(f32)) & (key_places >= query_start)
    return jnp.where(before | (key_places == query_places), 0.0, neg_big)


def forward_kernel(
    place_ref, bounds_ref, proj_ref, keep_ref, *refs, heads, bound_count
):
    out_ref, lse_ref, limit_ref, value_t_ref = refs[-4:]
    total = proj_ref.shape[0]
    blocks = total // BLOCK
    width = heads * HEAD_DIM
    load_keys(keep_ref, limit_ref, blocks)
    for j in range(blocks):
        rows = slice(j * BLOCK, (j + 1) * BLOCK)
        value_t_ref[:, rows] = jnp.transpose(proj_ref[rows, 2 * width :].astype(f32)).astype(bf16)

    def query_step(qi, _):
        query_first = pl.multiple_of(qi * BLOCK, BLOCK)
        query_at = pl.multiple_of(place_ref[qi], BLOCK)
        places, starts = start_row(query_first, bounds_ref, bound_count)
        queries = proj_ref[pl.ds(query_at, BLOCK), :width] * jnp.asarray(score_scale, bf16)

        def block_scores(kj):
            key_first = pl.multiple_of(kj * BLOCK, BLOCK)
            key_at = pl.multiple_of(place_ref[kj], BLOCK)
            bias = block_bias(limit_ref, key_first, places, starts)
            keys = proj_ref[pl.ds(key_at, BLOCK), width : 2 * width]
            heads_cols = [slice(h * HEAD_DIM, (h + 1) * HEAD_DIM) for h in range(heads)]
            return key_at, [dot_nt(keys[:, cols], queries[:, cols]) + bias for cols in heads_cols]

        def top_step(kj, tops):
            _, scores = block_scores(kj)
            return tuple(jnp.maximum(t, jnp.max(v, axis=0, keepdims=True)) for t, v in zip(tops, scores))

        first = first_block(query_first, bounds_ref, bound_count)
        tops = lax.fori_loop(first, qi + 1, top_step, (jnp.full((1, BLOCK), neg_big, f32),) * heads)

        def value_step(kj, carry):
            key_at, scores = block_scores(kj)
            values_t = value_t_ref[:, pl.ds(key_at, BLOCK)]
            out = []
            for h in range(heads):
                cols = slice(h * HEAD_DIM, (h + 1) * HEAD_DIM)
                weights = jnp.exp(scores[h] - tops[h])
                total_sum, mixed = carry[h]
                out.append(
                    (
                        total_sum + jnp.sum(weights, axis=0, keepdims=True),
                        mixed + dot_nn(values_t[cols, :], weights.astype(bf16)),
                    )
                )
            return tuple(out)

        empty = (jnp.zeros((1, BLOCK), f32), jnp.zeros((HEAD_DIM, BLOCK), f32))
        done = lax.fori_loop(first, qi + 1, value_step, (empty,) * heads)
        mixed_t = jnp.concatenate([mixed / total_sum for total_sum, mixed in done], axis=0)
        out_ref[pl.ds(query_at, BLOCK), :] = jnp.transpose(mixed_t).astype(out_ref.dtype)
        for h in range(heads):
            lse_ref[h : h + 1, pl.ds(query_first, BLOCK)] = tops[h] + jnp.log(done[h][0])
        return 0

    lax.fori_loop(0, blocks, query_step, 0)


def backward_kernel(
    place_ref, bounds_ref, proj_ref, keep_ref, mixed_ref, grad_ref, lse_ref, *refs, heads, bound_count
):
    out_ref, bias_ref, limit_ref, key_t_ref, key_acc, value_acc = refs[-6:]
    total = proj_ref.shape[0]
    blocks = total // BLOCK
    width = heads * HEAD_DIM
    load_keys(keep_ref, limit_ref, blocks)
    for j in range(blocks):
        rows = slice(j * BLOCK, (j + 1) * BLOCK)
        key_t_ref[:, rows] = jnp.transpose(proj_ref[rows, width : 2 * width].astype(f32)).astype(bf16)
    key_acc[...] = jnp.zeros_like(key_acc)
    value_acc[...] = jnp.zeros_like(value_acc)
    bias_ref[...] = jnp.zeros_like(bias_ref)

    def query_step(qi, _):
        query_first = pl.multiple_of(qi * BLOCK, BLOCK)
        query_at = pl.multiple_of(place_ref[qi], BLOCK)
        query_rows = pl.ds(query_at, BLOCK)
        places, starts = start_row(query_first, bounds_ref, bound_count)
        queries = proj_ref[query_rows, :width] * jnp.asarray(score_scale, bf16)
        grads = grad_ref[query_rows, :]
        product_t = jnp.transpose(grads.astype(f32) * mixed_ref[query_rows, :].astype(f32))
        lse = [lse_ref[h : h + 1, pl.ds(query_first, BLOCK)] for h in range(heads)]
        delta = [
            jnp.sum(product_t[h * HEAD_DIM : (h + 1) * HEAD_DIM, :], axis=0, keepdims=True) for h in range(heads)
        ]

        def key_step(kj, carry):
            key_first = pl.multiple_of(kj * BLOCK, BLOCK)
            key_rows = pl.ds(pl.multiple_of(place_ref[kj], BLOCK), BLOCK)
            bias = block_bias(limit_ref, key_first, places, starts)
            keys = proj_ref[key_rows, width : 2 * width]
            values = proj_ref[key_rows, 2 * width :]
            keys_t = key_t_ref[:, key_rows]
            out, key_parts, value_parts = [], [], []
            for h in range(heads):
                cols = slice(h * HEAD_DIM, (h + 1) * HEAD_DIM)
                scores = dot_nt(keys[:, cols], queries[:, cols]) + bias
                probs = jnp.exp(scores - lse[h])
                grad_probs = dot_nt(values[:, cols], grads[:, cols])
                grad_scores = (probs * (grad_probs - delta[h])).astype(bf16)
                value_parts.append(dot_nn(probs.astype(bf16), grads[:, cols]))
                key_parts.append(dot_nn(grad_scores, queries[:, cols]))
                out.append(carry[h] + dot_nn(keys_t[cols, :], grad_scores))
            key_acc[key_rows, :] += jnp.concatenate(key_parts, axis=1)
            value_acc[key_rows, :] += jnp.concatenate(value_parts, axis=1)
            return tuple(out)

        zero = jnp.zeros((HEAD_DIM, BLOCK), f32)
        done = lax.fori_loop(first_block(query_first, bounds_ref, bound_count), qi + 1, key_step, (zero,) * heads)
        grad_query = jnp.transpose(jnp.concatenate(done, axis=0)) * score_scale
        bias_ref[0:1, :] += jnp.sum(grad_query, axis=0, keepdims=True)
        out_ref[query_rows, :width] = grad_query.astype(bf16)
        return 0

    lax.fori_loop(0, blocks, query_step, 0)
    bias_ref[1:2, :] = jnp.sum(value_acc[...], axis=0, keepdims=True)
    out_ref[:, width : 2 * width] = key_acc[...].astype(bf16)
    out_ref[:, 2 * width :] = value_acc[...].astype(bf16)


ANY = pl.BlockSpec(memory_space=pl.ANY)
SMEM = pl.BlockSpec(memory_space=pltpu.SMEM)
VMEM = pl.BlockSpec(memory_space=pltpu.VMEM)


def attend_forward(place, bounds, proj, keep, heads, waits):
    total, width = proj.shape[0], heads * HEAD_DIM
    pairs = total * total // 6
    return pl.pallas_call(
        functools.partial(forward_kernel, heads=heads, bound_count=bounds.shape[0]),
        out_shape=(jax.ShapeDtypeStruct((total, width), bf16), jax.ShapeDtypeStruct((heads, total), f32)),
        in_specs=[SMEM, SMEM, VMEM, VMEM] + [ANY] * len(waits),
        out_specs=(VMEM, VMEM),
        scratch_shapes=[
            pltpu.VMEM((total, 128), f32),
            pltpu.VMEM((width, total), bf16),
        ],
        compiler_params=pltpu.CompilerParams(vmem_limit_bytes=40 << 20),
        cost_estimate=pl.CostEstimate(
            flops=16 * pairs * width // SMALL, bytes_accessed=1024, transcendentals=0
        ),
        name="attend_forward",
    )(place, bounds, proj, keep, *waits)


def attend_backward(place, bounds, proj, keep, mixed, grads, lse, heads, waits):
    total, width = proj.shape[0], heads * HEAD_DIM
    pairs = total * total // 6
    return pl.pallas_call(
        functools.partial(backward_kernel, heads=heads, bound_count=bounds.shape[0]),
        out_shape=(jax.ShapeDtypeStruct((total, 3 * width), bf16), jax.ShapeDtypeStruct((2, width), f32)),
        in_specs=[SMEM, SMEM, VMEM, VMEM, VMEM, VMEM, VMEM] + [ANY] * len(waits),
        out_specs=(VMEM, VMEM),
        scratch_shapes=[
            pltpu.VMEM((total, 128), f32),
            pltpu.VMEM((width, total), bf16),
            pltpu.VMEM((total, width), f32),
            pltpu.VMEM((total, width), f32),
        ],
        compiler_params=pltpu.CompilerParams(vmem_limit_bytes=50 << 20),
        cost_estimate=pl.CostEstimate(
            flops=40 * pairs * width // SMALL, bytes_accessed=1024, transcendentals=0
        ),
        name="attend_backward",
    )(place, bounds, proj, keep, mixed, grads, lse, *waits)


TN = (((0,), (0,)), ((), ()))
CHUNK = 16


def dot_tn(a, b):
    return lax.dot_general(a, b, TN, preferred_element_type=f32)


def fixed(*shape):
    return pl.BlockSpec(shape, lambda i: (0,) * len(shape))


def columns(rows, width, index):
    return pl.BlockSpec((rows, width), lambda i: (0, index))


def call(kernel, grid, inputs, outputs, name, flops, scratch=(), transcendentals=0):
    moved = sum(a.size * a.dtype.itemsize for a, spec in inputs if spec.memory_space is None)
    return pl.pallas_call(
        kernel,
        grid=(grid,),
        in_specs=[spec for _, spec in inputs],
        out_specs=tuple(spec for _, _, spec in outputs),
        out_shape=tuple(jax.ShapeDtypeStruct(shape, dtype) for shape, dtype, _ in outputs),
        scratch_shapes=list(scratch),
        compiler_params=pltpu.CompilerParams(
            vmem_limit_bytes=58 << 20, dimension_semantics=("arbitrary",)
        ),
        cost_estimate=pl.CostEstimate(
            flops=flops // SMALL, bytes_accessed=moved // SMALL, transcendentals=transcendentals // SMALL
        ),
        name=name,
    )(*[a for a, _ in inputs])


def row_sum(values):
    return jnp.sum(values, axis=-1, keepdims=True)


def fold(values):
    out = values[:8]
    for i in range(8, values.shape[0], 8):
        out = out + values[i : i + 8]
    return out


def unit_norm(values):
    center = values - jnp.mean(values, axis=-1, keepdims=True)
    inverse = lax.rsqrt(jnp.mean(center * center, axis=-1, keepdims=True) + eps)
    return center * inverse, inverse


def sub_norm(pieces, real, width):
    mean = sum(row_sum(p) for p in pieces) * (1.0 / width)
    centers = [p - mean for p in pieces]
    if real is not None:
        centers = [c * r for c, r in zip(centers, real)]
    inverse = lax.rsqrt(sum(row_sum(c * c) for c in centers) * (1.0 / width) + eps)
    return [c * inverse for c in centers], inverse


def sub_vectors(owner_ref, sub_ref, count, padded):
    rows = [sub_ref[owner_ref[p]] for p in range(count)]
    real = [r[2:3] for r in rows] if padded else None
    return [r[0:1] for r in rows], [r[1:2] for r in rows], real


def place_columns(share, width, first, rows):
    lane = lax.broadcasted_iota(jnp.int32, (128, width), 0)
    column = first + lax.broadcasted_iota(jnp.int32, (128, width), 1)
    matrix = jnp.where(lane == column % share, 1.0, 0.0).astype(bf16)
    device = lax.broadcasted_iota(jnp.int32, (rows, 1, width), 0)
    column = first + lax.broadcasted_iota(jnp.int32, (rows, 1, width), 2)
    return jnp.where(device == column // share, 1.0, 0.0), matrix


def unpack_kernel(place_ref, here_ref, *refs, share, hidden_share, line_at, halves):
    weight_ref, wide_ref, hidden_ref, bias_ref, lines_ref = refs[-5:]
    devices = lines_ref.shape[0]
    blocks = here_ref.shape[1]
    together = 2 if share % 16 else 1

    def block_of(i):
        if not halves:
            return here_ref[i].astype(f32)
        per = devices // 8
        row, own = i // per, i % per
        own_rows = here_ref[row // 2, own].astype(f32)
        other_rows = refs[0][row // 2, own].astype(f32)
        return jnp.where(place_ref[2] == row % 2, own_rows, other_rows)

    for i in range(0, devices, together):
        both = [block_of(i + j) for j in range(together)]
        for j in range(together):
            lines_ref[i + j] = both[j][line_at : line_at + 8, :256].astype(bf16).astype(f32)
        if share % 8 == 0:
            rows = jnp.concatenate([b[:share] for b in both], axis=0)
            weight_ref[i * share : (i + together) * share, :] = rows.astype(bf16)

    def spread(size, first, width):
        mine, matrix = place_columns(size, width, first, devices)
        out = []
        for part in range(2):
            lines = lines_ref[:, :, part * 128 : (part + 1) * 128].reshape(devices * 8, 128).astype(bf16)
            out.append(jnp.sum(dot_nn(lines, matrix).reshape(devices, 8, width) * mine, axis=0))
        return jnp.concatenate(out, axis=0)

    head_width = bias_ref.shape[1] // 3
    wide_ref[...] = spread(share, 0, wide_ref.shape[1])
    hidden_ref[...] = spread(hidden_share, place_ref[0], hidden_ref.shape[1])
    own = spread(share, place_ref[1], head_width)[:8]
    zero = jnp.zeros((1, head_width), f32)
    bias_ref[...] = jnp.broadcast_to(
        jnp.concatenate([own[2:3], zero, own[3:4]], axis=1), bias_ref.shape
    )


def pack_lines(values, share, first, devices):
    mine, matrix = place_columns(share, values.shape[1], first, devices)
    lines = (values[None] * mine).reshape(devices * 8, values.shape[1]).astype(bf16)
    return dot_nt(lines, matrix).reshape(devices, 8, 128)


def front_kernel(weight_ref, bias_ref, vec_ref, *refs, count):
    token_refs, (proj_ref, normed_ref) = refs[:count], refs[-2:]
    for s in range(count):
        unit, _ = unit_norm(token_refs[s][...].astype(f32))
        normed = (unit * vec_ref[0:1] + vec_ref[1:2]).astype(bf16)
        normed_ref[s] = normed
        proj_ref[s] = (dot_nn(normed, weight_ref[...]) + bias_ref[0:1]).astype(bf16)


def middle_forward_kernel(owner_ref, tokens_ref, left_ref, right_ref, sub_ref, vec_ref, *refs, count, padded):
    piece_refs, (low_ref, middle_ref, ffn_ref) = refs[:count], refs[-3:]
    head_width, width = low_ref.shape[2], middle_ref.shape[1]
    gains, offsets, real = sub_vectors(owner_ref, sub_ref, count, padded)
    units, _ = sub_norm([r[...].astype(f32) for r in piece_refs], real, width)
    middle = tokens_ref[...].astype(f32) + vec_ref[0:1]
    for p in range(count):
        low = (units[p] * gains[p] + offsets[p]).astype(bf16)
        low_ref[p] = low
        rows = pl.ds(pl.multiple_of(owner_ref[p] * head_width, head_width), head_width)
        middle = middle + dot_nn(low, jnp.concatenate([left_ref[rows, :], right_ref[rows, :]], axis=1))
    middle_ref[...] = middle
    unit, _ = unit_norm(middle)
    ffn_ref[...] = (unit * vec_ref[1:2] + vec_ref[2:3]).astype(bf16)


def middle_backward_kernel(
    owner_ref, out_grad_ref, middle_ref, left_ref, right_ref, sub_ref, vec_ref, *refs, count, addends, padded
):
    piece_refs, add_refs = refs[:count], refs[count : count + addends]
    grad_ref, grad_low_ref, *head_refs, sums_ref, sub_sums_ref = refs[count + addends :]
    head_width, width = head_refs[0].shape[1], middle_ref.shape[1]

    @pl.when(pl.program_id(0) == 0)
    def _():
        sums_ref[...] = jnp.zeros_like(sums_ref)
        sub_sums_ref[...] = jnp.zeros_like(sub_sums_ref)

    upstream = sum(r[...].astype(f32) for r in add_refs)
    unit, inverse = unit_norm(middle_ref[...])
    scaled = upstream * vec_ref[1:2]
    out_grad = out_grad_ref[...]
    grad = out_grad + inverse * (
        scaled - row_sum(scaled) * (1.0 / width) - unit * (row_sum(scaled * unit) * (1.0 / width))
    )
    grad_ref[...] = grad
    low = grad.astype(bf16)
    grad_low_ref[...] = low
    for i, terms in enumerate((grad, upstream * unit, upstream, out_grad)):
        sums_ref[i : i + 1, :] += jnp.sum(terms, axis=0, keepdims=True)
    gains, _, real = sub_vectors(owner_ref, sub_ref, count, padded)
    units, sub_inverse = sub_norm([r[...].astype(f32) for r in piece_refs], real, width)
    grads = []
    for p in range(count):
        rows = pl.ds(pl.multiple_of(owner_ref[p] * head_width, head_width), head_width)
        grads.append(dot_nt(low, jnp.concatenate([left_ref[rows, :], right_ref[rows, :]], axis=1)))
    sub_scaled = [g * gain for g, gain in zip(grads, gains)]
    mean = sum(row_sum(v) for v in sub_scaled) * (1.0 / width)
    along = sum(row_sum(v * u) for v, u in zip(sub_scaled, units)) * (1.0 / width)
    for p in range(count):
        head_refs[p][...] = ((sub_scaled[p] - mean - units[p] * along) * sub_inverse).astype(bf16)
        own = owner_ref[p]
        sub_sums_ref[own] += jnp.concatenate(
            [
                jnp.sum(grads[p] * units[p], axis=0, keepdims=True),
                jnp.sum(grads[p], axis=0, keepdims=True),
                jnp.zeros((6, head_width), f32),
            ],
            axis=0,
        )


def out_grad_kernel(owner_ref, low_ref, grad_ref, *refs, count, share, in_slots):
    head_width = low_ref.shape[2]
    *out_refs, part_ref = refs
    for p in range(count):
        own = owner_ref[p]
        part_ref[...] = dot_tn(low_ref[p], grad_ref[...])
        if in_slots:
            rows = head_width // count
            at = pl.ds(pl.multiple_of(own * rows, rows), rows)
            for q in range(count):
                first = pl.multiple_of(owner_ref[q] * share, share)
                parts = [
                    part_ref[pl.ds(pl.multiple_of(first + a * count * share, share), share), :]
                    for a in range(rows // share)
                ]
                out_refs[q][at, :] = jnp.concatenate(parts, axis=0).astype(bf16)
        else:
            rows = pl.ds(pl.multiple_of(own * head_width, head_width), head_width)
            out_refs[0][rows, :] = part_ref[...].astype(bf16)


def lane_fold(values):
    out = values[:, :128]
    for i in range(128, values.shape[1], 128):
        out = out + values[:, i : i + 128]
    return out


def normal_parts(values):
    density = jnp.exp(-0.5 * values * values)
    t = 1.0 / (1.0 + (0.3275911 * root_half) * jnp.abs(values))
    series = 0.5 * 1.061405429
    for c in (-1.453152027, 1.421413741, -0.284496736, 0.254829592):
        series = series * t + 0.5 * c
    tail = series * t * density
    return jnp.where(values >= 0, 1.0 - tail, tail), density


def up_kernel(up_ref, down_ref, vec_ref, *refs, count, waits):
    row_refs, grad_refs = refs[:count], refs[count : 2 * count]
    act_ref, slope_ref, back_ref, stat_ref, sums_ref, pre_ref, hid_ref, part_ref = refs[2 * count + waits :]
    rows = row_refs[0].shape[0]

    @pl.when(pl.program_id(0) == 0)
    def _():
        sums_ref[...] = jnp.zeros_like(sums_ref)

    pre_all = dot_nn(jnp.concatenate([r[...] for r in row_refs], axis=0), up_ref[...])
    hid_all = dot_nn(jnp.concatenate([r[...] for r in grad_refs], axis=0), down_ref[...])
    for s in range(count):
        pre_ref[s] = pre_all[s * rows : (s + 1) * rows]
        hid_ref[s] = hid_all[s * rows : (s + 1) * rows]
    for s in range(count):
        total = jnp.zeros((8, pre_ref.shape[2]), f32)
        for c in range(rows // CHUNK):
            at = slice(c * CHUNK, (c + 1) * CHUNK)
            pre = pre_ref[s, at, :] + vec_ref[0:1]
            phi, density = normal_parts(pre)
            activated = pre * phi
            back = hid_ref[s, at, :]
            scaled = back * vec_ref[1:2]
            act_ref[s, at, :] = activated
            slope_ref[s, at, :] = (phi + pre * inv_root_tau * density).astype(bf16)
            back_ref[s, at, :] = back.astype(bf16)
            for i, terms in enumerate((activated, activated * activated, scaled, scaled * activated)):
                part_ref[s, i, at, :] = lane_fold(terms)
            total = total + fold(back)
        sums_ref[...] += total
        for i in range(4):
            stat_ref[s, i : i + 1, :] = jnp.sum(jnp.transpose(part_ref[s, i]), axis=0, keepdims=True)


def back_kernel(up_ref, vec_ref, act_ref, slope_ref, back_ref, stat_ref, *refs, count):
    hidden_ref, pre_ref, *in_refs, sums_ref, col_ref = refs[-(4 + count) :]
    rows, width = act_ref.shape[1:]

    @pl.when(pl.program_id(0) == 0)
    def _():
        sums_ref[...] = jnp.zeros_like(sums_ref)

    for s in range(count):
        stats = stat_ref[s] * (1.0 / FF)
        mean, back_mean = stats[0:1], stats[2:3]
        inverse = lax.rsqrt(stats[1:2] - mean * mean + eps)
        along = (stats[3:4] - mean * back_mean) * inverse
        for i, line in enumerate((mean, inverse, back_mean, along)):
            col_ref[s, i] = jnp.transpose(jnp.broadcast_to(line, (128, rows)))
    for s in range(count):
        first = second = jnp.zeros((8, width), f32)
        for c in range(rows // CHUNK):
            at = slice(c * CHUNK, (c + 1) * CHUNK)
            spread = [jnp.concatenate([col_ref[s, i, at, :]] * (width // 128), axis=1) for i in range(4)]
            normed = (act_ref[s, at, :] - spread[0]) * spread[1]
            back = back_ref[s, at, :].astype(f32)
            hidden_ref[s, at, :] = (normed * vec_ref[1:2] + vec_ref[2:3]).astype(bf16)
            inner = back * vec_ref[1:2] - spread[2] - normed * spread[3]
            grad = inner * (spread[1] * slope_ref[s, at, :].astype(f32))
            pre_ref[s, at, :] = grad.astype(bf16)
            first, second = first + fold(grad), second + fold(back * normed)
        sums_ref[0] += first
        sums_ref[1] += second
    back_all = dot_nt(jnp.concatenate([pre_ref[s] for s in range(count)], axis=0), up_ref[...]).astype(bf16)
    for s in range(count):
        in_refs[s][...] = back_all[s * rows : (s + 1) * rows]


def ffn_grad_kernel(down_ref, *refs, count, pairs):
    row_refs, grad_refs = refs[:count], refs[count : 2 * count]
    hidden_refs, pre_refs = refs[2 * count : 2 * count + pairs], refs[2 * count + pairs : 2 * count + 2 * pairs]
    out_ref, *down_out_refs, up_acc, down_acc = refs[2 * count + 2 * pairs :]
    hidden_width = down_ref.shape[1]
    step = pl.program_id(0)

    @pl.when(step == 0)
    def _():
        up_acc[...] = jnp.zeros_like(up_acc)
        down_acc[...] = jnp.zeros_like(down_acc)

    rows_all = jnp.concatenate([r[...] for r in row_refs], axis=0)
    grads_all = jnp.concatenate([r[...] for r in grad_refs], axis=0)
    hidden = jnp.concatenate([r[i] for r in hidden_refs for i in range(r.shape[0])], axis=0)
    pre = jnp.concatenate([r[i] for r in pre_refs for i in range(r.shape[0])], axis=0)
    up_acc[...] += dot_tn(rows_all, pre)
    down_acc[...] += dot_tn(grads_all, hidden)
    rows = row_refs[0].shape[0]
    down = dot_nt(hidden, down_ref[...]).astype(bf16)
    for i in range(count):
        down_out_refs[i][...] = down[i * rows : (i + 1) * rows]

    @pl.when(step == pl.num_programs(0) - 1)
    def _():
        out_ref[:, :hidden_width] = up_acc[...].astype(bf16)
        out_ref[:, hidden_width:] = down_acc[...].astype(bf16)


def in_grad_kernel(weight_ref, *refs, count):
    proj_refs, out_refs = refs[:count], refs[-count:]
    for s in range(count):
        out_refs[s][...] = dot_nt(proj_refs[s][...], weight_ref[...]).astype(bf16)


def qkv_grad_kernel(
    place_ref, weight_ref, lines_ref, hidden_lines_ref, head_sums_ref, normed_ref, proj_ref, *refs, count, share,
    hidden_share,
):
    token_refs = refs[:count]
    out_ref, acc_ref, unit_acc, col_acc = refs[-4:]
    step = pl.program_id(0)

    @pl.when(step == 0)
    def _():
        acc_ref[...] = jnp.zeros_like(acc_ref)
        unit_acc[...] = jnp.zeros_like(unit_acc)
        col_acc[...] = jnp.zeros_like(col_acc)

    proj = jnp.concatenate([proj_ref[s] for s in range(count)], axis=0)
    normed = jnp.concatenate([normed_ref[s] for s in range(count)], axis=0)
    unit = jnp.concatenate([unit_norm(r[...].astype(f32))[0].astype(bf16) for r in token_refs], axis=0)
    acc_ref[...] += dot_tn(normed, proj)
    unit_acc[...] += dot_tn(unit, proj)
    col_acc[...] += fold(proj.astype(f32))

    @pl.when(step == pl.num_programs(0) - 1)
    def _():
        weight = weight_ref[...].astype(f32)
        width, three = weight.shape
        devices = out_ref.shape[0]
        lane = lax.broadcasted_iota(jnp.int32, (width, 128), 1)
        gain = row_sum(weight * unit_acc[...])
        offset = row_sum(weight * jnp.sum(col_acc[...], axis=0, keepdims=True))
        norm_lines = jnp.transpose(jnp.where(lane == 0, gain, jnp.where(lane == 1, offset, 0.0)))[:8]
        low = pack_lines(lines_ref[0:8] + norm_lines, share, 0, devices)
        head_width = three // 3
        heads = jnp.concatenate(
            [jnp.zeros((2, head_width), f32), head_sums_ref[...], jnp.zeros((4, head_width), f32)], axis=0
        )
        low = low + pack_lines(heads, share, place_ref[1], devices)
        high = pack_lines(lines_ref[8:16], share, 0, devices)
        high = high + pack_lines(hidden_lines_ref[...], hidden_share, place_ref[0], devices)
        lines = jnp.concatenate([low, high, jnp.zeros((devices, 8, three - 256), f32)], axis=2)
        block = share_block(share)
        for i in range(devices):
            rows_i = acc_ref[i * share : (i + 1) * share, :]
            tail = [jnp.zeros((block - share - 8, three), f32)] if block > share + 8 else []
            out_ref[i] = jnp.concatenate([rows_i, lines[i], *tail], axis=0).astype(bf16)


def share_block(share):
    return -(-(-(-share // 8) * 8 + 8) // 16) * 16


def finish_kernel(packed_ref, out_ref, lines_ref, *, count, share, width):
    devices, _, three = packed_ref.shape
    head_width = three // 3
    total = 0.0
    for f in range(count):
        piece = packed_ref[f].astype(f32)
        for i in range(f + count, devices, count):
            piece = piece + packed_ref[i].astype(f32)
        total = total + piece[share : share + 8]
        size = min(head_width, width - f * head_width)
        for part in range(3):
            if size > 0:
                out_ref[:, part * width + f * head_width : part * width + f * head_width + size] = piece[
                    :share, part * head_width : part * head_width + size
                ]
    lines_ref[...] = total


def body(
    row_size,
    ffn_size,
    tokens,
    seq_lengths,
    key_keep,
    pre_gain,
    pre_bias,
    qkv_weight,
    query_bias,
    value_bias,
    sub_gain,
    sub_bias,
    out_weight,
    out_bias,
    ffn_gain,
    ffn_bias,
    up_bias,
    hidden_gain,
    hidden_bias,
    down_bias,
    up_weight,
    down_weight,
    out_grad,
):
    ffn_index, row_index = lax.axis_index("ffn"), lax.axis_index("rows")
    devices = row_size * ffn_size
    row_count, width = tokens.shape
    pack_total = row_count * ffn_size
    head_count = width // HEAD_DIM
    heads = -(-head_count // ffn_size)
    head_width = heads * HEAD_DIM
    three = 3 * head_width
    padded = head_width * ffn_size
    extra = padded - width
    hidden_width = up_weight.shape[1]
    share, hidden_share = pre_gain.shape[0], up_bias.shape[0]
    share_rows = share_block(share)
    owners = [slot_owner(p, ffn_index, ffn_size) for p in range(ffn_size)]
    owner_row = jnp.stack(owners).astype(jnp.int32)
    slots = range(ffn_size)
    pairs = [(i, i + 1) for i in range(0, ffn_size, 2)]
    steps = row_count // BLOCK

    thirds = jnp.pad(qkv_weight.reshape(share, 3, width), ((0, 0), (0, 0), (0, extra)))
    pieces = thirds.reshape(share, 3, ffn_size, head_width).transpose(2, 0, 1, 3)
    pieces = pieces.reshape(ffn_size, share, three)
    lines = [
        pre_gain, pre_bias, query_bias, value_bias, sub_gain, sub_bias, out_bias, ffn_gain, ffn_bias, down_bias,
        up_bias, hidden_gain, hidden_bias,
    ]
    lines = jnp.stack([jnp.pad(v, (0, 128 - v.shape[0])) for v in lines])
    lines = jnp.concatenate([lines[:8], jnp.pad(lines[8:], ((0, 3), (0, 0)))], axis=1)
    share_eight = -(-share // 8) * 8
    lines = jnp.pad(lines, ((share_eight - share, share_rows - share_eight - 8), (0, three - 256)))
    out_flat = share * width // three
    lines = jnp.concatenate([lines, out_weight.reshape(out_flat, three)], axis=0)
    pieces = jnp.concatenate([pieces, jnp.broadcast_to(lines, (ffn_size,) + lines.shape)], axis=1)
    pieces = in_order([pieces[i] for i in slots], ffn_index, ffn_size)
    pieces = jnp.stack(in_order(exchange_slots(pieces, ffn_size), ffn_index, ffn_size))
    if ffn_size == 4:
        tokens_across = swap(after(tokens, pieces), 2)
        token_slots = [tokens, swap(tokens, 1), tokens_across, swap(tokens_across, 1)]
    else:
        token_slots = gather_slots(tokens, ffn_size)
    out_rows = pieces[:, share_rows:].reshape(ffn_size * share, width)
    half = width // 2
    left = jnp.concatenate([up_weight, out_rows[:, :half]], axis=1)
    right = jnp.concatenate([down_weight.T, out_rows[:, half:]], axis=1)
    gathered = pieces[:, :share_rows].reshape(ffn_size * share_rows, three)
    special = ffn_size == 4 and row_size == 8
    if special:
        gathered = row_step(gathered, 4, row_index)
        right = row_step(right, 1, row_index)
        gathered = row_step(gathered, 2, row_index, 1)
        left = row_step(after(left, tokens_across), 4, row_index)
        gathered = gathered.reshape(4, ffn_size, share_rows, three)
        gathered_across = swap_rows(gathered, 1)
        halves = [gathered_across]
    else:
        gathered, left, right = [lax.all_gather(v, "rows", axis=0, tiled=False) for v in (gathered, left, right)]
        halves = []
    if not halves:
        gathered = gathered.reshape(devices, share_rows, three)
    place_row = jnp.stack([ffn_index * hidden_width, ffn_index * head_width, row_index & 1]).astype(jnp.int32)
    qkv_own, wide, hidden_all, bias_rows = call(
        functools.partial(
            unpack_kernel, share=share, hidden_share=hidden_share, line_at=share_eight, halves=bool(halves)
        ),
        1,
        [(place_row, SMEM), *[(g, fixed(*g.shape)) for g in [gathered] + halves]],
        [
            ((width, three), bf16, fixed(width, three)),
            ((16, width), f32, fixed(16, width)),
            ((16, hidden_width), f32, fixed(16, hidden_width)),
            ((8, three), f32, fixed(8, three)),
        ],
        "unpack",
        devices * 64 * width * 16,
        [pltpu.VMEM((devices, 8, 256), f32)],
    )
    if share % 8:
        qkv_own = gathered[:, :share, :].reshape(width, three)
    hidden_vectors = jnp.pad(hidden_all[10:13], ((0, 5), (0, 0)))
    middle_vectors = jnp.pad(wide[6:9], ((0, 5), (0, 0)))
    sub_rows = jnp.pad(
        jnp.concatenate([wide[4:6], jnp.ones((1, width), f32)], axis=0), ((0, 5), (0, extra))
    )
    sub_rows = sub_rows.reshape(8, ffn_size, head_width).transpose(1, 0, 2)
    if ffn_size == 4:
        grad_low = after(out_grad, tokens_across).astype(bf16)
        grad_across = swap(grad_low, 2)
        grad_slots = [grad_low, swap(grad_low, 1), grad_across, swap(grad_across, 1)]
        early = [grad_across]
    else:
        early = []
        grad_slots = gather_slots(out_grad.astype(bf16), ffn_size)

    block_row = pl.BlockSpec((BLOCK, width), lambda i: (i, 0))
    proj, normed_low = call(
        functools.partial(front_kernel, count=ffn_size),
        steps,
        [(qkv_own, fixed(width, three)), (bias_rows, fixed(8, three)), (wide, fixed(16, width))]
        + [(t, block_row) for t in token_slots],
        [
            ((ffn_size, row_count, three), bf16, pl.BlockSpec((ffn_size, BLOCK, three), lambda i: (0, i, 0))),
            ((ffn_size, row_count, width), bf16, pl.BlockSpec((ffn_size, BLOCK, width), lambda i: (0, i, 0))),
        ],
        "front",
        2 * pack_total * width * three,
    )
    if special:
        left = row_step(left, 2, row_index, 1, wait=proj)
        right = row_step(after(right, gathered_across), 4, row_index, wait=proj)
        early += [left, right]
    proj, normed_low = proj.reshape(pack_total, three), normed_low.reshape(pack_total, width)

    bounds, running = [], jnp.int32(0)
    for i in range(seq_lengths.shape[1] - 1):
        running = running + seq_lengths[0, i]
        bounds.append(running)
    bounds = jnp.stack(bounds)
    firsts = jnp.arange(pack_total // BLOCK, dtype=jnp.int32) * BLOCK
    block_owner = firsts // row_count
    place = (block_owner ^ ffn_index if ffn_size == 4 else block_owner) * row_count + firsts % row_count
    keep = key_keep.reshape(pack_total // BLOCK, BLOCK)
    mixed_own, lse = attend_forward(place, bounds, proj, keep, heads, early)

    if special:
        left = row_step(left, 1, row_index, 2, wait=lse)
        right = row_step(right, 2, row_index, 1, wait=lse)
    left, right = left.reshape(width, -1), right.reshape(width, -1)
    up_in = (left, columns(width, hidden_width, 0))
    down_in = (right, columns(width, hidden_width, 0))
    if extra:
        out_in = [
            (jnp.pad(v[:, hidden_width:], ((0, extra), (0, 0))), columns(padded, half, 0)) for v in (left, right)
        ]
    else:
        out_in = [(v, columns(width, half, hidden_width // half)) for v in (left, right)]

    mixed_slots = exchange_slots(
        [mixed_own[p * row_count : (p + 1) * row_count] for p in slots], ffn_size
    )
    block_piece = pl.BlockSpec((BLOCK, head_width), lambda i: (i, 0))
    block_pieces = pl.BlockSpec((ffn_size, BLOCK, head_width), lambda i: (0, i, 0))
    middle_in = [*out_in, (sub_rows, fixed(ffn_size, 8, head_width)), (middle_vectors, fixed(8, width))]
    sub_low, middle, ffn_low = call(
        functools.partial(middle_forward_kernel, count=ffn_size, padded=bool(extra)),
        steps,
        [(owner_row, SMEM), (tokens, block_row), *middle_in, *[(m, block_piece) for m in mixed_slots]]
        + [(grad_slots[-1], ANY)],
        [
            ((ffn_size, row_count, head_width), bf16, block_pieces),
            ((row_count, width), f32, block_row),
            ((row_count, width), bf16, block_row),
        ],
        "middle_forward",
        2 * row_count * padded * width,
    )

    fine = BLOCK // 2
    block_fine = pl.BlockSpec((fine, width), lambda i: (i, 0))
    block_pair = pl.BlockSpec((2, fine, hidden_width), lambda i: (0, i, 0))
    block_pair_row = pl.BlockSpec((2, fine, width), lambda i: (0, i, 0))
    block_stat = pl.BlockSpec((2, 8, fine), lambda i: (0, 0, i))
    block_four = pl.BlockSpec((2, 4, fine), lambda i: (0, 0, i))
    hidden_in = (hidden_vectors, fixed(8, hidden_width))
    pair_shape = (2, row_count, hidden_width)

    def up_pair(rows, grads, waits):
        return call(
            functools.partial(up_kernel, count=2, waits=len(waits)),
            2 * steps,
            [up_in, down_in, hidden_in, *[(r, block_fine) for r in rows], *[(g, block_fine) for g in grads]]
            + [(w, ANY) for w in waits],
            [
                (pair_shape, f32, block_pair),
                (pair_shape, bf16, block_pair),
                (pair_shape, bf16, block_pair),
                ((2, 8, row_count), f32, block_stat),
                ((8, hidden_width), f32, fixed(8, hidden_width)),
            ],
            "up",
            8 * row_count * width * hidden_width,
            [
                pltpu.VMEM((2, fine, hidden_width), f32),
                pltpu.VMEM((2, fine, hidden_width), f32),
                pltpu.VMEM((2, 4, fine, 128), f32),
            ],
            4 * row_count * hidden_width,
        )

    if ffn_size == 4:
        across, beside = swap(ffn_low, 2), swap(ffn_low, 1)
        ups = [up_pair([ffn_low, beside], grad_slots[:2], [])]
        slanted = swap(after(across, ups[0][3]), 1)
        row_slots = [ffn_low, beside, across, slanted]
        ups.append(up_pair([across, slanted], grad_slots[2:], [ups[0][3]]))
    else:
        row_slots = gather_slots(ffn_low, ffn_size)
        ups = [up_pair(row_slots[i : i + 2], grad_slots[i : i + 2], []) for i, _ in pairs]
    stats = sum_slots([u[3] for u in ups], ffn_size)
    backs, wait_for = [None] * len(pairs), []
    for k in reversed(range(len(pairs))):
        act, slope, back = ups[k][:3]
        backs[k] = call(
            functools.partial(back_kernel, count=2),
            2 * steps,
            [up_in, hidden_in, (act, block_pair), (slope, block_pair), (back, block_pair)]
            + [(stats[2 * k : 2 * k + 2], block_four), *[(w, ANY) for w in wait_for]],
            [
                (pair_shape, bf16, block_pair),
                (pair_shape, bf16, block_pair),
                ((row_count, width), bf16, block_fine),
                ((row_count, width), bf16, block_fine),
                ((2, 8, hidden_width), f32, fixed(2, 8, hidden_width)),
            ],
            "back",
            4 * row_count * width * hidden_width,
            [pltpu.VMEM((2, 4, fine, 128), f32)],
        )
        wait_for = [backs[k][3]]

    def reduce_pairs(near, far, wait=None):
        passed = swap(far[1], 1)
        sent = far[0].astype(f32) + passed.astype(f32)
        sent = (sent if wait is None else after(sent, wait)).astype(bf16)
        return [near[0], swap(near[1], 1), swap(sent, 2)], sent

    def scatter_pairs(parts):
        return [lax.psum_scatter(jnp.stack(parts), "ffn", scatter_dimension=0, tiled=True)[0]]

    if ffn_size == 4:
        in_terms, _ = reduce_pairs(backs[0][2:4], backs[1][2:4])
    else:
        in_terms = scatter_pairs([v for b in backs for v in b[2:4]])
    block_quarter = pl.BlockSpec((BLOCK // 2, width), lambda i: (i, 0))
    block_pair_quarter = pl.BlockSpec((2, BLOCK // 2, hidden_width), lambda i: (0, i, 0))
    weight_part, *down_parts = call(
        functools.partial(ffn_grad_kernel, count=ffn_size, pairs=len(pairs)),
        2 * steps,
        [down_in, *[(r, block_quarter) for r in row_slots], *[(g, block_quarter) for g in grad_slots]]
        + [(b[0], block_pair_quarter) for b in backs]
        + [(b[1], block_pair_quarter) for b in backs],
        [
            ((width, 2 * hidden_width), bf16, fixed(width, 2 * hidden_width)),
        ]
        + [((row_count, width), bf16, block_quarter)] * ffn_size,
        "ffn_grads",
        6 * pack_total * width * hidden_width,
        [pltpu.VMEM((width, hidden_width), f32), pltpu.VMEM((width, hidden_width), f32)],
    )
    if special:
        weight_part = weight_part.reshape(2, 2, 2, width // row_size, 2 * hidden_width)
    else:
        ties = []
        weight_grad = lax.psum_scatter(weight_part, "rows", scatter_dimension=0, tiled=True).astype(f32)

    grad_middle, middle_low, *head_low, middle_sums, sub_sums = call(
        functools.partial(
            middle_backward_kernel, count=ffn_size, addends=len(in_terms), padded=bool(extra)
        ),
        steps,
        [(owner_row, SMEM), (out_grad, block_row), (middle, block_row), *middle_in]
        + [(m, block_piece) for m in mixed_slots]
        + [(t, block_row) for t in in_terms],
        [
            ((row_count, width), f32, block_row),
            ((row_count, width), bf16, block_row),
            *[((row_count, head_width), bf16, block_piece)] * ffn_size,
            ((8, width), f32, fixed(8, width)),
            ((ffn_size, 8, head_width), f32, fixed(ffn_size, 8, head_width)),
        ],
        "middle_backward",
        2 * row_count * padded * width,
    )
    grad_own = jnp.concatenate(exchange_slots(head_low, ffn_size), axis=0)
    out_shape = (row_size * share, width) if special else (padded, width)
    out_parts = call(
        functools.partial(out_grad_kernel, count=ffn_size, share=share, in_slots=special),
        1,
        [(owner_row, SMEM), (sub_low, fixed(ffn_size, row_count, head_width)), (middle_low, fixed(row_count, width))],
        [(out_shape, bf16, fixed(*out_shape))] * (ffn_size if special else 1),
        "out_grads",
        2 * row_count * padded * width,
        [pltpu.VMEM((head_width, width), f32)],
    )
    if special:
        weight_sent, weight_kept = row_split(weight_part, 1, row_index)
        weight_across = after(swap_rows(weight_sent, 1), middle_low)
        weight_sent, weight_kept = row_split(weight_kept + weight_across.astype(f32), 2, row_index)
        ties = [weight_sent]
        weight_across = swap_rows(weight_sent, 2)
        out_terms = exchange_slots([after(v, grad_own) if i > 1 else v for i, v in enumerate(out_parts)], ffn_size)
    else:
        out_weight_own = lax.psum_scatter(
            out_parts[0][:width], ("rows", "ffn"), scatter_dimension=0, tiled=True
        ).astype(f32)

    if ffn_size == 4:
        down_terms, layer_sent = reduce_pairs(down_parts[:2], down_parts[2:], grad_own)
        ties.append(layer_sent)
    else:
        down_terms = scatter_pairs(down_parts)
    layer_out = (middle + sum(t.astype(f32) for t in down_terms) + wide[9]).astype(bf16)

    sub_flat = sub_sums[:, :2].transpose(1, 0, 2).reshape(2, padded)[:, :width]
    lines = jnp.concatenate(
        [jnp.zeros((4, width), f32), sub_flat, middle_sums[:4], jnp.zeros((6, width), f32)], axis=0
    )
    back_sums = jnp.sum(sum(b[4] for b in backs), axis=1)
    hidden_lines = jnp.concatenate(
        [
            jnp.zeros((2, hidden_width), f32),
            back_sums,
            jnp.sum(sum(u[4] for u in ups), axis=0)[None],
            jnp.zeros((3, hidden_width), f32),
        ],
        axis=0,
    )
    ties += [lines, hidden_lines]

    grad_proj, head_bias_grads = attend_backward(place, bounds, proj, keep, mixed_own, grad_own, lse, heads, ties)

    def in_pair(k, waits):
        proj_specs = [
            pl.BlockSpec((BLOCK, three), lambda i, p=p: (p * steps + i, 0)) for p in pairs[k]
        ]
        return call(
            functools.partial(in_grad_kernel, count=2),
            steps,
            [(qkv_own, fixed(width, three)), *[(grad_proj, spec) for spec in proj_specs]]
            + [(w, ANY) for w in waits],
            [((row_count, width), bf16, block_row)] * 2,
            "in_grads",
            4 * row_count * width * three,
        )

    if special:
        weight_sent, weight_kept = row_split(weight_kept + after(weight_across, grad_proj).astype(f32), 4, row_index)
        weight_across = swap_rows(weight_sent, 4)
        out_sum = sum(after(v, grad_proj).astype(f32) for v in out_terms).reshape(2, 2, 2, share, width)
        out_sent, out_kept = row_split(out_sum, 1, row_index)
        out_across = swap_rows(out_sent, 1)
        far = in_pair(1, [down_terms[2], out_sent])
        sent = (far[0].astype(f32) + swap(far[1], 1).astype(f32)).astype(bf16)
        across = swap(sent, 2)
        out_sent, out_kept = row_split(out_kept + after(out_across, far[0]).astype(f32), 2, row_index)
        out_across = swap_rows(out_sent, 2)
        late = [weight_sent, out_sent, sent]
    else:
        late = []
    eighth = row_count // 4
    (packed,) = call(
        functools.partial(
            qkv_grad_kernel, count=ffn_size, share=share, hidden_share=hidden_share
        ),
        4,
        [
            (place_row, SMEM),
            (qkv_own, fixed(width, three)),
            (lines, fixed(16, width)),
            (hidden_lines, fixed(8, hidden_width)),
            (head_bias_grads, fixed(2, head_width)),
            (
                normed_low.reshape(ffn_size, row_count, width),
                pl.BlockSpec((ffn_size, eighth, width), lambda i: (0, i, 0)),
            ),
            (
                grad_proj.reshape(ffn_size, row_count, three),
                pl.BlockSpec((ffn_size, eighth, three), lambda i: (0, i, 0)),
            ),
            *[(t, pl.BlockSpec((eighth, width), lambda i: (i, 0))) for t in token_slots],
            *[(v, ANY) for v in late],
        ],
        [((devices, share_rows, three), bf16, fixed(devices, share_rows, three))],
        "qkv_grads",
        4 * pack_total * width * three,
        [pltpu.VMEM((width, three), f32), pltpu.VMEM((width, three), f32), pltpu.VMEM((8, three), f32)],
    )
    if special:
        near = in_pair(0, [packed, across])
        in_terms = [near[0], swap(near[1], 1), across]
        weight_grad = weight_kept + after(weight_across, near[0]).astype(f32)
        out_sent, out_kept = row_split(out_kept + after(out_across, packed).astype(f32), 4, row_index)
        out_weight_own = (out_kept + after(swap_rows(out_sent, 4), near[0]).astype(f32)).reshape(share, width)
    else:
        in_terms = scatter_pairs([v for k in range(len(pairs)) for v in in_pair(k, [])])
    packed = lax.all_to_all(packed, ("rows", "ffn"), split_axis=0, concat_axis=0, tiled=True)
    qkv_weight_grad, line_own = call(
        functools.partial(finish_kernel, count=ffn_size, share=share, width=width),
        1,
        [(packed, fixed(*packed.shape))],
        [((share, 3 * width), f32, fixed(share, 3 * width)), ((8, three), f32, fixed(8, three))],
        "finish",
        devices * share * three,
    )

    weight_grad = weight_grad.reshape(-1, 2 * hidden_width)
    up_weight_grad, down_weight_grad = weight_grad[:, :hidden_width], weight_grad[:, hidden_width:].T

    unit_own, inverse_own = unit_norm(tokens.astype(f32))
    in_scaled = sum(t.astype(f32) for t in in_terms) * wide[0]
    in_adjusted = (
        in_scaled
        - jnp.mean(in_scaled, axis=-1, keepdims=True)
        - unit_own * jnp.mean(in_scaled * unit_own, axis=-1, keepdims=True)
    )
    tokens_grad = grad_middle + in_adjusted * inverse_own

    vectors = [line_own[i, :share] for i in range(8)] + [line_own[i, 128 : 128 + share] for i in range(2)]
    small = vectors
    hidden_small = [line_own[i, 128 : 128 + hidden_share] for i in range(2, 5)]
    return (
        layer_out,
        tokens_grad,
        small[0],
        small[1],
        qkv_weight_grad,
        small[2],
        small[3],
        small[4],
        small[5],
        out_weight_own,
        small[6],
        small[7],
        small[8],
        hidden_small[0],
        hidden_small[1],
        hidden_small[2],
        small[9],
        up_weight_grad,
        down_weight_grad,
    )


def solution(mesh):
    flat, matrix = P(("rows", "ffn")), P(("rows", "ffn"), None)
    in_specs = (
        matrix, P("rows", None), P("rows"), flat, flat, matrix, flat, flat, flat, flat, matrix, flat, flat, flat,
        flat, flat, flat, flat, P("rows", "ffn"), P("ffn", "rows"), matrix,
    )
    out_specs = (
        matrix, matrix, flat, flat, matrix, flat, flat, flat, flat, matrix, flat, flat, flat, flat, flat, flat, flat,
        P("rows", "ffn"), P("ffn", "rows"),
    )
    return jax.shard_map(
        functools.partial(body, mesh.shape["rows"], mesh.shape["ffn"]),
        mesh=mesh,
        in_specs=in_specs,
        out_specs=out_specs,
        check_vma=False,
    )
```

```python
import functools

import jax
import jax.numpy as jnp
from jax import lax
from jax.experimental import pallas as pl
from jax.experimental.pallas import tpu as pltpu
from jax.sharding import PartitionSpec as P

HEAD_DIM = 64
FF = 3072
BLOCK = 256
SMALL = 20

eps = 1e-05
neg_big = -1e30
score_scale = 0.125
root_half = 0.7071067811865476
inv_root_tau = 0.3989422804014327

f32 = jnp.float32
bf16 = jnp.bfloat16


def swap(values, flip):
    return lax.ppermute(values, "ffn", [(i, i ^ flip) for i in range(4)])


def swap_rows(values, flip):
    return lax.ppermute(values, "rows", [(i, i ^ flip) for i in range(8)])


def slot_owner(slot, ffn_index, ffn_size):
    return ffn_index ^ slot if ffn_size == 4 else jnp.int32(slot)


def gather_slots(values, ffn_size):
    if ffn_size != 4:
        whole = lax.all_gather(values, "ffn", axis=0, tiled=False)
        return [whole[i] for i in range(ffn_size)]
    across = swap(values, 2)
    beside = swap(values, 1)
    return [values, beside, across, swap(across, 1)]


def exchange_slots(pieces, ffn_size):
    if ffn_size != 4:
        whole = lax.all_to_all(jnp.stack(pieces), "ffn", split_axis=0, concat_axis=0, tiled=True)
        return [whole[i] for i in range(ffn_size)]
    across = swap(pieces[2], 2)
    slanted = swap(pieces[3], 3)
    beside = swap(pieces[1], 1)
    return [pieces[0], beside, across, slanted]


def in_order(slots, ffn_index, ffn_size):
    if ffn_size != 4:
        return slots
    odd, high = (ffn_index & 1) > 0, (ffn_index & 2) > 0
    low = [jnp.where(odd, slots[p ^ 1], slots[p]) for p in range(4)]
    return [jnp.where(high, low[p ^ 2], low[p]) for p in range(4)]


def sum_slots(pairs, ffn_size):
    values = jnp.concatenate(pairs, axis=0)[:, :4, :]
    if ffn_size != 4:
        return lax.psum(values, "ffn")
    beside = swap(values, 1)
    values = values + jnp.stack([beside[1], beside[0], beside[3], beside[2]])
    across = swap(values, 2)
    return values + jnp.stack([across[2], across[3], across[0], across[1]])


ROW_AXIS = {4: 0, 2: 1, 1: 2}


def row_bit(flip, row_index):
    return (row_index >> (2 - ROW_AXIS[flip])) & 1


def row_step(whole, flip, row_index, outer=0, wait=None):
    bit = row_bit(flip, row_index)
    other = swap_rows(whole, flip)
    if wait is not None:
        other = after(other, wait)
    return jnp.stack([jnp.where(bit > 0, other, whole), jnp.where(bit > 0, whole, other)], axis=outer)


def row_split(whole, flip, row_index):
    axis, bit = ROW_AXIS[flip], row_bit(flip, row_index)
    sent = lax.dynamic_slice_in_dim(whole, 1 - bit, 1, axis).astype(bf16)
    return sent, lax.dynamic_slice_in_dim(whole, bit, 1, axis).astype(f32)


def split_add(whole, flip, row_index, wait):
    sent, kept = row_split(whole, flip, row_index)
    sent = after(sent, wait)
    return kept + swap_rows(sent, flip).astype(f32), sent


def row_halves(whole, flips, row_index, waits):
    sends = []
    for flip, wait in zip(flips, waits):
        sent, kept = row_split(whole, flip, row_index)
        sends.append(sent)
        other = swap_rows(sent, flip)
        whole = kept + (other if wait is None else after(other, wait)).astype(f32)
    return whole[0, 0, 0], sends


def after(values, other):
    first = lax.slice(other, (0,) * other.ndim, (1,) * other.ndim)
    first = first.reshape((1,) * values.ndim)
    return values + (first * 0).astype(values.dtype)


NT = (((1,), (1,)), ((), ()))


def dot_nt(a, b):
    return lax.dot_general(a, b, NT, preferred_element_type=f32)


def dot_nn(a, b):
    return jnp.dot(a, b, preferred_element_type=f32)


def start_row(first, bounds_ref, bound_count):
    places = first + lax.broadcasted_iota(jnp.int32, (1, BLOCK), 1)
    start = jnp.zeros((1, BLOCK), jnp.int32)
    for i in range(bound_count):
        bound = bounds_ref[i]
        start = jnp.where(places >= bound, jnp.maximum(start, bound), start)
    return places, start


def first_block(first, bounds_ref, bound_count):
    start = jnp.int32(0)
    for i in range(bound_count):
        bound = bounds_ref[i]
        start = jnp.where(first >= bound, jnp.maximum(start, bound), start)
    return start // BLOCK


def load_keys(keep_ref, limit_ref, blocks):
    for j in range(blocks):
        row = keep_ref[j : j + 1, :]
        places = j * BLOCK + lax.broadcasted_iota(jnp.int32, (1, BLOCK), 1)
        limits = jnp.where(row > 0, places, 1 << 24).astype(f32)
        column = jnp.transpose(jnp.broadcast_to(limits, (128, BLOCK)))
        limit_ref[j * BLOCK : (j + 1) * BLOCK, :] = column


def block_bias(limit_ref, key_first, query_places, query_start):
    limit = limit_ref[pl.ds(key_first, BLOCK), :]
    limit = jnp.concatenate([limit] * (BLOCK // 128), axis=1)
    key_places = key_first + lax.broadcasted_iota(jnp.int32, (BLOCK, BLOCK), 0)
    before = (limit < query_places.astype(f32)) & (key_places >= query_start)
    return jnp.where(before | (key_places == query_places), 0.0, neg_big)


def forward_kernel(
    place_ref, bounds_ref, proj_ref, keep_ref, *refs, heads, bound_count
):
    out_ref, lse_ref, limit_ref, value_t_ref = refs[-4:]
    total = proj_ref.shape[0]
    blocks = total // BLOCK
    width = heads * HEAD_DIM
    load_keys(keep_ref, limit_ref, blocks)
    for j in range(blocks):
        rows = slice(j * BLOCK, (j + 1) * BLOCK)
        value_t_ref[:, rows] = jnp.transpose(proj_ref[rows, 2 * width :].astype(f32)).astype(bf16)

    def query_step(qi, _):
        query_first = pl.multiple_of(qi * BLOCK, BLOCK)
        query_at = pl.multiple_of(place_ref[qi], BLOCK)
        places, starts = start_row(query_first, bounds_ref, bound_count)
        queries = proj_ref[pl.ds(query_at, BLOCK), :width] * jnp.asarray(score_scale, bf16)

        def block_scores(kj):
            key_first = pl.multiple_of(kj * BLOCK, BLOCK)
            key_at = pl.multiple_of(place_ref[kj], BLOCK)
            bias = block_bias(limit_ref, key_first, places, starts)
            keys = proj_ref[pl.ds(key_at, BLOCK), width : 2 * width]
            heads_cols = [slice(h * HEAD_DIM, (h + 1) * HEAD_DIM) for h in range(heads)]
            return key_at, [dot_nt(keys[:, cols], queries[:, cols]) + bias for cols in heads_cols]

        def top_step(kj, tops):
            _, scores = block_scores(kj)
            return tuple(jnp.maximum(t, jnp.max(v, axis=0, keepdims=True)) for t, v in zip(tops, scores))

        first = first_block(query_first, bounds_ref, bound_count)
        tops = lax.fori_loop(first, qi + 1, top_step, (jnp.full((1, BLOCK), neg_big, f32),) * heads)

        def value_step(kj, carry):
            key_at, scores = block_scores(kj)
            values_t = value_t_ref[:, pl.ds(key_at, BLOCK)]
            out = []
            for h in range(heads):
                cols = slice(h * HEAD_DIM, (h + 1) * HEAD_DIM)
                weights = jnp.exp(scores[h] - tops[h])
                total_sum, mixed = carry[h]
                out.append(
                    (
                        total_sum + jnp.sum(weights, axis=0, keepdims=True),
                        mixed + dot_nn(values_t[cols, :], weights.astype(bf16)),
                    )
                )
            return tuple(out)

        empty = (jnp.zeros((1, BLOCK), f32), jnp.zeros((HEAD_DIM, BLOCK), f32))
        done = lax.fori_loop(first, qi + 1, value_step, (empty,) * heads)
        mixed_t = jnp.concatenate([mixed / total_sum for total_sum, mixed in done], axis=0)
        out_ref[pl.ds(query_at, BLOCK), :] = jnp.transpose(mixed_t).astype(out_ref.dtype)
        for h in range(heads):
            lse_ref[h : h + 1, pl.ds(query_first, BLOCK)] = tops[h] + jnp.log(done[h][0])
        return 0

    lax.fori_loop(0, blocks, query_step, 0)


def backward_kernel(
    place_ref, bounds_ref, proj_ref, keep_ref, mixed_ref, grad_ref, lse_ref, *refs, heads, bound_count
):
    out_ref, bias_ref, limit_ref, key_t_ref, key_acc, value_acc = refs[-6:]
    total = proj_ref.shape[0]
    blocks = total // BLOCK
    width = heads * HEAD_DIM
    load_keys(keep_ref, limit_ref, blocks)
    for j in range(blocks):
        rows = slice(j * BLOCK, (j + 1) * BLOCK)
        key_t_ref[:, rows] = jnp.transpose(proj_ref[rows, width : 2 * width].astype(f32)).astype(bf16)
    key_acc[...] = jnp.zeros_like(key_acc)
    value_acc[...] = jnp.zeros_like(value_acc)
    bias_ref[...] = jnp.zeros_like(bias_ref)

    def query_step(qi, _):
        query_first = pl.multiple_of(qi * BLOCK, BLOCK)
        query_at = pl.multiple_of(place_ref[qi], BLOCK)
        query_rows = pl.ds(query_at, BLOCK)
        places, starts = start_row(query_first, bounds_ref, bound_count)
        queries = proj_ref[query_rows, :width] * jnp.asarray(score_scale, bf16)
        grads = grad_ref[query_rows, :]
        product_t = jnp.transpose(grads.astype(f32) * mixed_ref[query_rows, :].astype(f32))
        lse = [lse_ref[h : h + 1, pl.ds(query_first, BLOCK)] for h in range(heads)]
        delta = [
            jnp.sum(product_t[h * HEAD_DIM : (h + 1) * HEAD_DIM, :], axis=0, keepdims=True) for h in range(heads)
        ]

        def key_step(kj, carry):
            key_first = pl.multiple_of(kj * BLOCK, BLOCK)
            key_rows = pl.ds(pl.multiple_of(place_ref[kj], BLOCK), BLOCK)
            bias = block_bias(limit_ref, key_first, places, starts)
            keys = proj_ref[key_rows, width : 2 * width]
            values = proj_ref[key_rows, 2 * width :]
            keys_t = key_t_ref[:, key_rows]
            out, key_parts, value_parts = [], [], []
            for h in range(heads):
                cols = slice(h * HEAD_DIM, (h + 1) * HEAD_DIM)
                scores = dot_nt(keys[:, cols], queries[:, cols]) + bias
                probs = jnp.exp(scores - lse[h])
                grad_probs = dot_nt(values[:, cols], grads[:, cols])
                grad_scores = (probs * (grad_probs - delta[h])).astype(bf16)
                value_parts.append(dot_nn(probs.astype(bf16), grads[:, cols]))
                key_parts.append(dot_nn(grad_scores, queries[:, cols]))
                out.append(carry[h] + dot_nn(keys_t[cols, :], grad_scores))
            key_acc[key_rows, :] += jnp.concatenate(key_parts, axis=1)
            value_acc[key_rows, :] += jnp.concatenate(value_parts, axis=1)
            return tuple(out)

        zero = jnp.zeros((HEAD_DIM, BLOCK), f32)
        done = lax.fori_loop(first_block(query_first, bounds_ref, bound_count), qi + 1, key_step, (zero,) * heads)
        grad_query = jnp.transpose(jnp.concatenate(done, axis=0)) * score_scale
        bias_ref[0:1, :] += jnp.sum(grad_query, axis=0, keepdims=True)
        out_ref[query_rows, :width] = grad_query.astype(bf16)
        return 0

    lax.fori_loop(0, blocks, query_step, 0)
    bias_ref[1:2, :] = jnp.sum(value_acc[...], axis=0, keepdims=True)
    out_ref[:, width : 2 * width] = key_acc[...].astype(bf16)
    out_ref[:, 2 * width :] = value_acc[...].astype(bf16)


ANY = pl.BlockSpec(memory_space=pl.ANY)
SMEM = pl.BlockSpec(memory_space=pltpu.SMEM)
VMEM = pl.BlockSpec(memory_space=pltpu.VMEM)


def attend_forward(place, bounds, proj, keep, heads, waits):
    total, width = proj.shape[0], heads * HEAD_DIM
    pairs = total * total // 6
    return pl.pallas_call(
        functools.partial(forward_kernel, heads=heads, bound_count=bounds.shape[0]),
        out_shape=(jax.ShapeDtypeStruct((total, width), bf16), jax.ShapeDtypeStruct((heads, total), f32)),
        in_specs=[SMEM, SMEM, VMEM, VMEM] + [ANY] * len(waits),
        out_specs=(VMEM, VMEM),
        scratch_shapes=[
            pltpu.VMEM((total, 128), f32),
            pltpu.VMEM((width, total), bf16),
        ],
        compiler_params=pltpu.CompilerParams(vmem_limit_bytes=40 << 20),
        cost_estimate=pl.CostEstimate(
            flops=16 * pairs * width // SMALL, bytes_accessed=1024, transcendentals=0
        ),
        name="attend_forward",
    )(place, bounds, proj, keep, *waits)


def attend_backward(place, bounds, proj, keep, mixed, grads, lse, heads, waits):
    total, width = proj.shape[0], heads * HEAD_DIM
    pairs = total * total // 6
    return pl.pallas_call(
        functools.partial(backward_kernel, heads=heads, bound_count=bounds.shape[0]),
        out_shape=(jax.ShapeDtypeStruct((total, 3 * width), bf16), jax.ShapeDtypeStruct((2, width), f32)),
        in_specs=[SMEM, SMEM, VMEM, VMEM, VMEM, VMEM, VMEM] + [ANY] * len(waits),
        out_specs=(VMEM, VMEM),
        scratch_shapes=[
            pltpu.VMEM((total, 128), f32),
            pltpu.VMEM((width, total), bf16),
            pltpu.VMEM((total, width), f32),
            pltpu.VMEM((total, width), f32),
        ],
        compiler_params=pltpu.CompilerParams(vmem_limit_bytes=50 << 20),
        cost_estimate=pl.CostEstimate(
            flops=40 * pairs * width // SMALL, bytes_accessed=1024, transcendentals=0
        ),
        name="attend_backward",
    )(place, bounds, proj, keep, mixed, grads, lse, *waits)


TN = (((0,), (0,)), ((), ()))
CHUNK = 16


def dot_tn(a, b):
    return lax.dot_general(a, b, TN, preferred_element_type=f32)


def fixed(*shape):
    return pl.BlockSpec(shape, lambda i: (0,) * len(shape))


def columns(rows, width, index):
    return pl.BlockSpec((rows, width), lambda i: (0, index))


def call(kernel, grid, inputs, outputs, name, flops, scratch=(), transcendentals=0):
    moved = sum(a.size * a.dtype.itemsize for a, spec in inputs if spec.memory_space is None)
    return pl.pallas_call(
        kernel,
        grid=(grid,),
        in_specs=[spec for _, spec in inputs],
        out_specs=tuple(spec for _, _, spec in outputs),
        out_shape=tuple(jax.ShapeDtypeStruct(shape, dtype) for shape, dtype, _ in outputs),
        scratch_shapes=list(scratch),
        compiler_params=pltpu.CompilerParams(
            vmem_limit_bytes=58 << 20, dimension_semantics=("arbitrary",)
        ),
        cost_estimate=pl.CostEstimate(
            flops=flops // SMALL, bytes_accessed=moved // SMALL, transcendentals=transcendentals // SMALL
        ),
        name=name,
    )(*[a for a, _ in inputs])


def row_sum(values):
    return jnp.sum(values, axis=-1, keepdims=True)


def fold(values):
    out = values[:8]
    for i in range(8, values.shape[0], 8):
        out = out + values[i : i + 8]
    return out


def unit_norm(values):
    center = values - jnp.mean(values, axis=-1, keepdims=True)
    inverse = lax.rsqrt(jnp.mean(center * center, axis=-1, keepdims=True) + eps)
    return center * inverse, inverse


def sub_norm(pieces, real, width):
    mean = sum(row_sum(p) for p in pieces) * (1.0 / width)
    centers = [p - mean for p in pieces]
    if real is not None:
        centers = [c * r for c, r in zip(centers, real)]
    inverse = lax.rsqrt(sum(row_sum(c * c) for c in centers) * (1.0 / width) + eps)
    return [c * inverse for c in centers], inverse


def sub_vectors(owner_ref, sub_ref, count, padded):
    rows = [sub_ref[owner_ref[p]] for p in range(count)]
    real = [r[2:3] for r in rows] if padded else None
    return [r[0:1] for r in rows], [r[1:2] for r in rows], real


def place_columns(share, width, first, rows):
    lane = lax.broadcasted_iota(jnp.int32, (128, width), 0)
    column = first + lax.broadcasted_iota(jnp.int32, (128, width), 1)
    matrix = jnp.where(lane == column % share, 1.0, 0.0).astype(bf16)
    device = lax.broadcasted_iota(jnp.int32, (rows, 1, width), 0)
    column = first + lax.broadcasted_iota(jnp.int32, (rows, 1, width), 2)
    return jnp.where(device == column // share, 1.0, 0.0), matrix


def unpack_kernel(place_ref, here_ref, *refs, share, hidden_share, line_at, halves):
    weight_ref, wide_ref, hidden_ref, bias_ref, lines_ref = refs[-5:]
    devices = lines_ref.shape[0]
    blocks = here_ref.shape[1]
    together = 2 if share % 16 else 1

    def block_of(i):
        if not halves:
            return here_ref[i].astype(f32)
        per = devices // 8
        row, own = i // per, i % per
        own_rows = here_ref[row // 2, own].astype(f32)
        other_rows = refs[0][row // 2, own].astype(f32)
        return jnp.where(place_ref[2] == row % 2, own_rows, other_rows)

    for i in range(0, devices, together):
        both = [block_of(i + j) for j in range(together)]
        for j in range(together):
            lines_ref[i + j] = both[j][line_at : line_at + 8, :256].astype(bf16).astype(f32)
        if share % 8 == 0:
            rows = jnp.concatenate([b[:share] for b in both], axis=0)
            weight_ref[i * share : (i + together) * share, :] = rows.astype(bf16)

    def spread(size, first, width):
        mine, matrix = place_columns(size, width, first, devices)
        out = []
        for part in range(2):
            lines = lines_ref[:, :, part * 128 : (part + 1) * 128].reshape(devices * 8, 128).astype(bf16)
            out.append(jnp.sum(dot_nn(lines, matrix).reshape(devices, 8, width) * mine, axis=0))
        return jnp.concatenate(out, axis=0)

    head_width = bias_ref.shape[1] // 3
    wide_ref[...] = spread(share, 0, wide_ref.shape[1])
    hidden_ref[...] = spread(hidden_share, place_ref[0], hidden_ref.shape[1])
    own = spread(share, place_ref[1], head_width)[:8]
    zero = jnp.zeros((1, head_width), f32)
    bias_ref[...] = jnp.broadcast_to(
        jnp.concatenate([own[2:3], zero, own[3:4]], axis=1), bias_ref.shape
    )


def pack_lines(values, share, first, devices):
    mine, matrix = place_columns(share, values.shape[1], first, devices)
    lines = (values[None] * mine).reshape(devices * 8, values.shape[1]).astype(bf16)
    return dot_nt(lines, matrix).reshape(devices, 8, 128)


def front_kernel(weight_ref, bias_ref, vec_ref, *refs, count):
    token_refs, (proj_ref, normed_ref) = refs[:count], refs[-2:]
    for s in range(count):
        unit, _ = unit_norm(token_refs[s][...].astype(f32))
        normed = (unit * vec_ref[0:1] + vec_ref[1:2]).astype(bf16)
        normed_ref[s] = normed
        proj_ref[s] = (dot_nn(normed, weight_ref[...]) + bias_ref[0:1]).astype(bf16)


def middle_forward_kernel(owner_ref, tokens_ref, left_ref, right_ref, sub_ref, vec_ref, *refs, count, padded):
    piece_refs, (low_ref, middle_ref, ffn_ref) = refs[:count], refs[-3:]
    head_width, width = low_ref.shape[2], middle_ref.shape[1]
    gains, offsets, real = sub_vectors(owner_ref, sub_ref, count, padded)
    units, _ = sub_norm([r[...].astype(f32) for r in piece_refs], real, width)
    middle = tokens_ref[...].astype(f32) + vec_ref[0:1]
    for p in range(count):
        low = (units[p] * gains[p] + offsets[p]).astype(bf16)
        low_ref[p] = low
        rows = pl.ds(pl.multiple_of(owner_ref[p] * head_width, head_width), head_width)
        middle = middle + dot_nn(low, jnp.concatenate([left_ref[rows, :], right_ref[rows, :]], axis=1))
    middle_ref[...] = middle
    unit, _ = unit_norm(middle)
    ffn_ref[...] = (unit * vec_ref[1:2] + vec_ref[2:3]).astype(bf16)


def middle_backward_kernel(
    owner_ref, out_grad_ref, middle_ref, left_ref, right_ref, sub_ref, vec_ref, *refs, count, addends, padded
):
    piece_refs, add_refs = refs[:count], refs[count : count + addends]
    grad_ref, grad_low_ref, *head_refs, sums_ref, sub_sums_ref = refs[count + addends :]
    head_width, width = head_refs[0].shape[1], middle_ref.shape[1]

    @pl.when(pl.program_id(0) == 0)
    def _():
        sums_ref[...] = jnp.zeros_like(sums_ref)
        sub_sums_ref[...] = jnp.zeros_like(sub_sums_ref)

    upstream = sum(r[...].astype(f32) for r in add_refs)
    unit, inverse = unit_norm(middle_ref[...])
    scaled = upstream * vec_ref[1:2]
    out_grad = out_grad_ref[...]
    grad = out_grad + inverse * (
        scaled - row_sum(scaled) * (1.0 / width) - unit * (row_sum(scaled * unit) * (1.0 / width))
    )
    grad_ref[...] = grad
    low = grad.astype(bf16)
    grad_low_ref[...] = low
    for i, terms in enumerate((grad, upstream * unit, upstream, out_grad)):
        sums_ref[i : i + 1, :] += jnp.sum(terms, axis=0, keepdims=True)
    gains, _, real = sub_vectors(owner_ref, sub_ref, count, padded)
    units, sub_inverse = sub_norm([r[...].astype(f32) for r in piece_refs], real, width)
    grads = []
    for p in range(count):
        rows = pl.ds(pl.multiple_of(owner_ref[p] * head_width, head_width), head_width)
        grads.append(dot_nt(low, jnp.concatenate([left_ref[rows, :], right_ref[rows, :]], axis=1)))
    sub_scaled = [g * gain for g, gain in zip(grads, gains)]
    mean = sum(row_sum(v) for v in sub_scaled) * (1.0 / width)
    along = sum(row_sum(v * u) for v, u in zip(sub_scaled, units)) * (1.0 / width)
    for p in range(count):
        head_refs[p][...] = ((sub_scaled[p] - mean - units[p] * along) * sub_inverse).astype(bf16)
        own = owner_ref[p]
        sub_sums_ref[own] += jnp.concatenate(
            [
                jnp.sum(grads[p] * units[p], axis=0, keepdims=True),
                jnp.sum(grads[p], axis=0, keepdims=True),
                jnp.zeros((6, head_width), f32),
            ],
            axis=0,
        )


def out_grad_kernel(owner_ref, low_ref, grad_ref, *refs, count, share, in_slots):
    head_width = low_ref.shape[2]
    *out_refs, part_ref = refs
    for p in range(count):
        own = owner_ref[p]
        part_ref[...] = dot_tn(low_ref[p], grad_ref[...])
        if in_slots:
            rows = head_width // count
            at = pl.ds(pl.multiple_of(own * rows, rows), rows)
            for q in range(count):
                first = pl.multiple_of(owner_ref[q] * share, share)
                parts = [
                    part_ref[pl.ds(pl.multiple_of(first + a * count * share, share), share), :]
                    for a in range(rows // share)
                ]
                out_refs[q][at, :] = jnp.concatenate(parts, axis=0).astype(bf16)
        else:
            rows = pl.ds(pl.multiple_of(own * head_width, head_width), head_width)
            out_refs[0][rows, :] = part_ref[...].astype(bf16)


def lane_fold(values):
    out = values[:, :128]
    for i in range(128, values.shape[1], 128):
        out = out + values[:, i : i + 128]
    return out


def normal_parts(values):
    density = jnp.exp(-0.5 * values * values)
    t = 1.0 / (1.0 + (0.3275911 * root_half) * jnp.abs(values))
    series = 0.5 * 1.061405429
    for c in (-1.453152027, 1.421413741, -0.284496736, 0.254829592):
        series = series * t + 0.5 * c
    tail = series * t * density
    return jnp.where(values >= 0, 1.0 - tail, tail), density


def up_kernel(up_ref, down_ref, vec_ref, *refs, count, waits):
    row_refs, grad_refs = refs[:count], refs[count : 2 * count]
    act_ref, slope_ref, back_ref, stat_ref, sums_ref, pre_ref, hid_ref, part_ref = refs[2 * count + waits :]
    rows = row_refs[0].shape[0]

    @pl.when(pl.program_id(0) == 0)
    def _():
        sums_ref[...] = jnp.zeros_like(sums_ref)

    pre_all = dot_nn(jnp.concatenate([r[...] for r in row_refs], axis=0), up_ref[...])
    hid_all = dot_nn(jnp.concatenate([r[...] for r in grad_refs], axis=0), down_ref[...])
    for s in range(count):
        pre_ref[s] = pre_all[s * rows : (s + 1) * rows]
        hid_ref[s] = hid_all[s * rows : (s + 1) * rows]
    for s in range(count):
        total = jnp.zeros((8, pre_ref.shape[2]), f32)
        for c in range(rows // CHUNK):
            at = slice(c * CHUNK, (c + 1) * CHUNK)
            pre = pre_ref[s, at, :] + vec_ref[0:1]
            phi, density = normal_parts(pre)
            activated = pre * phi
            back = hid_ref[s, at, :]
            scaled = back * vec_ref[1:2]
            act_ref[s, at, :] = activated
            slope_ref[s, at, :] = (phi + pre * inv_root_tau * density).astype(bf16)
            back_ref[s, at, :] = back.astype(bf16)
            for i, terms in enumerate((activated, activated * activated, scaled, scaled * activated)):
                part_ref[s, i, at, :] = lane_fold(terms)
            total = total + fold(back)
        sums_ref[...] += total
        for i in range(4):
            stat_ref[s, i : i + 1, :] = jnp.sum(jnp.transpose(part_ref[s, i]), axis=0, keepdims=True)


def back_kernel(up_ref, vec_ref, act_ref, slope_ref, back_ref, stat_ref, *refs, count):
    hidden_ref, pre_ref, *in_refs, sums_ref, col_ref = refs[-(4 + count) :]
    rows, width = act_ref.shape[1:]

    @pl.when(pl.program_id(0) == 0)
    def _():
        sums_ref[...] = jnp.zeros_like(sums_ref)

    for s in range(count):
        stats = stat_ref[s] * (1.0 / FF)
        mean, back_mean = stats[0:1], stats[2:3]
        inverse = lax.rsqrt(stats[1:2] - mean * mean + eps)
        along = (stats[3:4] - mean * back_mean) * inverse
        for i, line in enumerate((mean, inverse, back_mean, along)):
            col_ref[s, i] = jnp.transpose(jnp.broadcast_to(line, (128, rows)))
    for s in range(count):
        first = second = jnp.zeros((8, width), f32)
        for c in range(rows // CHUNK):
            at = slice(c * CHUNK, (c + 1) * CHUNK)
            spread = [jnp.concatenate([col_ref[s, i, at, :]] * (width // 128), axis=1) for i in range(4)]
            normed = (act_ref[s, at, :] - spread[0]) * spread[1]
            back = back_ref[s, at, :].astype(f32)
            hidden_ref[s, at, :] = (normed * vec_ref[1:2] + vec_ref[2:3]).astype(bf16)
            inner = back * vec_ref[1:2] - spread[2] - normed * spread[3]
            grad = inner * (spread[1] * slope_ref[s, at, :].astype(f32))
            pre_ref[s, at, :] = grad.astype(bf16)
            first, second = first + fold(grad), second + fold(back * normed)
        sums_ref[0] += first
        sums_ref[1] += second
    back_all = dot_nt(jnp.concatenate([pre_ref[s] for s in range(count)], axis=0), up_ref[...]).astype(bf16)
    for s in range(count):
        in_refs[s][...] = back_all[s * rows : (s + 1) * rows]


def ffn_grad_kernel(down_ref, *refs, count, pairs):
    row_refs, grad_refs = refs[:count], refs[count : 2 * count]
    hidden_refs, pre_refs = refs[2 * count : 2 * count + pairs], refs[2 * count + pairs : 2 * count + 2 * pairs]
    out_ref, *down_out_refs, up_acc, down_acc = refs[-(3 + count) :]
    hidden_width = down_ref.shape[1]
    step = pl.program_id(0)

    @pl.when(step == 0)
    def _():
        up_acc[...] = jnp.zeros_like(up_acc)
        down_acc[...] = jnp.zeros_like(down_acc)

    rows_all = jnp.concatenate([r[...] for r in row_refs], axis=0)
    grads_all = jnp.concatenate([r[...] for r in grad_refs], axis=0)
    hidden = jnp.concatenate([r[i] for r in hidden_refs for i in range(r.shape[0])], axis=0)
    pre = jnp.concatenate([r[i] for r in pre_refs for i in range(r.shape[0])], axis=0)
    up_acc[...] += dot_tn(rows_all, pre)
    down_acc[...] += dot_tn(grads_all, hidden)
    rows = row_refs[0].shape[0]
    down = dot_nt(hidden, down_ref[...]).astype(bf16)
    for i in range(count):
        down_out_refs[i][...] = down[i * rows : (i + 1) * rows]

    @pl.when(step == pl.num_programs(0) - 1)
    def _():
        out_ref[:, :hidden_width] = up_acc[...].astype(bf16)
        out_ref[:, hidden_width:] = down_acc[...].astype(bf16)


def in_grad_kernel(weight_ref, *refs, count):
    proj_refs, out_refs = refs[:count], refs[-count:]
    for s in range(count):
        out_refs[s][...] = dot_nt(proj_refs[s][...], weight_ref[...]).astype(bf16)


def qkv_grad_kernel(
    place_ref, weight_ref, lines_ref, hidden_lines_ref, head_sums_ref, normed_ref, proj_ref, *refs, count, share,
    hidden_share,
):
    token_refs = refs[:count]
    out_ref, acc_ref, unit_acc, col_acc = refs[-4:]
    step = pl.program_id(0)

    @pl.when(step == 0)
    def _():
        acc_ref[...] = jnp.zeros_like(acc_ref)
        unit_acc[...] = jnp.zeros_like(unit_acc)
        col_acc[...] = jnp.zeros_like(col_acc)

    proj = jnp.concatenate([proj_ref[s] for s in range(count)], axis=0)
    normed = jnp.concatenate([normed_ref[s] for s in range(count)], axis=0)
    unit = jnp.concatenate([unit_norm(r[...].astype(f32))[0].astype(bf16) for r in token_refs], axis=0)
    acc_ref[...] += dot_tn(normed, proj)
    unit_acc[...] += dot_tn(unit, proj)
    col_acc[...] += fold(proj.astype(f32))

    @pl.when(step == pl.num_programs(0) - 1)
    def _():
        weight = weight_ref[...].astype(f32)
        width, three = weight.shape
        devices = out_ref.shape[0]
        lane = lax.broadcasted_iota(jnp.int32, (width, 128), 1)
        gain = row_sum(weight * unit_acc[...])
        offset = row_sum(weight * jnp.sum(col_acc[...], axis=0, keepdims=True))
        norm_lines = jnp.transpose(jnp.where(lane == 0, gain, jnp.where(lane == 1, offset, 0.0)))[:8]
        low = pack_lines(lines_ref[0:8] + norm_lines, share, 0, devices)
        head_width = three // 3
        heads = jnp.concatenate(
            [jnp.zeros((2, head_width), f32), head_sums_ref[...], jnp.zeros((4, head_width), f32)], axis=0
        )
        low = low + pack_lines(heads, share, place_ref[1], devices)
        high = pack_lines(lines_ref[8:16], share, 0, devices)
        high = high + pack_lines(hidden_lines_ref[...], hidden_share, place_ref[0], devices)
        lines = jnp.concatenate([low, high, jnp.zeros((devices, 8, three - 256), f32)], axis=2)
        block = share_block(share)
        for i in range(devices):
            rows_i = acc_ref[i * share : (i + 1) * share, :]
            tail = [jnp.zeros((block - share - 8, three), f32)] if block > share + 8 else []
            out_ref[i] = jnp.concatenate([rows_i, lines[i], *tail], axis=0).astype(bf16)


def share_block(share):
    return -(-(-(-share // 8) * 8 + 8) // 16) * 16


def finish_kernel(packed_ref, out_ref, lines_ref, *, count, share, width):
    devices, _, three = packed_ref.shape
    head_width = three // 3
    total = 0.0
    for f in range(count):
        piece = packed_ref[f].astype(f32)
        for i in range(f + count, devices, count):
            piece = piece + packed_ref[i].astype(f32)
        total = total + piece[share : share + 8]
        size = min(head_width, width - f * head_width)
        for part in range(3):
            if size > 0:
                out_ref[:, part * width + f * head_width : part * width + f * head_width + size] = piece[
                    :share, part * head_width : part * head_width + size
                ]
    lines_ref[...] = total


def body(
    row_size,
    ffn_size,
    tokens,
    seq_lengths,
    key_keep,
    pre_gain,
    pre_bias,
    qkv_weight,
    query_bias,
    value_bias,
    sub_gain,
    sub_bias,
    out_weight,
    out_bias,
    ffn_gain,
    ffn_bias,
    up_bias,
    hidden_gain,
    hidden_bias,
    down_bias,
    up_weight,
    down_weight,
    out_grad,
):
    ffn_index, row_index = lax.axis_index("ffn"), lax.axis_index("rows")
    devices = row_size * ffn_size
    row_count, width = tokens.shape
    pack_total = row_count * ffn_size
    head_count = width // HEAD_DIM
    heads = -(-head_count // ffn_size)
    head_width = heads * HEAD_DIM
    three = 3 * head_width
    padded = head_width * ffn_size
    extra = padded - width
    hidden_width = up_weight.shape[1]
    share, hidden_share = pre_gain.shape[0], up_bias.shape[0]
    share_rows = share_block(share)
    owners = [slot_owner(p, ffn_index, ffn_size) for p in range(ffn_size)]
    owner_row = jnp.stack(owners).astype(jnp.int32)
    slots = range(ffn_size)
    pairs = [(i, i + 1) for i in range(0, ffn_size, 2)]
    steps = row_count // BLOCK

    thirds = jnp.pad(qkv_weight.reshape(share, 3, width), ((0, 0), (0, 0), (0, extra)))
    pieces = thirds.reshape(share, 3, ffn_size, head_width).transpose(2, 0, 1, 3)
    pieces = pieces.reshape(ffn_size, share, three)
    lines = [
        pre_gain, pre_bias, query_bias, value_bias, sub_gain, sub_bias, out_bias, ffn_gain, ffn_bias, down_bias,
        up_bias, hidden_gain, hidden_bias,
    ]
    lines = jnp.stack([jnp.pad(v, (0, 128 - v.shape[0])) for v in lines])
    lines = jnp.concatenate([lines[:8], jnp.pad(lines[8:], ((0, 3), (0, 0)))], axis=1)
    share_eight = -(-share // 8) * 8
    lines = jnp.pad(lines, ((share_eight - share, share_rows - share_eight - 8), (0, three - 256)))
    out_flat = share * width // three
    lines = jnp.concatenate([lines, out_weight.reshape(out_flat, three)], axis=0)
    pieces = jnp.concatenate([pieces, jnp.broadcast_to(lines, (ffn_size,) + lines.shape)], axis=1)
    pieces = in_order([pieces[i] for i in slots], ffn_index, ffn_size)
    pieces = jnp.stack(in_order(exchange_slots(pieces, ffn_size), ffn_index, ffn_size))
    if ffn_size == 4:
        tokens_across = swap(after(tokens, pieces), 2)
        token_slots = [tokens, swap(tokens, 1), tokens_across, swap(tokens_across, 1)]
    else:
        token_slots = gather_slots(tokens, ffn_size)
    out_rows = pieces[:, share_rows:].reshape(ffn_size * share, width)
    half = width // 2
    left = jnp.concatenate([up_weight, out_rows[:, :half]], axis=1)
    right = jnp.concatenate([down_weight.T, out_rows[:, half:]], axis=1)
    gathered = pieces[:, :share_rows].reshape(ffn_size * share_rows, three)
    special = ffn_size == 4 and row_size == 8
    if special:
        gathered = row_step(gathered, 4, row_index)
        right = row_step(right, 1, row_index)
        gathered = row_step(gathered, 2, row_index, 1)
        left = row_step(after(left, tokens_across), 4, row_index)
        gathered = gathered.reshape(4, ffn_size, share_rows, three)
        gathered_across = swap_rows(gathered, 1)
        halves = [gathered_across]
    else:
        gathered, left, right = [lax.all_gather(v, "rows", axis=0, tiled=False) for v in (gathered, left, right)]
        halves = []
    if not halves:
        gathered = gathered.reshape(devices, share_rows, three)
    place_row = jnp.stack([ffn_index * hidden_width, ffn_index * head_width, row_index & 1]).astype(jnp.int32)
    qkv_own, wide, hidden_all, bias_rows = call(
        functools.partial(
            unpack_kernel, share=share, hidden_share=hidden_share, line_at=share_eight, halves=bool(halves)
        ),
        1,
        [(place_row, SMEM), *[(g, fixed(*g.shape)) for g in [gathered] + halves]],
        [
            ((width, three), bf16, fixed(width, three)),
            ((16, width), f32, fixed(16, width)),
            ((16, hidden_width), f32, fixed(16, hidden_width)),
            ((8, three), f32, fixed(8, three)),
        ],
        "unpack",
        devices * 64 * width * 16,
        [pltpu.VMEM((devices, 8, 256), f32)],
    )
    if share % 8:
        qkv_own = gathered[:, :share, :].reshape(width, three)
    hidden_vectors = jnp.pad(hidden_all[10:13], ((0, 5), (0, 0)))
    middle_vectors = jnp.pad(wide[6:9], ((0, 5), (0, 0)))
    sub_rows = jnp.pad(
        jnp.concatenate([wide[4:6], jnp.ones((1, width), f32)], axis=0), ((0, 5), (0, extra))
    )
    sub_rows = sub_rows.reshape(8, ffn_size, head_width).transpose(1, 0, 2)
    if ffn_size == 4:
        grad_low = after(out_grad, tokens_across).astype(bf16)
        grad_across = swap(grad_low, 2)
        grad_slots = [grad_low, swap(grad_low, 1), grad_across, swap(grad_across, 1)]
        early = [grad_across]
    else:
        early = []
        grad_slots = gather_slots(out_grad.astype(bf16), ffn_size)

    block_row = pl.BlockSpec((BLOCK, width), lambda i: (i, 0))
    proj, normed_low = call(
        functools.partial(front_kernel, count=ffn_size),
        steps,
        [(qkv_own, fixed(width, three)), (bias_rows, fixed(8, three)), (wide, fixed(16, width))]
        + [(t, block_row) for t in token_slots],
        [
            ((ffn_size, row_count, three), bf16, pl.BlockSpec((ffn_size, BLOCK, three), lambda i: (0, i, 0))),
            ((ffn_size, row_count, width), bf16, pl.BlockSpec((ffn_size, BLOCK, width), lambda i: (0, i, 0))),
        ],
        "front",
        2 * pack_total * width * three,
    )
    if special:
        left = row_step(left, 2, row_index, 1, wait=proj)
        right = row_step(after(right, gathered_across), 4, row_index, wait=proj)
        early += [left, right]
    proj, normed_low = proj.reshape(pack_total, three), normed_low.reshape(pack_total, width)

    bounds, running = [], jnp.int32(0)
    for i in range(seq_lengths.shape[1] - 1):
        running = running + seq_lengths[0, i]
        bounds.append(running)
    bounds = jnp.stack(bounds)
    firsts = jnp.arange(pack_total // BLOCK, dtype=jnp.int32) * BLOCK
    block_owner = firsts // row_count
    place = (block_owner ^ ffn_index if ffn_size == 4 else block_owner) * row_count + firsts % row_count
    keep = key_keep.reshape(pack_total // BLOCK, BLOCK)
    mixed_own, lse = attend_forward(place, bounds, proj, keep, heads, early)

    if special:
        left = row_step(left, 1, row_index, 2, wait=lse)
        right = row_step(right, 2, row_index, 1, wait=lse)
    left, right = left.reshape(width, -1), right.reshape(width, -1)
    up_in = (left, columns(width, hidden_width, 0))
    down_in = (right, columns(width, hidden_width, 0))
    if extra:
        out_in = [
            (jnp.pad(v[:, hidden_width:], ((0, extra), (0, 0))), columns(padded, half, 0)) for v in (left, right)
        ]
    else:
        out_in = [(v, columns(width, half, hidden_width // half)) for v in (left, right)]

    mixed_slots = exchange_slots(
        [mixed_own[p * row_count : (p + 1) * row_count] for p in slots], ffn_size
    )
    block_piece = pl.BlockSpec((BLOCK, head_width), lambda i: (i, 0))
    block_pieces = pl.BlockSpec((ffn_size, BLOCK, head_width), lambda i: (0, i, 0))
    middle_in = [*out_in, (sub_rows, fixed(ffn_size, 8, head_width)), (middle_vectors, fixed(8, width))]
    sub_low, middle, ffn_low = call(
        functools.partial(middle_forward_kernel, count=ffn_size, padded=bool(extra)),
        steps,
        [(owner_row, SMEM), (tokens, block_row), *middle_in, *[(m, block_piece) for m in mixed_slots]]
        + [(grad_slots[-1], ANY)],
        [
            ((ffn_size, row_count, head_width), bf16, block_pieces),
            ((row_count, width), f32, block_row),
            ((row_count, width), bf16, block_row),
        ],
        "middle_forward",
        2 * row_count * padded * width,
    )

    fine = BLOCK // 2
    block_fine = pl.BlockSpec((fine, width), lambda i: (i, 0))
    block_pair = pl.BlockSpec((2, fine, hidden_width), lambda i: (0, i, 0))
    block_pair_row = pl.BlockSpec((2, fine, width), lambda i: (0, i, 0))
    block_stat = pl.BlockSpec((2, 8, fine), lambda i: (0, 0, i))
    block_four = pl.BlockSpec((2, 4, fine), lambda i: (0, 0, i))
    hidden_in = (hidden_vectors, fixed(8, hidden_width))
    pair_shape = (2, row_count, hidden_width)

    def up_pair(rows, grads, waits):
        return call(
            functools.partial(up_kernel, count=2, waits=len(waits)),
            2 * steps,
            [up_in, down_in, hidden_in, *[(r, block_fine) for r in rows], *[(g, block_fine) for g in grads]]
            + [(w, ANY) for w in waits],
            [
                (pair_shape, f32, block_pair),
                (pair_shape, bf16, block_pair),
                (pair_shape, bf16, block_pair),
                ((2, 8, row_count), f32, block_stat),
                ((8, hidden_width), f32, fixed(8, hidden_width)),
            ],
            "up",
            8 * row_count * width * hidden_width,
            [
                pltpu.VMEM((2, fine, hidden_width), f32),
                pltpu.VMEM((2, fine, hidden_width), f32),
                pltpu.VMEM((2, 4, fine, 128), f32),
            ],
            4 * row_count * hidden_width,
        )

    if ffn_size == 4:
        across, beside = swap(ffn_low, 2), swap(ffn_low, 1)
        ups = [up_pair([ffn_low, beside], grad_slots[:2], [])]
        slanted = swap(after(across, ups[0][3]), 1)
        row_slots = [ffn_low, beside, across, slanted]
        ups.append(up_pair([across, slanted], grad_slots[2:], [ups[0][3]]))
    else:
        row_slots = gather_slots(ffn_low, ffn_size)
        ups = [up_pair(row_slots[i : i + 2], grad_slots[i : i + 2], []) for i, _ in pairs]
    stats = sum_slots([u[3] for u in ups], ffn_size)
    backs, wait_for = [None] * len(pairs), []
    for k in reversed(range(len(pairs))):
        act, slope, back = ups[k][:3]
        backs[k] = call(
            functools.partial(back_kernel, count=2),
            2 * steps,
            [up_in, hidden_in, (act, block_pair), (slope, block_pair), (back, block_pair)]
            + [(stats[2 * k : 2 * k + 2], block_four), *[(w, ANY) for w in wait_for]],
            [
                (pair_shape, bf16, block_pair),
                (pair_shape, bf16, block_pair),
                ((row_count, width), bf16, block_fine),
                ((row_count, width), bf16, block_fine),
                ((2, 8, hidden_width), f32, fixed(2, 8, hidden_width)),
            ],
            "back",
            4 * row_count * width * hidden_width,
            [pltpu.VMEM((2, 4, fine, 128), f32)],
        )
        wait_for = [backs[k][3]]

    def reduce_pairs(near, far, wait=None):
        passed = swap(far[1], 1)
        sent = far[0].astype(f32) + passed.astype(f32)
        sent = (sent if wait is None else after(sent, wait)).astype(bf16)
        return [near[0], swap(near[1], 1), swap(sent, 2)], sent

    def scatter_pairs(parts):
        return [lax.psum_scatter(jnp.stack(parts), "ffn", scatter_dimension=0, tiled=True)[0]]

    if ffn_size == 4:
        in_terms, in_sent = reduce_pairs(backs[0][2:4], backs[1][2:4])
        in_waits = [in_sent]
    else:
        in_terms = scatter_pairs([v for b in backs for v in b[2:4]])
        in_waits = []
    block_quarter = pl.BlockSpec((BLOCK // 2, width), lambda i: (i, 0))
    block_pair_quarter = pl.BlockSpec((2, BLOCK // 2, hidden_width), lambda i: (0, i, 0))
    weight_part, *down_parts = call(
        functools.partial(ffn_grad_kernel, count=ffn_size, pairs=len(pairs)),
        2 * steps,
        [down_in, *[(r, block_quarter) for r in row_slots], *[(g, block_quarter) for g in grad_slots]]
        + [(b[0], block_pair_quarter) for b in backs]
        + [(b[1], block_pair_quarter) for b in backs]
        + [(w, ANY) for w in in_waits],
        [
            ((width, 2 * hidden_width), bf16, fixed(width, 2 * hidden_width)),
        ]
        + [((row_count, width), bf16, block_quarter)] * ffn_size,
        "ffn_grads",
        6 * pack_total * width * hidden_width,
        [pltpu.VMEM((width, hidden_width), f32), pltpu.VMEM((width, hidden_width), f32)],
    )
    if special:
        weight_part = weight_part.reshape(2, 2, 2, width // row_size, 2 * hidden_width)
    else:
        ties = []
        weight_grad = lax.psum_scatter(weight_part, "rows", scatter_dimension=0, tiled=True).astype(f32)

    grad_middle, middle_low, *head_low, middle_sums, sub_sums = call(
        functools.partial(
            middle_backward_kernel, count=ffn_size, addends=len(in_terms), padded=bool(extra)
        ),
        steps,
        [(owner_row, SMEM), (out_grad, block_row), (middle, block_row), *middle_in]
        + [(m, block_piece) for m in mixed_slots]
        + [(t, block_row) for t in in_terms],
        [
            ((row_count, width), f32, block_row),
            ((row_count, width), bf16, block_row),
            *[((row_count, head_width), bf16, block_piece)] * ffn_size,
            ((8, width), f32, fixed(8, width)),
            ((ffn_size, 8, head_width), f32, fixed(ffn_size, 8, head_width)),
        ],
        "middle_backward",
        2 * row_count * padded * width,
    )
    grad_own = jnp.concatenate(exchange_slots(head_low, ffn_size), axis=0)
    out_shape = (row_size * share, width) if special else (padded, width)
    out_parts = call(
        functools.partial(out_grad_kernel, count=ffn_size, share=share, in_slots=special),
        1,
        [(owner_row, SMEM), (sub_low, fixed(ffn_size, row_count, head_width)), (middle_low, fixed(row_count, width))],
        [(out_shape, bf16, fixed(*out_shape))] * (ffn_size if special else 1),
        "out_grads",
        2 * row_count * padded * width,
        [pltpu.VMEM((head_width, width), f32)],
    )
    if special:
        weight_sent, weight_kept = row_split(weight_part, 1, row_index)
        weight_across = after(swap_rows(weight_sent, 1), middle_low)
        weight_sent, weight_kept = row_split(weight_kept + weight_across.astype(f32), 2, row_index)
        ties = [weight_sent]
        weight_across = swap_rows(weight_sent, 2)
        out_terms = exchange_slots(out_parts, ffn_size)
    else:
        out_weight_own = lax.psum_scatter(
            out_parts[0][:width], ("rows", "ffn"), scatter_dimension=0, tiled=True
        ).astype(f32)

    if ffn_size == 4:
        down_terms, layer_sent = reduce_pairs(down_parts[:2], down_parts[2:], grad_own)
        ties.append(layer_sent)
    else:
        down_terms = scatter_pairs(down_parts)
    layer_out = (middle + sum(t.astype(f32) for t in down_terms) + wide[9]).astype(bf16)

    sub_flat = sub_sums[:, :2].transpose(1, 0, 2).reshape(2, padded)[:, :width]
    lines = jnp.concatenate(
        [jnp.zeros((4, width), f32), sub_flat, middle_sums[:4], jnp.zeros((6, width), f32)], axis=0
    )
    back_sums = jnp.sum(sum(b[4] for b in backs), axis=1)
    hidden_lines = jnp.concatenate(
        [
            jnp.zeros((2, hidden_width), f32),
            back_sums,
            jnp.sum(sum(u[4] for u in ups), axis=0)[None],
            jnp.zeros((3, hidden_width), f32),
        ],
        axis=0,
    )
    ties += [lines, hidden_lines]

    grad_proj, head_bias_grads = attend_backward(place, bounds, proj, keep, mixed_own, grad_own, lse, heads, ties)

    def in_pair(k, waits):
        proj_specs = [
            pl.BlockSpec((BLOCK, three), lambda i, p=p: (p * steps + i, 0)) for p in pairs[k]
        ]
        return call(
            functools.partial(in_grad_kernel, count=2),
            steps,
            [(qkv_own, fixed(width, three)), *[(grad_proj, spec) for spec in proj_specs]]
            + [(w, ANY) for w in waits],
            [((row_count, width), bf16, block_row)] * 2,
            "in_grads",
            4 * row_count * width * three,
        )

    if special:
        weight_sent, weight_kept = row_split(weight_kept + after(weight_across, head_bias_grads).astype(f32), 4, row_index)
        weight_across = swap_rows(weight_sent, 4)
        out_sum = sum(after(v, head_bias_grads).astype(f32) for v in out_terms).reshape(2, 2, 2, share, width)
        out_sent, out_kept = row_split(out_sum, 1, row_index)
        out_across = swap_rows(out_sent, 1)
        far = in_pair(1, [down_terms[2], out_sent])
        sent = (far[0].astype(f32) + swap(far[1], 1).astype(f32)).astype(bf16)
        across = swap(sent, 2)
        out_sent, out_kept = row_split(out_kept + after(out_across, far[0]).astype(f32), 2, row_index)
        out_across = swap_rows(out_sent, 2)
        late = [weight_sent, out_sent, sent]
    else:
        late = []
    eighth = row_count // 4
    (packed,) = call(
        functools.partial(
            qkv_grad_kernel, count=ffn_size, share=share, hidden_share=hidden_share
        ),
        4,
        [
            (place_row, SMEM),
            (qkv_own, fixed(width, three)),
            (lines, fixed(16, width)),
            (hidden_lines, fixed(8, hidden_width)),
            (head_bias_grads, fixed(2, head_width)),
            (
                normed_low.reshape(ffn_size, row_count, width),
                pl.BlockSpec((ffn_size, eighth, width), lambda i: (0, i, 0)),
            ),
            (
                grad_proj.reshape(ffn_size, row_count, three),
                pl.BlockSpec((ffn_size, eighth, three), lambda i: (0, i, 0)),
            ),
            *[(t, pl.BlockSpec((eighth, width), lambda i: (i, 0))) for t in token_slots],
            *[(v, ANY) for v in late],
        ],
        [((devices, share_rows, three), bf16, fixed(devices, share_rows, three))],
        "qkv_grads",
        4 * pack_total * width * three,
        [pltpu.VMEM((width, three), f32), pltpu.VMEM((width, three), f32), pltpu.VMEM((8, three), f32)],
    )
    if special:
        near = in_pair(0, [packed, across])
        in_terms = [near[0], swap(near[1], 1), across]
        weight_grad = weight_kept + after(weight_across, near[0]).astype(f32)
        out_sent, out_kept = row_split(out_kept + after(out_across, packed).astype(f32), 4, row_index)
        out_weight_own = (out_kept + after(swap_rows(out_sent, 4), near[0]).astype(f32)).reshape(share, width)
    else:
        in_terms = scatter_pairs([v for k in range(len(pairs)) for v in in_pair(k, [])])
    packed = lax.all_to_all(packed, ("rows", "ffn"), split_axis=0, concat_axis=0, tiled=True)
    qkv_weight_grad, line_own = call(
        functools.partial(finish_kernel, count=ffn_size, share=share, width=width),
        1,
        [(packed, fixed(*packed.shape))],
        [((share, 3 * width), f32, fixed(share, 3 * width)), ((8, three), f32, fixed(8, three))],
        "finish",
        devices * share * three,
    )

    weight_grad = weight_grad.reshape(-1, 2 * hidden_width)
    up_weight_grad, down_weight_grad = weight_grad[:, :hidden_width], weight_grad[:, hidden_width:].T

    unit_own, inverse_own = unit_norm(tokens.astype(f32))
    in_scaled = sum(t.astype(f32) for t in in_terms) * wide[0]
    in_adjusted = (
        in_scaled
        - jnp.mean(in_scaled, axis=-1, keepdims=True)
        - unit_own * jnp.mean(in_scaled * unit_own, axis=-1, keepdims=True)
    )
    tokens_grad = grad_middle + in_adjusted * inverse_own

    vectors = [line_own[i, :share] for i in range(8)] + [line_own[i, 128 : 128 + share] for i in range(2)]
    small = vectors
    hidden_small = [line_own[i, 128 : 128 + hidden_share] for i in range(2, 5)]
    return (
        layer_out,
        tokens_grad,
        small[0],
        small[1],
        qkv_weight_grad,
        small[2],
        small[3],
        small[4],
        small[5],
        out_weight_own,
        small[6],
        small[7],
        small[8],
        hidden_small[0],
        hidden_small[1],
        hidden_small[2],
        small[9],
        up_weight_grad,
        down_weight_grad,
    )


def solution(mesh):
    flat, matrix = P(("rows", "ffn")), P(("rows", "ffn"), None)
    in_specs = (
        matrix, P("rows", None), P("rows"), flat, flat, matrix, flat, flat, flat, flat, matrix, flat, flat, flat,
        flat, flat, flat, flat, P("rows", "ffn"), P("ffn", "rows"), matrix,
    )
    out_specs = (
        matrix, matrix, flat, flat, matrix, flat, flat, flat, flat, matrix, flat, flat, flat, flat, flat, flat, flat,
        P("rows", "ffn"), P("ffn", "rows"),
    )
    return jax.shard_map(
        functools.partial(body, mesh.shape["rows"], mesh.shape["ffn"]),
        mesh=mesh,
        in_specs=in_specs,
        out_specs=out_specs,
        check_vma=False,
    )
```
